128 devices in a mesh: gx: 8 (over z, core), gy: 16 (over x, y).
Axes of the slice: x: 4, y: 4, z: 4, core: 2. Of those that a mesh axis runs over, the one named last changes fastest.
Arguments:
- soil_state: float32 [9, 64, 64, 2048], P(None, 'gx', None, 'gy'), may hold values from -6 to 6
- material: bfloat16 [3, 64, 64, 2048], P(None, 'gx', None, 'gy'), may hold values from 0.5 to 1.5
- dashpot: float32 [64, 2048], P('gx', 'gy'), may hold values from 0.02 to 0.2
- foot_cells: int32 [1024, 128], P(('gx', 'gy')), may hold values from 0 to 1023, as said below
- owner_table: int32 [3, 128], replicated, may hold values from 0 to 127, each once within a row
- stiffness: float32 [12, 12, 262144], P(None, None, ('gx', 'gy')), as said below
- beam_links: int32 [2, 262144], P(None, ('gx', 'gy')), may hold values from 0 to 127
- beam_count: int32 [1024], P(('gx', 'gy')), may hold values from 128 to 256
- inverse_mass: float32 [6, 131072], P(None, ('gx', 'gy')), may hold values from 0.25 to 1
- frame_displacement: float32 [6, 131072], P(None, ('gx', 'gy')), may hold values from -2 to 2
- frame_velocity: float32 [6, 131072], P(None, ('gx', 'gy')), may hold values from -2 to 2
Outputs:
- soil_after: float32 [9, 64, 64, 2048], P(None, 'gx', None, 'gy')
- base_force: float32 [3, 64, 2048], P(None, 'gx', 'gy')
- displacement_after: float32 [6, 131072], P(None, ('gx', 'gy'))
- velocity_after: float32 [6, 131072], P(None, ('gx', 'gy'))
The draws below stay inside these ranges and needn't reach their ends.
Inputs may be any that keep to these rules, and one draw needn't show every extreme that they name: `foot_cells`: the 8 rows of each device list each of its 1024 local surface cells (x-major) exactly once. `stiffness`: each beam's 12 x 12 matrix is symmetric.
All inputs are finite; a program needn't handle non-finite values.
Results may differ from the reference program's by a relative error of at most 0.0003.
Values sent between devices are 32-bit elements; how exact they have to be, the bound alone decides.
A program may use at most 128 MiB of HBM per device.

```python
import math
import jax
import jax.numpy as jnp
from jax import lax

CX = 8
CY = 128
CZ = 64
FOOT = 128
NODES = 128
BEAMS = 256
GROUPS = 4
SOIL_STEPS = 2
FRAME_STEPS = 4
NX = 64
NY = 2048
HOSTED = 8
GROUP = 2
BUILDINGS = 1024
N_GX = 8
N_GY = 16


def draw_foot_cells(key, part):
    key = jax.random.fold_in(key, 11)
    tile_count = BUILDINGS // HOSTED
    keys_all = jax.random.split(key, tile_count)
    orders = jax.vmap(lambda single: jax.random.permutation(single, HOSTED * FOOT))(keys_all)
    return orders.reshape(BUILDINGS, FOOT).astype(jnp.int32)


def draw_stiffness(key, part):
    key = jax.random.fold_in(key, 12)
    first_key, second_key = jax.random.split(key)
    beam_total = BUILDINGS * BEAMS
    coupling = jax.random.uniform(first_key, (12, 12, beam_total), jnp.float32, -0.08, 0.08)
    coupling = 0.5 * (coupling + jnp.transpose(coupling, (1, 0, 2)))
    diagonal = jax.random.uniform(second_key, (12, beam_total), jnp.float32, 1.0, 2.0)
    identity = jnp.eye(12, dtype=jnp.float32)[:, :, None]
    return (coupling * (1.0 - identity) + identity * diagonal[:, None, :]).astype(jnp.float32)


def with_ends(result, stream_key, smallest, high):
    dims = result.shape
    place = [jax.random.randint(jax.random.fold_in(stream_key, axis), (), 0, dims[axis]) for axis in range(len(dims))]
    result = result.at[tuple(place)].set(smallest)
    longest = dims.index(max(dims))
    place[longest] = (place[longest] + 1) % dims[longest]
    return result.at[tuple(place)].set(high)


def steps_of(rng, dims, cuts, smallest, largest):
    loudness = 1.0
    for position, shards_of in cuts:
        heights = jax.random.uniform(jax.random.fold_in(jax.random.fold_in(rng, 6), position), (shards_of,), jnp.float32, smallest / len(cuts), largest / len(cuts))
        loudness = loudness * jnp.repeat(jnp.exp(heights), dims[position] // shards_of).reshape((-1,) + (1,) * (len(dims) - 1 - position))
    return loudness


def noise(own_key, shape, deviation, limit, shards=(), kind=jnp.bfloat16):
    gain = steps_of(own_key, shape, shards, -0.22, 0.18) if shards else 1.0
    entries = jax.random.normal(own_key, shape, jnp.float32) * deviation * gain
    return jnp.minimum(jnp.maximum(entries, -limit), limit).astype(kind)


def setup_inputs(seed: int = 0) -> dict:
    streams_of = jax.random.split(jax.random.key(seed), 12)
    return {
        "soil_state": noise(streams_of[0], (9, NX, CZ, NY), 1.0, 6.0, ((1, 8), (3, 16)), jnp.float32),
        "material": jnp.clip(jnp.exp(math.log(1.5) - 1.0986123 * jax.random.uniform(streams_of[1], (3, NX, CZ, NY), jnp.float32) ** steps_of(streams_of[1], (3, NX, CZ, NY), ((1, 8), (3, 16)), -0.2, 0.2)), 0.5, 1.5).astype(jnp.bfloat16),
        "dashpot": jnp.clip(jnp.exp(math.log(0.2) - 2.3025851 * jax.random.uniform(streams_of[2], (NX, NY), jnp.float32) ** steps_of(streams_of[2], (NX, NY), ((0, 8), (1, 16)), -0.2, 0.2)), 0.02, 0.2),
        "foot_cells": draw_foot_cells(jax.random.fold_in(streams_of[11], 71), 0),
        "owner_table": jax.vmap(lambda own: jax.random.permutation(own, N_GX * N_GY))(jax.random.split(streams_of[4], (GROUPS - 1))).reshape((GROUPS - 1, N_GX * N_GY)).astype(jnp.int32),
        "stiffness": draw_stiffness(jax.random.fold_in(streams_of[11], 71), 0),
        "beam_links": with_ends(jax.random.randint(streams_of[6], (2, BUILDINGS * BEAMS), 0, NODES), jax.random.fold_in(streams_of[6], 1), 0, NODES - 1).astype(jnp.int32),
        "beam_count": with_ends(jax.random.randint(streams_of[7], (BUILDINGS,), BEAMS // 2, BEAMS + 1), jax.random.fold_in(streams_of[7], 1), BEAMS // 2, BEAMS).astype(jnp.int32),
        "inverse_mass": jnp.clip(jnp.exp(math.log(1.0) - 1.3862944 * jax.random.uniform(streams_of[8], (6, BUILDINGS * NODES), jnp.float32) ** steps_of(streams_of[8], (6, BUILDINGS * NODES), ((1, 128),), -0.2, 0.2)), 0.25, 1.0),
        "frame_displacement": noise(streams_of[9], (6, BUILDINGS * NODES), 0.3, 2.0, ((1, 128),), jnp.float32),
        "frame_velocity": noise(streams_of[10], (6, BUILDINGS * NODES), 0.3, 2.0, ((1, 128),), jnp.float32),
    }


COEF_NEAR = 9.0 / 8.0
COEF_FAR = -1.0 / 24.0
TIME_SOIL = 0.18
TIME_FRAME = 0.05


def shifted(field, padding, anchor, extent, axis_dim, offset):
    starts = [anchor[k] + padding[k] + (offset if k == axis_dim else 0) for k in range(3)]
    return lax.slice(field, starts, [starts[k] + extent[k] for k in range(3)])


def derivative(field, padding, anchor, extent, axis_dim, forward):
    def taken(offset):
        return shifted(field, padding, anchor, extent, axis_dim, offset)
    if forward:
        return COEF_NEAR * (taken(1) - taken(0)) + COEF_FAR * (taken(2) - taken(-1))
    return COEF_NEAR * (taken(0) - taken(-1)) + COEF_FAR * (taken(1) - taken(-2))


def velocity_update(velocity, stresses, inverse_density, padding, anchor, extent):
    def along(member, axis_dim):
        return derivative(stresses[member], padding, anchor, extent, axis_dim, False)
    accel_x = along(0, 0) + along(3, 2) + along(4, 1)
    accel_y = along(3, 0) + along(1, 2) + along(5, 1)
    accel_z = along(4, 0) + along(5, 2) + along(2, 1)
    return velocity + TIME_SOIL * inverse_density[None] * jnp.stack([accel_x, accel_y, accel_z])


def stress_update(stresses, velocity, lame_first, lame_shear, padding, extent):
    def along(member, axis_dim):
        return derivative(velocity[member], padding, (0, 0, 0), extent, axis_dim, True)
    strain_x = along(0, 0)
    strain_y = along(1, 2)
    strain_z = along(2, 1)
    volume = strain_x + strain_y + strain_z
    normal_x = stresses[0] + TIME_SOIL * (lame_first * volume + 2.0 * lame_shear * strain_x)
    normal_y = stresses[1] + TIME_SOIL * (lame_first * volume + 2.0 * lame_shear * strain_y)
    normal_z = stresses[2] + TIME_SOIL * (lame_first * volume + 2.0 * lame_shear * strain_z)
    shear_xy = stresses[3] + TIME_SOIL * lame_shear * (along(0, 2) + along(1, 0))
    shear_xz = stresses[4] + TIME_SOIL * lame_shear * (along(0, 1) + along(2, 0))
    shear_yz = stresses[5] + TIME_SOIL * lame_shear * (along(1, 1) + along(2, 2))
    return jnp.stack([normal_x, normal_y, normal_z, shear_xy, shear_xz, shear_yz])


def frame_steps(displacement, velocity, stiffness, beam_links, beam_count, inverse_mass, drive, damping):
    buildings = beam_count.shape[0]
    beams_all = beam_links.shape[1]
    per_building = beams_all // buildings
    per_nodes = displacement.shape[1] // buildings
    beam_index = jnp.arange(beams_all, dtype=jnp.int32)
    holder = beam_index // per_building
    first_node = (holder * per_nodes + beam_links[0]).astype(jnp.int32)
    second_node = (holder * per_nodes + beam_links[1]).astype(jnp.int32)
    active = (beam_index % per_building < beam_count[holder]).astype(jnp.float32)
    footing = jnp.arange(buildings, dtype=jnp.int32) * per_nodes
    footing_sum = jnp.zeros((3, buildings), jnp.float32)
    for counter in range(FRAME_STEPS):
        beam_ends = jnp.concatenate([displacement[:, first_node], displacement[:, second_node]], 0)
        forces = jnp.einsum("abe,be->ae", stiffness, beam_ends, precision=lax.Precision.HIGHEST) * active[None]
        internal = jnp.zeros_like(displacement).at[:, first_node].add(forces[:6]).at[:, second_node].add(forces[6:])
        footing_force = drive - damping[None] * velocity[:3, footing]
        node_loads = (-internal).at[:3, footing].add(footing_force)
        velocity = velocity + TIME_FRAME * inverse_mass * node_loads
        displacement = displacement + TIME_FRAME * velocity
        footing_sum = footing_sum + velocity[:3, footing]
    return displacement, velocity, footing_sum


def reference(soil_state, material, dashpot, foot_cells, owner_table, stiffness, beam_links, beam_count, inverse_mass, frame_displacement, frame_velocity):
    coeffs = material.astype(jnp.float32)
    inverse_density, lame_first, lame_shear = coeffs[0], coeffs[1], coeffs[2]
    current = soil_state
    extent = soil_state.shape[1:]
    widening = ((0, 0), (2, 2), (2, 2), (2, 2))
    for counter in range(SOIL_STEPS):
        stresses = jnp.pad(current[3:], widening)
        velocity = velocity_update(current[:3], stresses, inverse_density, (2, 2, 2), (0, 0, 0), extent)
        moving = jnp.pad(velocity, widening)
        updated = stress_update(current[3:], moving, lame_first, lame_shear, (2, 2, 2), extent)
        current = jnp.concatenate([velocity, updated], 0)
    devices = N_GX * N_GY
    surface = current[:3, :, 0, :].reshape(3, NX * NY)
    building = jnp.arange(BUILDINGS, dtype=jnp.int32)
    host_device = building // HOSTED
    cell_rows = (host_device // N_GY)[:, None] * CX + foot_cells // CY
    cell_columns = (host_device % N_GY)[:, None] * CY + foot_cells % CY
    cell_flat = (cell_rows * NY + cell_columns).astype(jnp.int32)
    cell_velocity = surface[:, cell_flat]
    cell_damping = dashpot.reshape(NX * NY)[cell_flat]
    drive = jnp.sum(cell_damping[None] * cell_velocity, axis=2)
    damping = jnp.sum(cell_damping, axis=1)
    device_index = jnp.arange(devices, dtype=jnp.int32)
    group_rows = jnp.arange(GROUPS - 1, dtype=jnp.int32)[:, None]
    inverse = jnp.zeros_like(owner_table).at[group_rows, owner_table].set(jnp.broadcast_to(device_index[None], owner_table.shape))
    source = jnp.concatenate([device_index[:, None], inverse.T], 1)
    slot_order = (source[:, :, None] * HOSTED + (jnp.arange(GROUPS, dtype=jnp.int32) * GROUP)[None, :, None] + jnp.arange(GROUP, dtype=jnp.int32)[None, None, :]).reshape(BUILDINGS).astype(jnp.int32)
    displacement_after, velocity_after, footing_sum = frame_steps(frame_displacement, frame_velocity, stiffness, beam_links, beam_count, inverse_mass, drive[:, slot_order], damping[slot_order])
    host_sum = jnp.zeros((3, BUILDINGS), jnp.float32).at[:, slot_order].set(footing_sum)
    impulse = cell_damping[None] * (FRAME_STEPS * cell_velocity - host_sum[:, :, None])
    base_force = jnp.zeros((3, NX * NY), jnp.float32).at[:, cell_flat.reshape(-1)].set(impulse.reshape(3, -1)).reshape(3, NX, NY)
    return current, base_force, displacement_after, velocity_after
```

```python
import functools

import jax
import jax.numpy as jnp
from jax import lax
from jax.experimental import pallas as pl
from jax.experimental.pallas import tpu as pltpu
from jax.sharding import PartitionSpec as P

GROUPS = 4
FRAME_STEPS = 4
NEAR = 9.0 / 8.0
FAR = -1.0 / 24.0
TIME_SOIL = 0.18
TIME_FRAME = 0.05
MESH = pl.DeviceIdType.MESH
ROW = 8
COL = 2
F32 = jnp.float32
BF16 = jnp.bfloat16

VX, VY, VZ, SXX, SYY, SZZ, SXY, SXZ, SYZ = range(9)


def lane_gather(values, index):
    return lax.gather(
        values,
        index[:, :, None],
        lax.GatherDimensionNumbers(
            offset_dims=(),
            collapsed_slice_dims=(1,),
            start_index_map=(1,),
            operand_batching_dims=(0,),
            start_indices_batching_dims=(0,),
        ),
        (1, 1),
        mode=lax.GatherScatterMode.PROMISE_IN_BOUNDS,
    )


def iota(shape, dim):
    return lax.broadcasted_iota(jnp.int32, shape, dim)


def stencil(near_high, near_low, far_high, far_low):
    return NEAR * (near_high - near_low) + FAR * (far_high - far_low)


def rolled(value, shift):
    return pltpu.roll(value, shift, 1)


def kernel(
    n_gx,
    n_gy,
    soil,
    material,
    dashpot,
    foot,
    table,
    stiff,
    links,
    count,
    inverse_mass,
    frame_disp,
    frame_vel,
    soil_out,
    force_out,
    disp_out,
    vel_out,
    first,
    vel_a,
    str_a,
    vel_b,
    str_b,
    raw,
    coef,
    matrix,
    spread,
    pack_up,
    pack_down,
    from_low,
    from_high,
    owners,
    bids,
    damp_vec,
    disp,
    vel,
    imass,
    foot_sum,
    index,
    row_buf,
    rows_all,
    load_sem,
    store_sem,
    x_send,
    x_recv,
    y_send,
    y_recv,
    a_send,
    a_recv,
    b_send,
    b_recv,
):
    gx = lax.axis_index("gx")
    gy = lax.axis_index("gy")
    me = gx * n_gy + gy
    n_dev = n_gx * n_gy
    gx_up, gx_down = lax.rem(gx + 1, n_gx), lax.rem(gx + n_gx - 1, n_gx)
    gy_up, gy_down = lax.rem(gy + 1, n_gy), lax.rem(gy + n_gy - 1, n_gy)
    cells_x, cells_z, cells_y = soil.shape[1:]
    tiles_z = cells_z // 8
    buildings = foot.shape[0]
    inner = pl.ds(COL, cells_x)
    rows = pl.ds(ROW, cells_z)

    def load(k, source, target):
        copy = pltpu.make_async_copy(source, target, load_sem.at[k])
        copy.start()
        return copy

    load_stress = load(0, soil.at[pl.ds(SXX, 6)], first.at[pl.ds(SXX, 6), inner, rows])
    load_velocity = load(1, soil.at[pl.ds(0, 3)], first.at[pl.ds(0, 3), inner, rows])
    load_material = load(2, material, raw)
    load_matrix = load(3, stiff, matrix)

    barrier = pltpu.get_barrier_semaphore()
    for k in range(1, n_gx):
        pl.semaphore_signal(
            barrier, inc=1, device_id={"gx": lax.rem(gx + k, n_gx)}, device_id_type=MESH
        )
    for k in range(1, n_gy):
        pl.semaphore_signal(
            barrier, inc=1, device_id={"gy": lax.rem(gy + k, n_gy)}, device_id_type=MESH
        )

    zero_tile = jnp.zeros((8, cells_y), F32)

    def clear(x, carry):
        for ref, members in (
            (first, (SZZ, SXZ, SYZ)),
            (vel_a, (0, 1, 2)),
            (str_a, (2, 4, 5)),
            (vel_b, (0, 1, 2)),
        ):
            for member in members:
                ref[member, x, pl.ds(0, 8), :] = zero_tile
                ref[member, x, pl.ds(ROW + cells_z, 8), :] = zero_tile
        return carry

    lax.fori_loop(COL, COL + cells_x, clear, 0)

    pl.semaphore_wait(barrier, n_gx + n_gy - 2)

    def remote(source, target, send, recv, device):
        copy = pltpu.make_async_remote_copy(
            src_ref=source,
            dst_ref=target,
            send_sem=send,
            recv_sem=recv,
            device_id=device,
            device_id_type=MESH,
        )
        copy.start()
        return copy

    def send_x(stage, source, start, target, groups, up, down):
        copies = []
        for k, (origin, member, size) in enumerate(groups):
            ids, into = pl.ds(origin, size), pl.ds(member, size)
            copies.append(
                remote(
                    source.at[ids, pl.ds(start + cells_x - up, up), rows if start else pl.ds(0, cells_z)],
                    target.at[into, pl.ds(COL - up, up), rows],
                    x_send.at[stage, k, 0],
                    x_recv.at[stage, k, 0],
                    {"gx": gx_up},
                )
            )
            copies.append(
                remote(
                    source.at[ids, pl.ds(start, down), rows if start else pl.ds(0, cells_z)],
                    target.at[into, pl.ds(COL + cells_x, down), rows],
                    x_send.at[stage, k, 1],
                    x_recv.at[stage, k, 1],
                    {"gx": gx_down},
                )
            )
        return copies

    def send_y(stage):
        return [
            remote(
                pack_up.at[stage],
                from_low.at[stage],
                y_send.at[stage, 0],
                y_recv.at[stage, 0],
                {"gy": gy_up},
            ),
            remote(
                pack_down.at[stage],
                from_high.at[stage],
                y_send.at[stage, 1],
                y_recv.at[stage, 1],
                {"gy": gy_down},
            ),
        ]

    def finish(copies):
        for copy in copies:
            copy.wait()

    def outside_zero_x(ref, members, low, high):
        @pl.when(gx == 0)
        def _():
            for member in members:
                for layer in range(low):
                    ref[member, COL - 1 - layer, rows, :] = jnp.zeros((cells_z, cells_y), F32)

        @pl.when(gx == n_gx - 1)
        def _():
            for member in members:
                for layer in range(high):
                    ref[member, COL + cells_x + layer, rows, :] = jnp.zeros((cells_z, cells_y), F32)

    def outside_zero_y(stage):
        @pl.when(gy == 0)
        def _():
            from_low[stage] = jnp.zeros(from_low.shape[1:], F32)

        @pl.when(gy == n_gy - 1)
        def _():
            from_high[stage] = jnp.zeros(from_high.shape[1:], F32)

    lane = iota((8, cells_y), 1)
    lane_single, lane_double = lane, lane // 2

    def pack(packed, values, tile, up):
        ups, downs = packed
        if up == 2:
            up_mask, down_mask = lane_double == tile, lane_single == tile
            up_shift, down_shift = lax.rem(2 * tile + 2, 128), tile
        else:
            up_mask, down_mask = lane_single == tile, lane_double == tile
            up_shift, down_shift = tile + 1, 2 * tile
        ups = tuple(
            jnp.where(up_mask, rolled(value, up_shift), old) for value, old in zip(values, ups)
        )
        downs = tuple(
            jnp.where(down_mask, rolled(value, down_shift), old) for value, old in zip(values, downs)
        )
        return ups, downs

    nothing = (tuple([zero_tile] * 3), tuple([zero_tile] * 3))

    def keep_packed(stage, packed):
        for k in range(3):
            pack_up[stage, k] = packed[0][k]
            pack_down[stage, k] = packed[1][k]

    def along_y(value, stage, k, tile, forward):
        if forward:
            low = jnp.where(
                lane == cells_y - 1, rolled(from_low[stage, k], lax.rem(127 - tile, 128)), value
            )
            beyond = rolled(from_high[stage, k], lax.rem(128 - 2 * tile, 128))
            near, far = jnp.where(lane < 1, beyond, value), jnp.where(lane < 2, beyond, value)
            return stencil(rolled(near, 127), value, rolled(far, 126), rolled(low, 1))
        beyond = rolled(from_low[stage, k], lax.rem(254 - 2 * tile, 128))
        near = jnp.where(lane == cells_y - 1, beyond, value)
        far = jnp.where(lane >= cells_y - 2, beyond, value)
        high = jnp.where(lane < 1, rolled(from_high[stage, k], lax.rem(128 - tile, 128)), value)
        return stencil(value, rolled(near, 1), rolled(high, 127), rolled(far, 2))

    def at(ref, member, x, row):
        return ref[member, x, pl.ds(row, 8), :]

    def along_x(ref, member, x, row, forward):
        shift = 1 if forward else 0
        return stencil(
            at(ref, member, x + shift, row),
            at(ref, member, x + shift - 1, row),
            at(ref, member, x + shift + 1, row),
            at(ref, member, x + shift - 2, row),
        )

    def along_z(ref, member, x, row, forward):
        shift = 1 if forward else 0
        return stencil(
            at(ref, member, x, row + shift),
            at(ref, member, x, row + shift - 1),
            at(ref, member, x, row + shift + 1),
            at(ref, member, x, row + shift - 2),
        )

    def velocity_layers(stage, stress, base, old, new, begin, end, packed):
        sxx, syy, szz, sxy, sxz, syz = range(base, base + 6)

        def layer(i, packed):
            cell = lax.rem(i + cells_x - 1, cells_x)
            x = cell + COL
            for z in range(tiles_z):
                row = ROW + 8 * z
                tile = cell * tiles_z + z
                y_of = [
                    along_y(at(stress, member, x, row), stage, k, tile, False)
                    for k, member in enumerate((sxy, syy, syz))
                ]
                accel = (
                    along_x(stress, sxx, x, row, False) + y_of[0] + along_z(stress, sxz, x, row, False),
                    along_x(stress, sxy, x, row, False) + y_of[1] + along_z(stress, syz, x, row, False),
                    along_x(stress, sxz, x, row, False) + y_of[2] + along_z(stress, szz, x, row, False),
                )
                density = coef[0, cell, pl.ds(8 * z, 8), :]
                after = [at(old, k, x, row) + density * accel[k] for k in range(3)]
                for k in range(3):
                    new[k, x, pl.ds(row, 8), :] = after[k]
                packed = pack(packed, after, tile, 1)
            return packed

        return lax.fori_loop(begin, end, layer, packed)

    def stress_layers(stage, moving, stress, base, new, new_x, new_row, begin, end, packed):
        def layer(i, packed):
            cell = lax.rem(i + cells_x - 2, cells_x)
            x = cell + COL
            for z in range(tiles_z):
                row = ROW + 8 * z
                tile = cell * tiles_z + z
                y_of = [
                    along_y(at(moving, k, x, row), stage, k, tile, True) for k in range(3)
                ]
                x_of = [along_x(moving, k, x, row, True) for k in range(3)]
                z_of = [along_z(moving, k, x, row, True) for k in range(3)]
                lame = coef[1, cell, pl.ds(8 * z, 8), :]
                shear = coef[2, cell, pl.ds(8 * z, 8), :]
                volume = lame * (x_of[0] + y_of[1] + z_of[2])
                twice = shear + shear
                change = (
                    volume + twice * x_of[0],
                    volume + twice * y_of[1],
                    volume + twice * z_of[2],
                    shear * (y_of[0] + x_of[1]),
                    shear * (z_of[0] + x_of[2]),
                    shear * (z_of[1] + y_of[2]),
                )
                after = [at(stress, base + k, x, row) + change[k] for k in range(6)]
                for k in range(6):
                    new[k, cell + new_x, pl.ds(new_row + 8 * z, 8), :] = after[k]
                if packed is not None:
                    packed = pack(packed, (after[3], after[1], after[5]), tile, 2)
            return packed

        if packed is None:

            def bare(i, carry):
                layer(i, None)
                return carry

            lax.fori_loop(begin, end, bare, 0)
            return None
        return lax.fori_loop(begin, end, layer, packed)

    stress_groups = ((SXX, SXX, 1), (SXY, SXY, 2))
    inner_groups = ((0, 0, 1), (3, 3, 2))
    move_groups = ((0, 0, 3),)

    sent = send_x(0, soil, 0, first, stress_groups, 2, 1)
    load_stress.wait()

    def pack_first(cell, packed):
        for z in range(tiles_z):
            values = [at(first, k, cell + COL, ROW + 8 * z) for k in (SXY, SYY, SYZ)]
            packed = pack(packed, values, cell * tiles_z + z, 2)
        return packed

    keep_packed(0, lax.fori_loop(0, cells_x, pack_first, nothing))
    sent += send_y(0)

    load_material.wait()

    def widen(cell, carry):
        for k in range(3):
            coef[k, cell] = TIME_SOIL * raw[k, cell].astype(F32)
        return carry

    lax.fori_loop(0, cells_x, widen, 0)
    load_velocity.wait()

    finish(sent)
    outside_zero_x(first, (SXX, SXY, SXZ), 2, 1)
    outside_zero_y(0)

    packed = velocity_layers(0, first, SXX, first, vel_a, 0, 3, nothing)
    sent = send_x(1, vel_a, COL, vel_a, move_groups, 1, 2)
    packed = velocity_layers(0, first, SXX, first, vel_a, 3, cells_x, packed)
    keep_packed(1, packed)
    sent += send_y(1)

    big = (128, 128)
    big_lane = iota(big, 1)
    big_lane_f = big_lane.astype(F32)
    small_row = iota((8, 128), 0)
    small_lane = iota((8, 128), 1)

    for b in range(buildings):
        for h in range(2):
            piece = pl.ds(b * 256 + h * 128, 128)
            live = iota((1, 128), 1) + h * 128 < count[b]
            for end in range(2):
                nodes = links[pl.ds(end, 1), piece]
                index[b, h * 2 + end] = jnp.broadcast_to(nodes, (8, 128))
                kept = jnp.where(live, nodes, -1).astype(F32)
                columns = jnp.broadcast_to(kept, big).T
                spread[b, pl.ds(h * 128, 128), pl.ds(end * 128, 128)] = (
                    jnp.where(columns == big_lane_f, 1.0, 0.0).astype(BF16)
                )

    group_of = (iota((n_dev, 128), 1) // 2) % GROUPS
    holder = iota((n_dev, 128), 0)
    for j in range(1, GROUPS):
        entries = table[pl.ds(j - 1, 1), :].astype(F32)
        columns = jnp.broadcast_to(entries, (128, n_dev)).T.astype(jnp.int32)
        holder = jnp.where(group_of == j, columns, holder)
    owners[...] = holder

    bid = jnp.zeros((16, 128), F32)
    for b in range(buildings):
        cell = foot[pl.ds(b, 1), :]
        place_x = jnp.where(iota((16, 128), 0) == cell // cells_y, float(b), 0.0).astype(BF16)
        place_y = jnp.where(iota(big, 0) == cell % cells_y, 1.0, 0.0).astype(BF16)
        bid += lax.dot_general(
            place_x, place_y, (((1,), (1,)), ((), ())), preferred_element_type=F32
        )
    bids[...] = bid[0:8].astype(jnp.int32)

    blank = jnp.zeros((2, 128), F32)
    for b in range(buildings):
        piece = pl.ds(b * 128, 128)
        disp[b] = jnp.concatenate([frame_disp[:, piece], blank], 0)
        vel[b] = jnp.concatenate([frame_vel[:, piece], blank], 0)
        imass[b] = TIME_FRAME * jnp.concatenate([inverse_mass[:, piece], blank], 0)
        foot_sum[b] = jnp.zeros((8, 128), F32)

    finish(sent)
    outside_zero_x(vel_a, (0, 1, 2), 1, 2)
    outside_zero_y(1)

    packed = stress_layers(1, vel_a, first, SXX, str_a, COL, ROW, 0, 3, nothing)
    sent = send_x(2, str_a, COL, str_a, inner_groups, 2, 1)
    packed = stress_layers(1, vel_a, first, SXX, str_a, COL, ROW, 3, cells_x, packed)
    keep_packed(2, packed)
    sent += send_y(2)
    finish(sent)
    outside_zero_x(str_a, (0, 3, 4), 2, 1)
    outside_zero_y(2)

    packed = velocity_layers(2, str_a, 0, vel_a, vel_b, 0, 3, nothing)
    sent = send_x(3, vel_b, COL, vel_b, move_groups, 1, 2)
    packed = velocity_layers(2, str_a, 0, vel_a, vel_b, 3, cells_x, packed)
    keep_packed(3, packed)
    sent += send_y(3)

    store_velocity = pltpu.make_async_copy(
        vel_b.at[:, inner, rows], soil_out.at[pl.ds(0, 3)], store_sem.at[0]
    )
    store_velocity.start()

    surface = [vel_b[k, inner, ROW, :] for k in range(3)]
    dash = dashpot[...]
    terms = [dash * surface[0], dash * surface[1], dash * surface[2], dash]
    bid = bids[...]
    sums = [
        jnp.sum(jnp.where(bid == b, term, 0.0), axis=0, keepdims=True)
        for term in terms
        for b in range(buildings)
    ]
    sums = jnp.concatenate(sums + [jnp.zeros((128 - len(sums), 128), F32)], 0)
    mine = jnp.sum(sums.T, axis=0, keepdims=True)

    def gather_rows(turn, value):
        row_buf[turn, gy] = value
        sent = [
            remote(
                row_buf.at[turn, gy],
                row_buf.at[turn, gy],
                a_send.at[turn, k - 1],
                a_recv.at[turn, k - 1],
                {"gy": lax.rem(gy + k, n_gy)},
            )
            for k in range(1, n_gy)
        ]
        finish(sent)
        rows_all[turn, gx] = row_buf[turn].reshape(n_gy, 128)
        return [
            remote(
                rows_all.at[turn, gx],
                rows_all.at[turn, gx],
                b_send.at[turn, k - 1],
                b_recv.at[turn, k - 1],
                {"gx": lax.rem(gx + k, n_gx)},
            )
            for k in range(1, n_gx)
        ]

    gathering = gather_rows(0, mine)

    finish(sent)
    outside_zero_x(vel_b, (0, 1, 2), 1, 2)
    outside_zero_y(3)
    stress_layers(3, vel_b, str_a, 0, str_b, 0, 0, 0, cells_x, None)
    store_stress = pltpu.make_async_copy(str_b, soil_out.at[pl.ds(3, 6)], store_sem.at[1])
    store_stress.start()

    finish(gathering)
    arrived = rows_all[0].reshape(n_dev, 128)
    owned = jnp.sum(jnp.where(owners[...] == me, arrived, 0.0), axis=0, keepdims=True)
    owned = jnp.broadcast_to(owned, (8, 128))

    at_footing = (small_row < 3) & (small_lane == 0)
    load_matrix.wait()
    drives, dampers = [], []
    for b in range(buildings):
        pick = jnp.minimum(small_row * buildings + b, 127)
        drives.append(jnp.where(at_footing, lane_gather(owned, pick), 0.0))
        pick = jnp.full((8, 128), 3 * buildings + b, jnp.int32)
        dampers.append(jnp.where(at_footing, lane_gather(owned, pick), 0.0))
    for b in range(buildings):
        damp_vec[0, b] = drives[b]
        damp_vec[1, b] = dampers[b]

    def frame_step(step, carry):
        for b in range(buildings):
            place = disp[b]
            forces = []
            for h in range(2):
                ends = (
                    lane_gather(place, index[b, h * 2]),
                    lane_gather(place, index[b, h * 2 + 1]),
                )
                piece = pl.ds(b * 256 + h * 128, 128)
                total = None
                for a in range(12):
                    row = ends[a // 6][a % 6 : a % 6 + 1, :]
                    term = matrix[a, :, piece] * row
                    total = term if total is None else total + term
                forces.append(jnp.concatenate([total, jnp.zeros((4, 128), F32)], 0))
            forces = jnp.concatenate(forces, 1)
            high = forces.astype(BF16)
            low = (forces - high.astype(F32)).astype(BF16)
            parts = jnp.dot(
                jnp.concatenate([high, low], 0), spread[b], preferred_element_type=F32
            )
            parts = parts[0:16] + parts[16:32]
            internal = parts[0:8, 0:128] + parts[6:14, 128:256]
            speed = vel[b]
            loads = damp_vec[0, b] - damp_vec[1, b] * speed - internal
            speed = speed + imass[b] * loads
            vel[b] = speed
            disp[b] = place + TIME_FRAME * speed
            foot_sum[b] += speed
        return carry

    lax.fori_loop(0, FRAME_STEPS, frame_step, 0)

    back = jnp.zeros((8, 128), F32)
    for b in range(buildings):
        whole = jnp.broadcast_to(foot_sum[b][:, 0:1], (8, 128))
        back = jnp.where(small_lane == small_row * buildings + b, whole, back)
    back = jnp.where(small_row < 3, back, 0.0)
    gathering = gather_rows(1, jnp.sum(back, axis=0, keepdims=True))
    for b in range(buildings):
        piece = pl.ds(b * 128, 128)
        disp_out[:, piece] = disp[b][0:6]
        vel_out[:, piece] = vel[b][0:6]
    wanted = owners[pl.ds(me, 1), :]
    finish(gathering)
    arrived = rows_all[1].reshape(n_dev, 128)
    held = jnp.where(iota((n_dev, 128), 0) == wanted, arrived, 0.0)
    held = jnp.broadcast_to(jnp.sum(held, axis=0, keepdims=True), (8, 128))
    for k in range(3):
        total = lane_gather(held, bid + k * buildings)
        force_out[k] = dash * (FRAME_STEPS * surface[k] - total)

    finish(sent[:0])
    store_velocity.wait()
    store_stress.wait()


def shards(n_gx, n_gy, *args):
    soil, material, dashpot, foot, table, stiff, links = args[:7]
    cells_x, cells_z, cells_y = soil.shape[1:]
    buildings = foot.shape[0]
    wide = (cells_x + 2 * COL, cells_z + 2 * ROW, cells_y)
    n_dev = n_gx * n_gy
    anywhere = pl.BlockSpec(memory_space=pl.ANY)
    vmem = pl.BlockSpec(memory_space=pltpu.VMEM)
    smem = pl.BlockSpec(memory_space=pltpu.SMEM)
    dma = pltpu.SemaphoreType.DMA
    return pl.pallas_call(
        functools.partial(kernel, n_gx, n_gy),
        out_shape=(
            jax.ShapeDtypeStruct(soil.shape, F32),
            jax.ShapeDtypeStruct((3, cells_x, cells_y), F32),
            jax.ShapeDtypeStruct(args[9].shape, F32),
            jax.ShapeDtypeStruct(args[10].shape, F32),
        ),
        in_specs=[anywhere, anywhere, vmem, vmem, vmem, anywhere, vmem, smem, vmem, vmem, vmem],
        out_specs=(anywhere, vmem, vmem, vmem),
        scratch_shapes=[
            pltpu.VMEM((9,) + wide, F32),
            pltpu.VMEM((3,) + wide, F32),
            pltpu.VMEM((6,) + wide, F32),
            pltpu.VMEM((3,) + wide, F32),
            pltpu.VMEM((6, cells_x, cells_z, cells_y), F32),
            pltpu.VMEM(material.shape, BF16),
            pltpu.VMEM(material.shape, F32),
            pltpu.VMEM(stiff.shape, F32),
            pltpu.VMEM((buildings, 256, 256), BF16),
            pltpu.VMEM((4, 3, 8, 128), F32),
            pltpu.VMEM((4, 3, 8, 128), F32),
            pltpu.VMEM((4, 3, 8, 128), F32),
            pltpu.VMEM((4, 3, 8, 128), F32),
            pltpu.VMEM((n_dev, 128), jnp.int32),
            pltpu.VMEM((8, 128), jnp.int32),
            pltpu.VMEM((2, buildings, 8, 128), F32),
            pltpu.VMEM((buildings, 8, 128), F32),
            pltpu.VMEM((buildings, 8, 128), F32),
            pltpu.VMEM((buildings, 8, 128), F32),
            pltpu.VMEM((buildings, 8, 128), F32),
            pltpu.VMEM((buildings, 4, 8, 128), jnp.int32),
            pltpu.VMEM((2, n_gy, 1, 128), F32),
            pltpu.VMEM((2, n_gx, n_gy, 128), F32),
            dma((4,)),
            dma((2,)),
            dma((4, 2, 2)),
            dma((4, 2, 2)),
            dma((4, 2)),
            dma((4, 2)),
            dma((2, n_gy - 1)),
            dma((2, n_gy - 1)),
            dma((2, n_gx - 1)),
            dma((2, n_gx - 1)),
        ],
        compiler_params=pltpu.CompilerParams(
            collective_id=0, has_side_effects=True, vmem_limit_bytes=48 * 1024 * 1024
        ),
    )(*args)


def solution(mesh):
    placed = (
        P(None, "gx", None, "gy"),
        P(None, "gx", None, "gy"),
        P("gx", "gy"),
        P(("gx", "gy"), None),
        P(),
        P(None, None, ("gx", "gy")),
        P(None, ("gx", "gy")),
        P(("gx", "gy")),
        P(None, ("gx", "gy")),
        P(None, ("gx", "gy")),
        P(None, ("gx", "gy")),
    )
    return jax.shard_map(
        functools.partial(shards, mesh.shape["gx"], mesh.shape["gy"]),
        mesh=mesh,
        in_specs=placed,
        out_specs=(
            P(None, "gx", None, "gy"),
            P(None, "gx", "gy"),
            P(None, ("gx", "gy")),
            P(None, ("gx", "gy")),
        ),
        check_vma=False,
    )
```

```python
import functools

import jax
import jax.numpy as jnp
from jax import lax
from jax.experimental import pallas as pl
from jax.experimental.pallas import tpu as pltpu
from jax.sharding import PartitionSpec as P

GROUPS = 4
FRAME_STEPS = 4
NEAR = 9.0 / 8.0
FAR = -1.0 / 24.0
TIME_SOIL = 0.18
TIME_FRAME = 0.05
MESH = pl.DeviceIdType.MESH
ROW = 8
COL = 2
F32 = jnp.float32
BF16 = jnp.bfloat16

VX, VY, VZ, SXX, SYY, SZZ, SXY, SXZ, SYZ = range(9)


def lane_gather(values, index):
    return lax.gather(
        values,
        index[:, :, None],
        lax.GatherDimensionNumbers(
            offset_dims=(),
            collapsed_slice_dims=(1,),
            start_index_map=(1,),
            operand_batching_dims=(0,),
            start_indices_batching_dims=(0,),
        ),
        (1, 1),
        mode=lax.GatherScatterMode.PROMISE_IN_BOUNDS,
    )


def iota(shape, dim):
    return lax.broadcasted_iota(jnp.int32, shape, dim)


def stencil(near_high, near_low, far_high, far_low):
    return NEAR * (near_high - near_low) + FAR * (far_high - far_low)


def rolled(value, shift):
    return pltpu.roll(value, shift, 1)


def kernel(
    n_gx,
    n_gy,
    soil,
    material,
    hbm_dashpot,
    hbm_foot,
    hbm_table,
    stiff,
    hbm_links,
    hbm_count,
    hbm_inverse_mass,
    hbm_frame_disp,
    hbm_frame_vel,
    moved_out,
    str_b,
    force_out,
    disp_out,
    vel_out,
    first,
    vel_a,
    str_a,
    vel_b,
    raw,
    coef,
    matrix,
    dashpot,
    foot,
    table,
    links,
    count,
    inverse_mass,
    frame_disp,
    frame_vel,
    spread,
    band,
    edges,
    from_low,
    from_high,
    correction,
    owners,
    bids,
    damp_vec,
    disp,
    vel,
    imass,
    foot_sum,
    internal,
    index,
    row_buf,
    rows_all,
    load_sem,
    x_send,
    x_recv,
    y_send,
    y_recv,
    a_send,
    a_recv,
    b_send,
    b_recv,
):
    gx = lax.axis_index("gx")
    gy = lax.axis_index("gy")
    me = gx * n_gy + gy
    n_dev = n_gx * n_gy
    gx_up, gx_down = lax.rem(gx + 1, n_gx), lax.rem(gx + n_gx - 1, n_gx)
    gy_up, gy_down = lax.rem(gy + 1, n_gy), lax.rem(gy + n_gy - 1, n_gy)
    cells_x, cells_z, cells_y = soil.shape[1:]
    tiles_z = cells_z // 8
    buildings = foot.shape[0]
    inner = pl.ds(COL, cells_x)
    rows = pl.ds(ROW, cells_z)

    def load(k, source, target):
        copy = pltpu.make_async_copy(source, target, load_sem.at[k])
        copy.start()
        return copy

    load_stress = load(0, soil.at[pl.ds(SXX, 6)], first.at[pl.ds(SXX, 6), inner, rows])
    load_velocity = load(1, soil.at[pl.ds(0, 3)], first.at[pl.ds(0, 3), inner, rows])
    load_material = load(2, material, raw)
    load_small = [
        load(4 + k, source, target)
        for k, (source, target) in enumerate(
            (
                (hbm_dashpot, dashpot),
                (hbm_foot, foot),
                (hbm_table, table),
                (hbm_links, links),
                (hbm_count, count),
                (hbm_inverse_mass, inverse_mass),
                (hbm_frame_disp, frame_disp),
                (hbm_frame_vel, frame_vel),
            )
        )
    ]
    load_matrix = load(3, stiff, matrix)

    barrier = pltpu.get_barrier_semaphore()
    for k in range(1, n_gx):
        pl.semaphore_signal(
            barrier, inc=1, device_id={"gx": lax.rem(gx + k, n_gx)}, device_id_type=MESH
        )
    for k in range(1, n_gy):
        pl.semaphore_signal(
            barrier, inc=1, device_id={"gy": lax.rem(gy + k, n_gy)}, device_id_type=MESH
        )

    zero_tile = jnp.zeros((8, cells_y), F32)

    def clear(x, carry):
        for ref, members in (
            (first, (SZZ, SXZ, SYZ)),
            (vel_a, (0, 1, 2)),
            (str_a, (2, 4, 5)),
            (vel_b, (0, 1, 2)),
        ):
            for member in members:
                ref[member, x, pl.ds(0, 8), :] = zero_tile
                ref[member, x, pl.ds(ROW + cells_z, 8), :] = zero_tile
        return carry

    lax.fori_loop(COL, COL + cells_x, clear, 0)

    pl.semaphore_wait(barrier, n_gx + n_gy - 2)

    def remote(source, target, send, recv, device):
        copy = pltpu.make_async_remote_copy(
            src_ref=source,
            dst_ref=target,
            send_sem=send,
            recv_sem=recv,
            device_id=device,
            device_id_type=MESH,
        )
        copy.start()
        return copy

    def send_x(stage, source, start, target, groups, up, down):
        copies = []
        for k, (origin, member, size) in enumerate(groups):
            ids, into = pl.ds(origin, size), pl.ds(member, size)
            copies.append(
                remote(
                    source.at[ids, pl.ds(start + cells_x - up, up), rows if start else pl.ds(0, cells_z)],
                    target.at[into, pl.ds(COL - up, up), rows],
                    x_send.at[stage, k, 0],
                    x_recv.at[stage, k, 0],
                    {"gx": gx_up},
                )
            )
            copies.append(
                remote(
                    source.at[ids, pl.ds(start, down), rows if start else pl.ds(0, cells_z)],
                    target.at[into, pl.ds(COL + cells_x, down), rows],
                    x_send.at[stage, k, 1],
                    x_recv.at[stage, k, 1],
                    {"gx": gx_down},
                )
            )
        return copies

    def send_y(stage):
        return [
            remote(
                edges.at[stage],
                from_low.at[stage],
                y_send.at[stage, 0],
                y_recv.at[stage, 0],
                {"gy": gy_up},
            ),
            remote(
                edges.at[stage],
                from_high.at[stage],
                y_send.at[stage, 1],
                y_recv.at[stage, 1],
                {"gy": gy_down},
            ),
        ]

    leaving = []

    def finish(copies):
        for copy in copies:
            copy.wait_recv()
        leaving.extend(copies)

    def outside_zero_x(ref, members, low, high):
        @pl.when(gx == 0)
        def _():
            for member in members:
                for layer in range(low):
                    ref[member, COL - 1 - layer, rows, :] = jnp.zeros((cells_z, cells_y), F32)

        @pl.when(gx == n_gx - 1)
        def _():
            for member in members:
                for layer in range(high):
                    ref[member, COL + cells_x + layer, rows, :] = jnp.zeros((cells_z, cells_y), F32)

    lane = iota((8, cells_y), 1)
    slot = lane & 3

    def pack(stage, values, cell):
        group = cell // 4
        for k in range(3):
            packed = edges[stage, k, group]
            for z in range(tiles_z):
                place = (cell & 3) * tiles_z + z
                packed = jnp.where(
                    lane >> 2 == place, rolled(values[z][k], (4 * place + 2) & 127), packed
                )
            edges[stage, k, group] = packed

    def prepare(stage, forward):
        for k in range(3):
            for group in range(edges.shape[2]):
                low = jnp.where(gy > 0, from_low[stage, k, group], 0.0)
                high = jnp.where(gy < n_gy - 1, from_high[stage, k, group], 0.0)
                beyond = jnp.where(slot < 2, low, high)
                back_2, back_1 = rolled(beyond, 126), rolled(beyond, 127)
                on_1, on_2 = rolled(beyond, 1), rolled(beyond, 2)
                if forward:
                    value = jnp.where(
                        slot == 0,
                        FAR * back_2,
                        jnp.where(
                            slot == 1,
                            NEAR * back_1 + FAR * back_2,
                            jnp.where(slot == 2, -FAR * on_1, 0.0),
                        ),
                    )
                else:
                    value = jnp.where(
                        slot == 1,
                        FAR * back_1,
                        jnp.where(
                            slot == 2,
                            -NEAR * on_1 - FAR * on_2,
                            jnp.where(slot == 3, -FAR * on_2, 0.0),
                        ),
                    )
                correction[stage, k, group] = value

    at_edge = (lane < 2) | (lane >= cells_y - 2)

    def along_y(ref, members, stage, cell, forward):
        parts = []
        for member in members:
            value = ref[member, cell + COL, rows, :]
            high = value.astype(BF16)
            low = (value - high.astype(F32)).astype(BF16)
            parts.append(jnp.concatenate([high, low], 1))
        both = jnp.dot(
            jnp.concatenate(parts, 0), band[int(forward)], preferred_element_type=F32
        )
        group = cell // 4
        result = []
        for z in range(tiles_z):
            shift = (254 - 4 * ((cell & 3) * tiles_z + z)) & 127
            line = []
            for k in range(3):
                tile = slice(k * cells_z + 8 * z, k * cells_z + 8 * z + 8)
                inside = NEAR * both[tile, 0:128] + FAR * both[tile, 128:256]
                line.append(
                    inside + jnp.where(at_edge, rolled(correction[stage, k, group], shift), 0.0)
                )
            result.append(line)
        return result

    def at(ref, member, x, row):
        return ref[member, x, pl.ds(row, 8), :]

    def along_x(ref, member, x, row, forward):
        shift = 1 if forward else 0
        return stencil(
            at(ref, member, x + shift, row),
            at(ref, member, x + shift - 1, row),
            at(ref, member, x + shift + 1, row),
            at(ref, member, x + shift - 2, row),
        )

    def along_z(ref, member, x, row, forward):
        shift = 1 if forward else 0
        return stencil(
            at(ref, member, x, row + shift),
            at(ref, member, x, row + shift - 1),
            at(ref, member, x, row + shift + 1),
            at(ref, member, x, row + shift - 2),
        )

    def velocity_layers(stage, stress, base, old, new, begin, end, out=None):
        sxx, syy, szz, sxy, sxz, syz = range(base, base + 6)

        def layer(i, carry):
            cell = (i + cells_x - 1) & (cells_x - 1)
            x = cell + COL
            y_all = along_y(stress, (sxy, syy, syz), stage, cell, False)
            results = []
            for z in range(tiles_z):
                row = ROW + 8 * z
                y_of = y_all[z]
                accel = (
                    along_x(stress, sxx, x, row, False) + y_of[0] + along_z(stress, sxz, x, row, False),
                    along_x(stress, sxy, x, row, False) + y_of[1] + along_z(stress, syz, x, row, False),
                    along_x(stress, sxz, x, row, False) + y_of[2] + along_z(stress, szz, x, row, False),
                )
                density = coef[0, cell, pl.ds(8 * z, 8), :]
                after = [at(old, k, x, row) + density * accel[k] for k in range(3)]
                for k in range(3):
                    new[k, x, pl.ds(row, 8), :] = after[k]
                    if out is not None:
                        out[k, cell, pl.ds(8 * z, 8), :] = after[k]
                results.append(after)
            pack(stage + 1, results, cell)
            return carry

        lax.fori_loop(begin, end, layer, 0)

    def stress_layers(stage, moving, stress, base, new, new_x, new_row, begin, end, packing):
        def layer(i, carry):
            cell = (i + cells_x - 2) & (cells_x - 1)
            x = cell + COL
            y_all = along_y(moving, (0, 1, 2), stage, cell, True)
            results = []
            for z in range(tiles_z):
                row = ROW + 8 * z
                y_of = y_all[z]
                x_of = [along_x(moving, k, x, row, True) for k in range(3)]
                z_of = [along_z(moving, k, x, row, True) for k in range(3)]
                lame = coef[1, cell, pl.ds(8 * z, 8), :]
                shear = coef[2, cell, pl.ds(8 * z, 8), :]
                volume = lame * (x_of[0] + y_of[1] + z_of[2])
                twice = shear + shear
                change = (
                    volume + twice * x_of[0],
                    volume + twice * y_of[1],
                    volume + twice * z_of[2],
                    shear * (y_of[0] + x_of[1]),
                    shear * (z_of[0] + x_of[2]),
                    shear * (z_of[1] + y_of[2]),
                )
                after = [at(stress, base + k, x, row) + change[k] for k in range(6)]
                for k in range(6):
                    new[k, cell + new_x, pl.ds(new_row + 8 * z, 8), :] = after[k]
                results.append((after[3], after[1], after[5]))
            if packing:
                pack(stage + 1, results, cell)
            return carry

        lax.fori_loop(begin, end, layer, 0)

    stress_groups = ((SXX, SXX, 1), (SXY, SXY, 2))
    inner_groups = ((0, 0, 1), (3, 3, 2))
    move_groups = ((0, 0, 3),)

    sent = send_x(0, soil, 0, first, stress_groups, 2, 1)
    load_stress.wait()

    edges[...] = jnp.zeros(edges.shape, F32)

    def pack_first(cell, carry):
        values = [
            [at(first, k, cell + COL, ROW + 8 * z) for k in (SXY, SYY, SYZ)] for z in range(tiles_z)
        ]
        pack(0, values, cell)
        return carry

    lax.fori_loop(0, cells_x, pack_first, 0)
    sent += send_y(0)

    source = iota((256, 256), 0) & 127
    column = iota((256, 256), 1)
    wanted = column & 127
    for forward in range(2):
        reach = jnp.where(column < 128, 0, 1)
        plus = source == wanted + forward + reach
        minus = source == wanted + forward - 1 - reach
        band[forward] = jnp.where(plus, 1.0, jnp.where(minus, -1.0, 0.0)).astype(BF16)

    load_material.wait()

    def widen(cell, carry):
        for k in range(3):
            coef[k, cell] = TIME_SOIL * raw[k, cell].astype(F32)
        return carry

    lax.fori_loop(0, cells_x, widen, 0)
    load_velocity.wait()

    finish(sent)
    outside_zero_x(first, (SXX, SXY, SXZ), 2, 1)
    prepare(0, False)

    velocity_layers(0, first, SXX, first, vel_a, 0, 3)
    sent = send_x(1, vel_a, COL, vel_a, move_groups, 1, 2)
    velocity_layers(0, first, SXX, first, vel_a, 3, cells_x)
    sent += send_y(1)

    for copy in load_small:
        copy.wait()
    big = (128, 128)
    big_lane = iota(big, 1)
    big_lane_f = big_lane.astype(F32)
    small_row = iota((8, 128), 0)
    small_lane = iota((8, 128), 1)

    for b in range(buildings):
        for h in range(2):
            piece = pl.ds(b * 256 + h * 128, 128)
            live = iota((1, 128), 1) + h * 128 < count[b]
            for end in range(2):
                nodes = links[pl.ds(end, 1), piece]
                index[b, h * 2 + end] = jnp.broadcast_to(nodes, (8, 128))
                kept = jnp.where(live, nodes, -1).astype(F32)
                columns = jnp.broadcast_to(kept, big).T
                spread[b, pl.ds(h * 128, 128), pl.ds(end * 128, 128)] = (
                    jnp.where(columns == big_lane_f, 1.0, 0.0).astype(BF16)
                )

    group_of = (iota((n_dev, 128), 1) // 2) % GROUPS
    holder = iota((n_dev, 128), 0)
    for j in range(1, GROUPS):
        entries = table[pl.ds(j - 1, 1), :].astype(F32)
        columns = jnp.broadcast_to(entries, (128, n_dev)).T.astype(jnp.int32)
        holder = jnp.where(group_of == j, columns, holder)
    owners[...] = holder

    bid = jnp.zeros((16, 128), F32)
    for b in range(buildings):
        cell = foot[pl.ds(b, 1), :]
        place_x = jnp.where(iota((16, 128), 0) == cell // cells_y, float(b), 0.0).astype(BF16)
        place_y = jnp.where(iota(big, 0) == cell % cells_y, 1.0, 0.0).astype(BF16)
        bid += lax.dot_general(
            place_x, place_y, (((1,), (1,)), ((), ())), preferred_element_type=F32
        )
    bids[...] = bid[0:8].astype(jnp.int32)

    blank = jnp.zeros((2, 128), F32)
    for b in range(buildings):
        piece = pl.ds(b * 128, 128)
        disp[b] = jnp.concatenate([frame_disp[:, piece], blank], 0)
        vel[b] = jnp.concatenate([frame_vel[:, piece], blank], 0)
        imass[b] = TIME_FRAME * jnp.concatenate([inverse_mass[:, piece], blank], 0)
        foot_sum[b] = jnp.zeros((8, 128), F32)

    load_matrix.wait()

    def internal_forces(b):
        place = disp[b]
        forces = []
        for h in range(2):
            ends = (
                lane_gather(place, index[b, h * 2]),
                lane_gather(place, index[b, h * 2 + 1]),
            )
            piece = pl.ds(b * 256 + h * 128, 128)
            total = None
            for a in range(12):
                row = ends[a // 6][a % 6 : a % 6 + 1, :]
                term = matrix[a, :, piece] * row
                total = term if total is None else total + term
            forces.append(jnp.concatenate([total, jnp.zeros((4, 128), F32)], 0))
        forces = jnp.concatenate(forces, 1)
        high = forces.astype(BF16)
        low = (forces - high.astype(F32)).astype(BF16)
        parts = jnp.dot(
            jnp.concatenate([high, low], 0), spread[b], preferred_element_type=F32
        )
        parts = parts[0:16] + parts[16:32]
        internal[b] = parts[0:8, 0:128] + parts[6:14, 128:256]

    def advance(b):
        speed = vel[b]
        loads = damp_vec[0, b] - damp_vec[1, b] * speed - internal[b]
        speed = speed + imass[b] * loads
        vel[b] = speed
        disp[b] = disp[b] + TIME_FRAME * speed
        foot_sum[b] += speed

    for b in range(buildings):
        internal_forces(b)

    finish(sent)
    outside_zero_x(vel_a, (0, 1, 2), 1, 2)
    prepare(1, True)

    stress_layers(1, vel_a, first, SXX, str_a, COL, ROW, 0, 3, True)
    sent = send_x(2, str_a, COL, str_a, inner_groups, 2, 1)
    stress_layers(1, vel_a, first, SXX, str_a, COL, ROW, 3, cells_x, True)
    sent += send_y(2)
    finish(sent)
    outside_zero_x(str_a, (0, 3, 4), 2, 1)
    prepare(2, False)

    velocity_layers(2, str_a, 0, vel_a, vel_b, 0, 3, moved_out)
    sent_x = send_x(3, vel_b, COL, vel_b, move_groups, 1, 2)
    velocity_layers(2, str_a, 0, vel_a, vel_b, 3, cells_x, moved_out)
    sent_y = send_y(3)

    surface = [vel_b[k, inner, ROW, :] for k in range(3)]
    dash = dashpot[...]
    terms = [dash * surface[0], dash * surface[1], dash * surface[2], dash]
    bid = bids[...]
    sums = [
        jnp.sum(jnp.where(bid == b, term, 0.0), axis=0, keepdims=True)
        for term in terms
        for b in range(buildings)
    ]
    sums = jnp.concatenate(sums + [jnp.zeros((128 - len(sums), 128), F32)], 0)
    mine = jnp.sum(sums.T, axis=0, keepdims=True)

    def gather_along_gy(turn, value):
        row_buf[turn, gy] = value
        return [
            remote(
                row_buf.at[turn, gy],
                row_buf.at[turn, gy],
                a_send.at[turn, k - 1],
                a_recv.at[turn, k - 1],
                {"gy": lax.rem(gy + k, n_gy)},
            )
            for k in range(1, n_gy)
        ]

    def gather_along_gx(turn):
        rows_all[turn, gx] = row_buf[turn].reshape(n_gy, 128)
        return [
            remote(
                rows_all.at[turn, gx],
                rows_all.at[turn, gx],
                b_send.at[turn, k - 1],
                b_recv.at[turn, k - 1],
                {"gx": lax.rem(gx + k, n_gx)},
            )
            for k in range(1, n_gx)
        ]

    gathering = gather_along_gy(0, mine)

    finish(sent_y)
    prepare(3, True)
    stress_layers(3, vel_b, str_a, 0, str_b, 0, 0, 3, cells_x, False)
    finish(gathering)
    gathering = gather_along_gx(0)
    finish(sent_x)
    outside_zero_x(vel_b, (0, 1, 2), 1, 2)
    stress_layers(3, vel_b, str_a, 0, str_b, 0, 0, 0, 3, False)
    finish(gathering)
    arrived = rows_all[0].reshape(n_dev, 128)
    owned = jnp.sum(jnp.where(owners[...] == me, arrived, 0.0), axis=0, keepdims=True)
    owned = jnp.broadcast_to(owned, (8, 128))

    at_footing = (small_row < 3) & (small_lane == 0)
    drives, dampers = [], []
    for b in range(buildings):
        pick = jnp.minimum(small_row * buildings + b, 127)
        drives.append(jnp.where(at_footing, lane_gather(owned, pick), 0.0))
        pick = jnp.full((8, 128), 3 * buildings + b, jnp.int32)
        dampers.append(jnp.where(at_footing, lane_gather(owned, pick), 0.0))
    for b in range(buildings):
        damp_vec[0, b] = drives[b]
        damp_vec[1, b] = dampers[b]

    def frame_step(step, carry):
        for b in range(buildings):
            advance(b)
            internal_forces(b)
        return carry

    lax.fori_loop(0, FRAME_STEPS - 1, frame_step, 0)
    for b in range(buildings):
        advance(b)

    back = jnp.zeros((8, 128), F32)
    for b in range(buildings):
        whole = jnp.broadcast_to(foot_sum[b][:, 0:1], (8, 128))
        back = jnp.where(small_lane == small_row * buildings + b, whole, back)
    back = jnp.where(small_row < 3, back, 0.0)
    gathering = gather_along_gy(1, jnp.sum(back, axis=0, keepdims=True))
    for b in range(buildings):
        piece = pl.ds(b * 128, 128)
        disp_out[:, piece] = disp[b][0:6]
        vel_out[:, piece] = vel[b][0:6]
    wanted = owners[pl.ds(me, 1), :]
    finish(gathering)
    gathering = gather_along_gx(1)
    finish(gathering)
    arrived = rows_all[1].reshape(n_dev, 128)
    held = jnp.where(iota((n_dev, 128), 0) == wanted, arrived, 0.0)
    held = jnp.broadcast_to(jnp.sum(held, axis=0, keepdims=True), (8, 128))
    for k in range(3):
        total = lane_gather(held, bid + k * buildings)
        force_out[k] = dash * (FRAME_STEPS * surface[k] - total)

    for copy in leaving:
        copy.wait_send()


def write_out(moved, stress, force, disp, vel, soil_out, force_out, disp_out, vel_out, sem):
    copies = [
        pltpu.make_async_copy(source, target, sem.at[k])
        for k, (source, target) in enumerate(
            (
                (stress, soil_out.at[pl.ds(3, 6)]),
                (moved, soil_out.at[pl.ds(0, 3)]),
                (force, force_out),
                (disp, disp_out),
                (vel, vel_out),
            )
        )
    ]
    for copy in copies:
        copy.start()
    for copy in copies:
        copy.wait()


def shards(n_gx, n_gy, *args):
    soil, material, dashpot, foot, table, stiff, links = args[:7]
    cells_x, cells_z, cells_y = soil.shape[1:]
    buildings = foot.shape[0]
    wide = (cells_x + 2 * COL, cells_z + 2 * ROW, cells_y)
    n_dev = n_gx * n_gy
    anywhere = pl.BlockSpec(memory_space=pl.ANY)
    vmem = pl.BlockSpec(memory_space=pltpu.VMEM)
    dma = pltpu.SemaphoreType.DMA
    limit = 40 * 1024 * 1024
    kept = (
        pltpu.VMEM((3, cells_x, cells_z, cells_y), F32),
        pltpu.VMEM((6, cells_x, cells_z, cells_y), F32),
        pltpu.VMEM((3, cells_x, cells_y), F32),
        pltpu.VMEM(args[9].shape, F32),
        pltpu.VMEM(args[10].shape, F32),
    )
    results = pl.pallas_call(
        functools.partial(kernel, n_gx, n_gy),
        out_shape=kept,
        in_specs=[pl.BlockSpec(memory_space=pltpu.HBM)] * len(args),
        out_specs=(vmem,) * len(kept),
        scratch_shapes=[
            pltpu.VMEM((9,) + wide, F32),
            pltpu.VMEM((3,) + wide, F32),
            pltpu.VMEM((6,) + wide, F32),
            pltpu.VMEM((3,) + wide, F32),
            pltpu.VMEM(material.shape, BF16),
            pltpu.VMEM(material.shape, F32),
            pltpu.VMEM(stiff.shape, F32),
            pltpu.VMEM(dashpot.shape, F32),
            pltpu.VMEM(foot.shape, jnp.int32),
            pltpu.VMEM(table.shape, jnp.int32),
            pltpu.VMEM(links.shape, jnp.int32),
            pltpu.SMEM(args[7].shape, jnp.int32),
            pltpu.VMEM(args[8].shape, F32),
            pltpu.VMEM(args[9].shape, F32),
            pltpu.VMEM(args[10].shape, F32),
            pltpu.VMEM((buildings, 256, 256), BF16),
            pltpu.VMEM((2, 256, 256), BF16),
            pltpu.VMEM((4, 3, cells_x // 4, 8, 128), F32),
            pltpu.VMEM((4, 3, cells_x // 4, 8, 128), F32),
            pltpu.VMEM((4, 3, cells_x // 4, 8, 128), F32),
            pltpu.VMEM((4, 3, cells_x // 4, 8, 128), F32),
            pltpu.VMEM((n_dev, 128), jnp.int32),
            pltpu.VMEM((8, 128), jnp.int32),
            pltpu.VMEM((2, buildings, 8, 128), F32),
            pltpu.VMEM((buildings, 8, 128), F32),
            pltpu.VMEM((buildings, 8, 128), F32),
            pltpu.VMEM((buildings, 8, 128), F32),
            pltpu.VMEM((buildings, 8, 128), F32),
            pltpu.VMEM((buildings, 8, 128), F32),
            pltpu.VMEM((buildings, 4, 8, 128), jnp.int32),
            pltpu.VMEM((2, n_gy, 1, 128), F32),
            pltpu.VMEM((2, n_gx, n_gy, 128), F32),
            dma((12,)),
            dma((4, 2, 2)),
            dma((4, 2, 2)),
            dma((4, 2)),
            dma((4, 2)),
            dma((2, n_gy - 1)),
            dma((2, n_gy - 1)),
            dma((2, n_gx - 1)),
            dma((2, n_gx - 1)),
        ],
        compiler_params=pltpu.CompilerParams(
            collective_id=0, has_side_effects=True, vmem_limit_bytes=limit
        ),
    )(*(pltpu.with_memory_space_constraint(value, pltpu.HBM) for value in args))
    return pl.pallas_call(
        write_out,
        out_shape=(
            jax.ShapeDtypeStruct(soil.shape, F32),
            jax.ShapeDtypeStruct((3, cells_x, cells_y), F32),
            jax.ShapeDtypeStruct(args[9].shape, F32),
            jax.ShapeDtypeStruct(args[10].shape, F32),
        ),
        in_specs=[vmem] * len(kept),
        out_specs=(anywhere,) * 4,
        scratch_shapes=[dma((len(kept),))],
        compiler_params=pltpu.CompilerParams(vmem_limit_bytes=limit),
    )(*results)


def solution(mesh):
    placed = (
        P(None, "gx", None, "gy"),
        P(None, "gx", None, "gy"),
        P("gx", "gy"),
        P(("gx", "gy"), None),
        P(),
        P(None, None, ("gx", "gy")),
        P(None, ("gx", "gy")),
        P(("gx", "gy")),
        P(None, ("gx", "gy")),
        P(None, ("gx", "gy")),
        P(None, ("gx", "gy")),
    )
    return jax.shard_map(
        functools.partial(shards, mesh.shape["gx"], mesh.shape["gy"]),
        mesh=mesh,
        in_specs=placed,
        out_specs=(
            P(None, "gx", None, "gy"),
            P(None, "gx", "gy"),
            P(None, ("gx", "gy")),
            P(None, ("gx", "gy")),
        ),
        check_vma=False,
    )
```

```python
import functools

import jax
import jax.numpy as jnp
from jax import lax
from jax.experimental import pallas as pl
from jax.experimental.pallas import tpu as pltpu
from jax.sharding import PartitionSpec as P

GROUPS = 4
FRAME_STEPS = 4
NEAR = 9.0 / 8.0
FAR = -1.0 / 24.0
TIME_SOIL = 0.18
TIME_FRAME = 0.05
MESH = pl.DeviceIdType.MESH
ROW = 8
COL = 2
LOW, HIGH = 5, 4
F32 = jnp.float32
BF16 = jnp.bfloat16

VX, VY, VZ, SXX, SYY, SZZ, SXY, SXZ, SYZ = range(9)


def lane_gather(values, index):
    return lax.gather(
        values,
        index[:, :, None],
        lax.GatherDimensionNumbers(
            offset_dims=(),
            collapsed_slice_dims=(1,),
            start_index_map=(1,),
            operand_batching_dims=(0,),
            start_indices_batching_dims=(0,),
        ),
        (1, 1),
        mode=lax.GatherScatterMode.PROMISE_IN_BOUNDS,
    )


def iota(shape, dim):
    return lax.broadcasted_iota(jnp.int32, shape, dim)


def stencil(near_high, near_low, far_high, far_low):
    return NEAR * (near_high - near_low) + FAR * (far_high - far_low)


def rolled(value, shift):
    return pltpu.roll(value, shift, 1)


def kernel(
    n_gx,
    n_gy,
    soil,
    material,
    hbm_dashpot,
    hbm_foot,
    hbm_table,
    stiff,
    hbm_links,
    hbm_count,
    hbm_inverse_mass,
    hbm_frame_disp,
    hbm_frame_vel,
    moved_out,
    str_b,
    force_out,
    disp_out,
    vel_out,
    first,
    vel_a,
    str_a,
    vel_b,
    raw,
    coef,
    matrix,
    dashpot,
    foot,
    table,
    links,
    count,
    inverse_mass,
    frame_disp,
    frame_vel,
    spread,
    band,
    edges,
    from_low,
    from_high,
    correction,
    top,
    rims,
    rims_in,
    owners,
    bids,
    damp_vec,
    disp,
    vel,
    imass,
    foot_sum,
    internal,
    index,
    row_buf,
    rows_all,
    load_sem,
    x_send,
    x_recv,
    y_send,
    y_recv,
    a_send,
    a_recv,
    b_send,
    b_recv,
    t_send,
    t_recv,
):
    gx = lax.axis_index("gx")
    gy = lax.axis_index("gy")
    me = gx * n_gy + gy
    n_dev = n_gx * n_gy
    gx_up, gx_down = lax.rem(gx + 1, n_gx), lax.rem(gx + n_gx - 1, n_gx)
    gy_up, gy_down = lax.rem(gy + 1, n_gy), lax.rem(gy + n_gy - 1, n_gy)
    cells_x, cells_z, cells_y = soil.shape[1:]
    tiles_z = cells_z // 8
    buildings = foot.shape[0]
    inner = pl.ds(COL, cells_x)
    rows = pl.ds(ROW, cells_z)

    def load(k, source, target):
        copy = pltpu.make_async_copy(source, target, load_sem.at[k])
        copy.start()
        return copy

    load_stress = load(0, soil.at[pl.ds(SXX, 6)], first.at[pl.ds(SXX, 6), inner, rows])
    load_velocity = load(1, soil.at[pl.ds(0, 3)], first.at[pl.ds(0, 3), inner, rows])
    load_material = load(2, material, raw)
    load_small = [
        load(4 + k, source, target)
        for k, (source, target) in enumerate(
            (
                (hbm_dashpot, dashpot),
                (hbm_foot, foot),
                (hbm_table, table),
                (hbm_links, links),
                (hbm_count, count),
                (hbm_inverse_mass, inverse_mass),
                (hbm_frame_disp, frame_disp),
                (hbm_frame_vel, frame_vel),
            )
        )
    ]
    load_matrix = load(3, stiff, matrix)

    barrier = pltpu.get_barrier_semaphore()
    for k in range(1, n_gx):
        pl.semaphore_signal(
            barrier, inc=1, device_id={"gx": lax.rem(gx + k, n_gx)}, device_id_type=MESH
        )
    for k in range(1, n_gy):
        pl.semaphore_signal(
            barrier, inc=1, device_id={"gy": lax.rem(gy + k, n_gy)}, device_id_type=MESH
        )

    corners = [
        {"gx": row, "gy": column} for row in (gx_down, gx_up) for column in (gy_down, gy_up)
    ]
    for device in corners:
        pl.semaphore_signal(barrier, inc=1, device_id=device, device_id_type=MESH)

    zero_tile = jnp.zeros((8, cells_y), F32)

    def clear(x, carry):
        for ref, members in (
            (first, (SZZ, SXZ, SYZ)),
            (vel_a, (0, 1, 2)),
            (str_a, (2, 4, 5)),
            (vel_b, (0, 1, 2)),
        ):
            for member in members:
                ref[member, x, pl.ds(0, 8), :] = zero_tile
                ref[member, x, pl.ds(ROW + cells_z, 8), :] = zero_tile
        return carry

    lax.fori_loop(COL, COL + cells_x, clear, 0)

    def clear_top(x, carry):
        for member in (VX, VY, VZ, SZZ, SXZ, SYZ):
            for part in range(2):
                top[member, x, part, pl.ds(0, 8), :] = zero_tile
        return carry

    lax.fori_loop(0, top.shape[1], clear_top, 0)

    def remote(source, target, send, recv, device):
        copy = pltpu.make_async_remote_copy(
            src_ref=source,
            dst_ref=target,
            send_sem=send,
            recv_sem=recv,
            device_id=device,
            device_id_type=MESH,
        )
        copy.start()
        return copy

    def send_x(stage, source, start, target, groups, up, down):
        copies = []
        for k, (origin, member, size) in enumerate(groups):
            ids, into = pl.ds(origin, size), pl.ds(member, size)
            copies.append(
                remote(
                    source.at[ids, pl.ds(start + cells_x - up, up), rows if start else pl.ds(0, cells_z)],
                    target.at[into, pl.ds(COL - up, up), rows],
                    x_send.at[stage, k, 0],
                    x_recv.at[stage, k, 0],
                    {"gx": gx_up},
                )
            )
            copies.append(
                remote(
                    source.at[ids, pl.ds(start, down), rows if start else pl.ds(0, cells_z)],
                    target.at[into, pl.ds(COL + cells_x, down), rows],
                    x_send.at[stage, k, 1],
                    x_recv.at[stage, k, 1],
                    {"gx": gx_down},
                )
            )
        return copies

    def send_y(stage):
        return [
            remote(
                edges.at[stage],
                from_low.at[stage],
                y_send.at[stage, 0],
                y_recv.at[stage, 0],
                {"gy": gy_up},
            ),
            remote(
                edges.at[stage],
                from_high.at[stage],
                y_send.at[stage, 1],
                y_recv.at[stage, 1],
                {"gy": gy_down},
            ),
        ]

    leaving = []

    def finish(copies):
        for copy in copies:
            copy.wait_recv()
        leaving.extend(copies)

    def outside_zero_x(ref, members, low, high):
        @pl.when(gx == 0)
        def _():
            for member in members:
                for layer in range(low):
                    ref[member, COL - 1 - layer, rows, :] = jnp.zeros((cells_z, cells_y), F32)

        @pl.when(gx == n_gx - 1)
        def _():
            for member in members:
                for layer in range(high):
                    ref[member, COL + cells_x + layer, rows, :] = jnp.zeros((cells_z, cells_y), F32)

    lane = iota((8, cells_y), 1)
    slot = lane & 3

    def pack(stage, values, cell):
        group = cell // 4
        for k in range(3):
            packed = edges[stage, k, group]
            for z in range(tiles_z):
                place = (cell & 3) * tiles_z + z
                packed = jnp.where(
                    lane >> 2 == place, rolled(values[z][k], (4 * place + 2) & 127), packed
                )
            edges[stage, k, group] = packed

    def prepare(stage, forward):
        for k in range(3):
            for group in range(edges.shape[2]):
                low = jnp.where(gy > 0, from_low[stage, k, group], 0.0)
                high = jnp.where(gy < n_gy - 1, from_high[stage, k, group], 0.0)
                beyond = jnp.where(slot < 2, low, high)
                back_2, back_1 = rolled(beyond, 126), rolled(beyond, 127)
                on_1, on_2 = rolled(beyond, 1), rolled(beyond, 2)
                if forward:
                    value = jnp.where(
                        slot == 0,
                        FAR * back_2,
                        jnp.where(
                            slot == 1,
                            NEAR * back_1 + FAR * back_2,
                            jnp.where(slot == 2, -FAR * on_1, 0.0),
                        ),
                    )
                else:
                    value = jnp.where(
                        slot == 1,
                        FAR * back_1,
                        jnp.where(
                            slot == 2,
                            -NEAR * on_1 - FAR * on_2,
                            jnp.where(slot == 3, -FAR * on_2, 0.0),
                        ),
                    )
                correction[stage, k, group] = value

    at_edge = (lane < 2) | (lane >= cells_y - 2)

    def along_y(ref, members, stage, cell, forward):
        parts = []
        for member in members:
            value = ref[member, cell + COL, rows, :]
            high = value.astype(BF16)
            low = (value - high.astype(F32)).astype(BF16)
            parts.append(jnp.concatenate([high, low], 1))
        both = jnp.dot(
            jnp.concatenate(parts, 0), band[int(forward)], preferred_element_type=F32
        )
        group = cell // 4
        result = []
        for z in range(tiles_z):
            shift = (254 - 4 * ((cell & 3) * tiles_z + z)) & 127
            line = []
            for k in range(3):
                tile = slice(k * cells_z + 8 * z, k * cells_z + 8 * z + 8)
                inside = NEAR * both[tile, 0:128] + FAR * both[tile, 128:256]
                line.append(
                    inside + jnp.where(at_edge, rolled(correction[stage, k, group], shift), 0.0)
                )
            result.append(line)
        return result

    def at(ref, member, x, row):
        return ref[member, x, pl.ds(row, 8), :]

    def along_x(ref, member, x, row, forward):
        shift = 1 if forward else 0
        return stencil(
            at(ref, member, x + shift, row),
            at(ref, member, x + shift - 1, row),
            at(ref, member, x + shift + 1, row),
            at(ref, member, x + shift - 2, row),
        )

    def along_z(ref, member, x, row, forward):
        shift = 1 if forward else 0
        return stencil(
            at(ref, member, x, row + shift),
            at(ref, member, x, row + shift - 1),
            at(ref, member, x, row + shift + 1),
            at(ref, member, x, row + shift - 2),
        )

    def velocity_layers(stage, stress, base, old, new, begin, end, out=None):
        sxx, syy, szz, sxy, sxz, syz = range(base, base + 6)

        def layer(i, carry):
            cell = (i + cells_x - 1) & (cells_x - 1)
            x = cell + COL
            y_all = along_y(stress, (sxy, syy, syz), stage, cell, False)
            results = []
            for z in range(tiles_z):
                row = ROW + 8 * z
                y_of = y_all[z]
                accel = (
                    along_x(stress, sxx, x, row, False) + y_of[0] + along_z(stress, sxz, x, row, False),
                    along_x(stress, sxy, x, row, False) + y_of[1] + along_z(stress, syz, x, row, False),
                    along_x(stress, sxz, x, row, False) + y_of[2] + along_z(stress, szz, x, row, False),
                )
                density = coef[0, cell, pl.ds(8 * z, 8), :]
                after = [at(old, k, x, row) + density * accel[k] for k in range(3)]
                for k in range(3):
                    new[k, x, pl.ds(row, 8), :] = after[k]
                    if out is not None:
                        out[k, cell, pl.ds(8 * z, 8), :] = after[k]
                results.append(after)
            pack(stage + 1, results, cell)
            return carry

        lax.fori_loop(begin, end, layer, 0)

    def stress_layers(stage, moving, stress, base, new, new_x, new_row, begin, end, packing):
        def layer(i, carry):
            cell = (i + cells_x - 2) & (cells_x - 1)
            x = cell + COL
            y_all = along_y(moving, (0, 1, 2), stage, cell, True)
            results = []
            for z in range(tiles_z):
                row = ROW + 8 * z
                y_of = y_all[z]
                x_of = [along_x(moving, k, x, row, True) for k in range(3)]
                z_of = [along_z(moving, k, x, row, True) for k in range(3)]
                lame = coef[1, cell, pl.ds(8 * z, 8), :]
                shear = coef[2, cell, pl.ds(8 * z, 8), :]
                volume = lame * (x_of[0] + y_of[1] + z_of[2])
                twice = shear + shear
                change = (
                    volume + twice * x_of[0],
                    volume + twice * y_of[1],
                    volume + twice * z_of[2],
                    shear * (y_of[0] + x_of[1]),
                    shear * (z_of[0] + x_of[2]),
                    shear * (z_of[1] + y_of[2]),
                )
                after = [at(stress, base + k, x, row) + change[k] for k in range(6)]
                for k in range(6):
                    new[k, cell + new_x, pl.ds(new_row + 8 * z, 8), :] = after[k]
                results.append((after[3], after[1], after[5]))
            if packing:
                pack(stage + 1, results, cell)
            return carry

        lax.fori_loop(begin, end, layer, 0)

    stress_groups = ((SXX, SXX, 1), (SXY, SXY, 2))
    inner_groups = ((0, 0, 1), (3, 3, 2))
    move_groups = ((0, 0, 3),)

    fields = rims.shape[0]
    wide_lane = lane

    def pack_rims(cell, carry):
        for member in range(fields):
            if member < 9:
                value = at(first, member, cell + COL, ROW)
            else:
                value = coef[member - 9, cell, pl.ds(0, 8), :]
            top[member, cell + LOW, 0, pl.ds(8, 8), :] = value
            rims[member] = jnp.where(
                wide_lane >> 4 == cell, rolled(value, (16 * cell + LOW) & 127), rims[member]
            )
        return carry

    def send_top():
        copies = []
        top_rows = pl.ds(8, 8)
        flow = (
            (first, VX, 3, VX, 3, 3, ROW, COL),
            (first, SXX, 6, SXX, LOW, HIGH, ROW, COL),
            (coef, 0, 3, 9, 3, 3, 0, 0),
        )
        for k, (source, origin, size, member, up, down, row, layer) in enumerate(flow):
            copies.append(
                remote(
                    source.at[pl.ds(origin, size), pl.ds(layer + cells_x - up, up), pl.ds(row, 8)],
                    top.at[pl.ds(member, size), pl.ds(LOW - up, up), 0, top_rows],
                    t_send.at[k],
                    t_recv.at[k],
                    {"gx": gx_up},
                )
            )
            copies.append(
                remote(
                    source.at[pl.ds(origin, size), pl.ds(layer, down), pl.ds(row, 8)],
                    top.at[pl.ds(member, size), pl.ds(LOW + cells_x, down), 0, top_rows],
                    t_send.at[3 + k],
                    t_recv.at[3 + k],
                    {"gx": gx_down},
                )
            )
        for k, (device, row, column, size) in enumerate(
            (
                ({"gx": gx_up, "gy": gy_up}, 0, 0, fields - 2),
                ({"gx": gx_up, "gy": gy_down}, 0, 1, fields - 2),
                ({"gx": gx_down, "gy": gy_up}, 2, 0, fields - 2),
                ({"gx": gx_down, "gy": gy_down}, 2, 1, fields - 2),
                ({"gy": gy_up}, 1, 0, fields),
                ({"gy": gy_down}, 1, 1, fields),
            )
        ):
            copies.append(
                remote(
                    rims.at[pl.ds(0, size)],
                    rims_in.at[row, column, pl.ds(0, size)],
                    t_send.at[6 + k],
                    t_recv.at[6 + k],
                    device,
                )
            )
        return copies

    def unpack_rims():
        spot = wide_lane & 15

        def fill(row, member, shown, x, cell):
            low = jnp.where(shown & (gy > 0), rims_in[row, 0, member], 0.0)
            high = jnp.where(shown & (gy < n_gy - 1), rims_in[row, 1, member], 0.0)
            both = jnp.where(spot < LOW, low, high)
            both = rolled(both, (256 - LOW - 16 * cell) & 127)
            near = (wide_lane < HIGH) | (wide_lane >= 128 - LOW)
            top[member, x, 1, pl.ds(8, 8), :] = jnp.where(near, both, 0.0)

        def layer_inside(cell, carry):
            for member in range(fields):
                fill(1, member, True, cell + LOW, cell)
            return carry

        lax.fori_loop(0, cells_x, layer_inside, 0)

        def layer_low(x, carry):
            for member in range(fields - 2):
                fill(0, member, gx > 0, x, x + cells_x - LOW)
            for member in range(fields - 2, fields):
                top[member, x, 1, pl.ds(8, 8), :] = zero_tile
            return carry

        lax.fori_loop(0, LOW, layer_low, 0)

        def layer_high(cell, carry):
            for member in range(fields - 2):
                fill(2, member, gx < n_gx - 1, cell + LOW + cells_x, cell)
            for member in range(fields - 2, fields):
                top[member, cell + LOW + cells_x, 1, pl.ds(8, 8), :] = zero_tile
            return carry

        lax.fori_loop(0, HIGH, layer_high, 0)

        def outside(x, carry):
            for member in range(fields):
                top[member, x, 0, pl.ds(8, 8), :] = zero_tile
            return carry

        @pl.when(gx == 0)
        def _():
            lax.fori_loop(0, LOW, outside, 0)

        @pl.when(gx == n_gx - 1)
        def _():
            lax.fori_loop(LOW + cells_x, LOW + cells_x + HIGH, outside, 0)

    def top_at(member, x, part, row=8):
        return top[member, x, part, pl.ds(row, 8), :]

    def top_along_y(member, x, forward):
        parts = [top_at(member, x, 0), top_at(member, x, 1)]

        def moved(shift):
            mine, other = [rolled(part, shift & 127) for part in parts]
            across = wide_lane < shift if shift > 0 else wide_lane >= 128 + shift
            return jnp.where(across, other, mine), jnp.where(across, mine, other)

        if forward:
            terms = (moved(-1), parts, moved(-2), moved(1))
        else:
            terms = (parts, moved(1), moved(-1), moved(2))
        return [stencil(*(term[part] for term in terms)) for part in range(2)]

    def top_along_x(member, x, part, shift):
        return stencil(
            top_at(member, x + shift, part),
            top_at(member, x + shift - 1, part),
            top_at(member, x + shift + 1, part),
            top_at(member, x + shift - 2, part),
        )

    def top_along_z(member, x, part, shift):
        return stencil(
            top_at(member, x, part, 8 + shift),
            top_at(member, x, part, 7 + shift),
            top_at(member, x, part, 9 + shift),
            top_at(member, x, part, 6 + shift),
        )

    def top_velocity(x, parts):
        y_of = [top_along_y(member, x, False) for member in (SXY, SYY, SYZ)]
        for part in range(parts):
            accel = (
                top_along_x(SXX, x, part, 0) + y_of[0][part] + top_along_z(SXZ, x, part, 0),
                top_along_x(SXY, x, part, 0) + y_of[1][part] + top_along_z(SYZ, x, part, 0),
                top_along_x(SXZ, x, part, 0) + y_of[2][part] + top_along_z(SZZ, x, part, 0),
            )
            for k in range(3):
                top[k, x, part, pl.ds(8, 8), :] = (
                    top_at(k, x, part) + top_at(9, x, part) * accel[k]
                )

    def top_stress(x):
        y_of = [top_along_y(member, x, True) for member in range(3)]
        for part in range(2):
            x_of = [top_along_x(member, x, part, 1) for member in range(3)]
            z_of = [top_along_z(member, x, part, 1) for member in range(3)]
            shear = top_at(11, x, part)
            volume = top_at(10, x, part) * (x_of[0] + y_of[1][part] + z_of[2])
            twice = shear + shear
            change = (
                volume + twice * x_of[0],
                volume + twice * y_of[1][part],
                volume + twice * z_of[2],
                shear * (y_of[0][part] + x_of[1]),
                shear * (z_of[0] + x_of[2]),
                shear * (z_of[1] + y_of[2][part]),
            )
            for k in range(6):
                top[SXX + k, x, part, pl.ds(8, 8), :] = top_at(SXX + k, x, part) + change[k]

    def top_layers(update, begin, end, *more):
        def layer(x, carry):
            update(x, *more)
            return carry

        lax.fori_loop(begin, end, layer, 0)

    load_stress.wait()

    edges[...] = jnp.zeros(edges.shape, F32)

    def pack_first(cell, carry):
        values = [
            [at(first, k, cell + COL, ROW + 8 * z) for k in (SXY, SYY, SYZ)] for z in range(tiles_z)
        ]
        pack(0, values, cell)
        return carry

    lax.fori_loop(0, cells_x, pack_first, 0)

    load_material.wait()

    def widen(cell, carry):
        for k in range(3):
            coef[k, cell] = TIME_SOIL * raw[k, cell].astype(F32)
        return carry

    lax.fori_loop(0, cells_x, widen, 0)
    load_velocity.wait()
    rims[...] = jnp.zeros(rims.shape, F32)
    lax.fori_loop(0, cells_x, pack_rims, 0)
    pl.semaphore_wait(barrier, n_gx + n_gy + 2)
    sent_top = send_top()
    sent = send_x(0, soil, 0, first, stress_groups, 2, 1)
    sent += send_y(0)

    source = iota((256, 256), 0) & 127
    column = iota((256, 256), 1)
    wanted = column & 127
    for forward in range(2):
        reach = jnp.where(column < 128, 0, 1)
        plus = source == wanted + forward + reach
        minus = source == wanted + forward - 1 - reach
        band[forward] = jnp.where(plus, 1.0, jnp.where(minus, -1.0, 0.0)).astype(BF16)


    for copy in load_small:
        copy.wait()
    big = (128, 128)
    big_lane = iota(big, 1)
    big_lane_f = big_lane.astype(F32)
    small_row = iota((8, 128), 0)
    small_lane = iota((8, 128), 1)

    for b in range(buildings):
        for h in range(2):
            piece = pl.ds(b * 256 + h * 128, 128)
            live = iota((1, 128), 1) + h * 128 < count[b]
            for end in range(2):
                nodes = links[pl.ds(end, 1), piece]
                index[b, h * 2 + end] = jnp.broadcast_to(nodes, (8, 128))
                kept = jnp.where(live, nodes, -1).astype(F32)
                columns = jnp.broadcast_to(kept, big).T
                spread[b, pl.ds(h * 128, 128), pl.ds(end * 128, 128)] = (
                    jnp.where(columns == big_lane_f, 1.0, 0.0).astype(BF16)
                )

    group_of = (iota((n_dev, 128), 1) // 2) % GROUPS
    holder = iota((n_dev, 128), 0)
    for j in range(1, GROUPS):
        entries = table[pl.ds(j - 1, 1), :].astype(F32)
        columns = jnp.broadcast_to(entries, (128, n_dev)).T.astype(jnp.int32)
        holder = jnp.where(group_of == j, columns, holder)
    owners[...] = holder

    bid = jnp.zeros((16, 128), F32)
    for b in range(buildings):
        cell = foot[pl.ds(b, 1), :]
        place_x = jnp.where(iota((16, 128), 0) == cell // cells_y, float(b), 0.0).astype(BF16)
        place_y = jnp.where(iota(big, 0) == cell % cells_y, 1.0, 0.0).astype(BF16)
        bid += lax.dot_general(
            place_x, place_y, (((1,), (1,)), ((), ())), preferred_element_type=F32
        )
    bids[...] = bid[0:8].astype(jnp.int32)

    blank = jnp.zeros((2, 128), F32)
    for b in range(buildings):
        piece = pl.ds(b * 128, 128)
        disp[b] = jnp.concatenate([frame_disp[:, piece], blank], 0)
        vel[b] = jnp.concatenate([frame_vel[:, piece], blank], 0)
        imass[b] = TIME_FRAME * jnp.concatenate([inverse_mass[:, piece], blank], 0)
        foot_sum[b] = jnp.zeros((8, 128), F32)

    load_matrix.wait()

    def internal_forces(b):
        place = disp[b]
        forces = []
        for h in range(2):
            ends = (
                lane_gather(place, index[b, h * 2]),
                lane_gather(place, index[b, h * 2 + 1]),
            )
            piece = pl.ds(b * 256 + h * 128, 128)
            total = None
            for a in range(12):
                row = ends[a // 6][a % 6 : a % 6 + 1, :]
                term = matrix[a, :, piece] * row
                total = term if total is None else total + term
            forces.append(jnp.concatenate([total, jnp.zeros((4, 128), F32)], 0))
        forces = jnp.concatenate(forces, 1)
        high = forces.astype(BF16)
        low = (forces - high.astype(F32)).astype(BF16)
        parts = jnp.dot(
            jnp.concatenate([high, low], 0), spread[b], preferred_element_type=F32
        )
        parts = parts[0:16] + parts[16:32]
        internal[b] = parts[0:8, 0:128] + parts[6:14, 128:256]

    def advance(b):
        speed = vel[b]
        loads = damp_vec[0, b] - damp_vec[1, b] * speed - internal[b]
        speed = speed + imass[b] * loads
        vel[b] = speed
        disp[b] = disp[b] + TIME_FRAME * speed
        foot_sum[b] += speed

    for b in range(buildings):
        internal_forces(b)

    finish(sent_top)
    unpack_rims()
    top_layers(top_velocity, LOW - 3, LOW + cells_x + 3, 2)
    top_layers(top_stress, LOW - 2, LOW + cells_x + 1)
    top_layers(top_velocity, LOW, LOW + cells_x, 1)

    surface = [top[k, pl.ds(LOW, cells_x), 0, 8, :] for k in range(3)]
    dash = dashpot[...]
    terms = [dash * surface[0], dash * surface[1], dash * surface[2], dash]
    bid = bids[...]
    sums = [
        jnp.sum(jnp.where(bid == b, term, 0.0), axis=0, keepdims=True)
        for term in terms
        for b in range(buildings)
    ]
    sums = jnp.concatenate(sums + [jnp.zeros((128 - len(sums), 128), F32)], 0)
    mine = jnp.sum(sums.T, axis=0, keepdims=True)

    def gather_along_gy(turn, value):
        row_buf[turn, gy] = value
        return [
            remote(
                row_buf.at[turn, gy],
                row_buf.at[turn, gy],
                a_send.at[turn, k - 1],
                a_recv.at[turn, k - 1],
                {"gy": lax.rem(gy + k, n_gy)},
            )
            for k in range(1, n_gy)
        ]

    def gather_along_gx(turn):
        rows_all[turn, gx] = row_buf[turn].reshape(n_gy, 128)
        return [
            remote(
                rows_all.at[turn, gx],
                rows_all.at[turn, gx],
                b_send.at[turn, k - 1],
                b_recv.at[turn, k - 1],
                {"gx": lax.rem(gx + k, n_gx)},
            )
            for k in range(1, n_gx)
        ]

    gathering = gather_along_gy(0, mine)

    finish(sent)
    outside_zero_x(first, (SXX, SXY, SXZ), 2, 1)
    prepare(0, False)

    velocity_layers(0, first, SXX, first, vel_a, 0, 3)
    sent = send_x(1, vel_a, COL, vel_a, move_groups, 1, 2)
    velocity_layers(0, first, SXX, first, vel_a, 3, cells_x)
    sent += send_y(1)

    finish(gathering)
    gathering = gather_along_gx(0)

    finish(sent)
    outside_zero_x(vel_a, (0, 1, 2), 1, 2)
    prepare(1, True)

    stress_layers(1, vel_a, first, SXX, str_a, COL, ROW, 0, 3, True)
    sent = send_x(2, str_a, COL, str_a, inner_groups, 2, 1)
    stress_layers(1, vel_a, first, SXX, str_a, COL, ROW, 3, cells_x, True)
    sent += send_y(2)
    finish(gathering)
    arrived = rows_all[0].reshape(n_dev, 128)
    owned = jnp.sum(jnp.where(owners[...] == me, arrived, 0.0), axis=0, keepdims=True)
    owned = jnp.broadcast_to(owned, (8, 128))

    at_footing = (small_row < 3) & (small_lane == 0)
    drives, dampers = [], []
    for b in range(buildings):
        pick = jnp.minimum(small_row * buildings + b, 127)
        drives.append(jnp.where(at_footing, lane_gather(owned, pick), 0.0))
        pick = jnp.full((8, 128), 3 * buildings + b, jnp.int32)
        dampers.append(jnp.where(at_footing, lane_gather(owned, pick), 0.0))
    for b in range(buildings):
        damp_vec[0, b] = drives[b]
        damp_vec[1, b] = dampers[b]

    def frame_step(step, carry):
        for b in range(buildings):
            advance(b)
            internal_forces(b)
        return carry

    lax.fori_loop(0, FRAME_STEPS - 1, frame_step, 0)
    for b in range(buildings):
        advance(b)

    back = jnp.zeros((8, 128), F32)
    for b in range(buildings):
        whole = jnp.broadcast_to(foot_sum[b][:, 0:1], (8, 128))
        back = jnp.where(small_lane == small_row * buildings + b, whole, back)
    back = jnp.where(small_row < 3, back, 0.0)
    gathering = gather_along_gy(1, jnp.sum(back, axis=0, keepdims=True))

    finish(sent)
    outside_zero_x(str_a, (0, 3, 4), 2, 1)
    prepare(2, False)

    velocity_layers(2, str_a, 0, vel_a, vel_b, 0, 3, moved_out)
    sent_x = send_x(3, vel_b, COL, vel_b, move_groups, 1, 2)
    velocity_layers(2, str_a, 0, vel_a, vel_b, 3, cells_x, moved_out)
    sent_y = send_y(3)

    for b in range(buildings):
        piece = pl.ds(b * 128, 128)
        disp_out[:, piece] = disp[b][0:6]
        vel_out[:, piece] = vel[b][0:6]
    finish(gathering)
    gathering = gather_along_gx(1)

    finish(sent_y)
    prepare(3, True)
    stress_layers(3, vel_b, str_a, 0, str_b, 0, 0, 3, cells_x, False)
    finish(sent_x)
    outside_zero_x(vel_b, (0, 1, 2), 1, 2)
    stress_layers(3, vel_b, str_a, 0, str_b, 0, 0, 0, 3, False)

    wanted = owners[pl.ds(me, 1), :]
    finish(gathering)
    arrived = rows_all[1].reshape(n_dev, 128)
    held = jnp.where(iota((n_dev, 128), 0) == wanted, arrived, 0.0)
    held = jnp.broadcast_to(jnp.sum(held, axis=0, keepdims=True), (8, 128))
    for k in range(3):
        total = lane_gather(held, bid + k * buildings)
        force_out[k] = dash * (FRAME_STEPS * surface[k] - total)

    for copy in leaving:
        copy.wait_send()


def write_out(moved, stress, force, disp, vel, soil_out, force_out, disp_out, vel_out, sem):
    copies = [
        pltpu.make_async_copy(source, target, sem.at[k])
        for k, (source, target) in enumerate(
            (
                (stress, soil_out.at[pl.ds(3, 6)]),
                (moved, soil_out.at[pl.ds(0, 3)]),
                (force, force_out),
                (disp, disp_out),
                (vel, vel_out),
            )
        )
    ]
    for copy in copies:
        copy.start()
    for copy in copies:
        copy.wait()


def shards(n_gx, n_gy, *args):
    soil, material, dashpot, foot, table, stiff, links = args[:7]
    cells_x, cells_z, cells_y = soil.shape[1:]
    buildings = foot.shape[0]
    wide = (cells_x + 2 * COL, cells_z + 2 * ROW, cells_y)
    n_dev = n_gx * n_gy
    anywhere = pl.BlockSpec(memory_space=pl.ANY)
    vmem = pl.BlockSpec(memory_space=pltpu.VMEM)
    dma = pltpu.SemaphoreType.DMA
    limit = 40 * 1024 * 1024
    kept = (
        pltpu.VMEM((3, cells_x, cells_z, cells_y), F32),
        pltpu.VMEM((6, cells_x, cells_z, cells_y), F32),
        pltpu.VMEM((3, cells_x, cells_y), F32),
        pltpu.VMEM(args[9].shape, F32),
        pltpu.VMEM(args[10].shape, F32),
    )
    results = pl.pallas_call(
        functools.partial(kernel, n_gx, n_gy),
        out_shape=kept,
        in_specs=[pl.BlockSpec(memory_space=pltpu.HBM)] * len(args),
        out_specs=(vmem,) * len(kept),
        scratch_shapes=[
            pltpu.VMEM((9,) + wide, F32),
            pltpu.VMEM((3,) + wide, F32),
            pltpu.VMEM((6,) + wide, F32),
            pltpu.VMEM((3,) + wide, F32),
            pltpu.VMEM(material.shape, BF16),
            pltpu.VMEM(material.shape, F32),
            pltpu.VMEM(stiff.shape, F32),
            pltpu.VMEM(dashpot.shape, F32),
            pltpu.VMEM(foot.shape, jnp.int32),
            pltpu.VMEM(table.shape, jnp.int32),
            pltpu.VMEM(links.shape, jnp.int32),
            pltpu.SMEM(args[7].shape, jnp.int32),
            pltpu.VMEM(args[8].shape, F32),
            pltpu.VMEM(args[9].shape, F32),
            pltpu.VMEM(args[10].shape, F32),
            pltpu.VMEM((buildings, 256, 256), BF16),
            pltpu.VMEM((2, 256, 256), BF16),
            pltpu.VMEM((4, 3, cells_x // 4, 8, 128), F32),
            pltpu.VMEM((4, 3, cells_x // 4, 8, 128), F32),
            pltpu.VMEM((4, 3, cells_x // 4, 8, 128), F32),
            pltpu.VMEM((4, 3, cells_x // 4, 8, 128), F32),
            pltpu.VMEM((12, cells_x + LOW + HIGH, 2, 24, 128), F32),
            pltpu.VMEM((12, 8, 128), F32),
            pltpu.VMEM((3, 2, 12, 8, 128), F32),
            pltpu.VMEM((n_dev, 128), jnp.int32),
            pltpu.VMEM((8, 128), jnp.int32),
            pltpu.VMEM((2, buildings, 8, 128), F32),
            pltpu.VMEM((buildings, 8, 128), F32),
            pltpu.VMEM((buildings, 8, 128), F32),
            pltpu.VMEM((buildings, 8, 128), F32),
            pltpu.VMEM((buildings, 8, 128), F32),
            pltpu.VMEM((buildings, 8, 128), F32),
            pltpu.VMEM((buildings, 4, 8, 128), jnp.int32),
            pltpu.VMEM((2, n_gy, 1, 128), F32),
            pltpu.VMEM((2, n_gx, n_gy, 128), F32),
            dma((12,)),
            dma((4, 2, 2)),
            dma((4, 2, 2)),
            dma((4, 2)),
            dma((4, 2)),
            dma((2, n_gy - 1)),
            dma((2, n_gy - 1)),
            dma((2, n_gx - 1)),
            dma((2, n_gx - 1)),
            dma((12,)),
            dma((12,)),
        ],
        compiler_params=pltpu.CompilerParams(
            collective_id=0, has_side_effects=True, vmem_limit_bytes=limit
        ),
    )(*(pltpu.with_memory_space_constraint(value, pltpu.HBM) for value in args))
    return pl.pallas_call(
        write_out,
        out_shape=(
            jax.ShapeDtypeStruct(soil.shape, F32),
            jax.ShapeDtypeStruct((3, cells_x, cells_y), F32),
            jax.ShapeDtypeStruct(args[9].shape, F32),
            jax.ShapeDtypeStruct(args[10].shape, F32),
        ),
        in_specs=[vmem] * len(kept),
        out_specs=(anywhere,) * 4,
        scratch_shapes=[dma((len(kept),))],
        compiler_params=pltpu.CompilerParams(vmem_limit_bytes=limit),
    )(*results)


def solution(mesh):
    placed = (
        P(None, "gx", None, "gy"),
        P(None, "gx", None, "gy"),
        P("gx", "gy"),
        P(("gx", "gy"), None),
        P(),
        P(None, None, ("gx", "gy")),
        P(None, ("gx", "gy")),
        P(("gx", "gy")),
        P(None, ("gx", "gy")),
        P(None, ("gx", "gy")),
        P(None, ("gx", "gy")),
    )
    return jax.shard_map(
        functools.partial(shards, mesh.shape["gx"], mesh.shape["gy"]),
        mesh=mesh,
        in_specs=placed,
        out_specs=(
            P(None, "gx", None, "gy"),
            P(None, "gx", "gy"),
            P(None, ("gx", "gy")),
            P(None, ("gx", "gy")),
        ),
        check_vma=False,
    )
```

```python
import functools

import jax
import jax.numpy as jnp
from jax import lax
from jax.experimental import pallas as pl
from jax.experimental.pallas import tpu as pltpu
from jax.sharding import PartitionSpec as P

GROUPS = 4
FRAME_STEPS = 4
NEAR = 9.0 / 8.0
FAR = -1.0 / 24.0
TIME_SOIL = 0.18
TIME_FRAME = 0.05
MESH = pl.DeviceIdType.MESH
ROW = 8
COL = 2
LOW, HIGH = 5, 4
RIM = LOW + HIGH
SLOTS = 128 // RIM
F32 = jnp.float32
BF16 = jnp.bfloat16

VX, VY, VZ, SXX, SYY, SZZ, SXY, SXZ, SYZ = range(9)


def lane_gather(values, index):
    return lax.gather(
        values,
        index[:, :, None],
        lax.GatherDimensionNumbers(
            offset_dims=(),
            collapsed_slice_dims=(1,),
            start_index_map=(1,),
            operand_batching_dims=(0,),
            start_indices_batching_dims=(0,),
        ),
        (1, 1),
        mode=lax.GatherScatterMode.PROMISE_IN_BOUNDS,
    )


def iota(shape, dim):
    return lax.broadcasted_iota(jnp.int32, shape, dim)


def stencil(near_high, near_low, far_high, far_low):
    return NEAR * (near_high - near_low) + FAR * (far_high - far_low)


def rolled(value, shift):
    return pltpu.roll(value, shift, 1)


def kernel(
    n_gx,
    n_gy,
    soil,
    material,
    hbm_dashpot,
    hbm_foot,
    hbm_table,
    stiff,
    hbm_links,
    hbm_count,
    hbm_inverse_mass,
    hbm_frame_disp,
    hbm_frame_vel,
    moved_out,
    str_b,
    force_out,
    disp_out,
    vel_out,
    first,
    vel_a,
    str_a,
    vel_b,
    raw,
    coef,
    matrix,
    dashpot,
    foot,
    table,
    links,
    count,
    inverse_mass,
    frame_disp,
    frame_vel,
    spread,
    band,
    edges,
    from_low,
    from_high,
    correction,
    top,
    rims,
    rims_in,
    owners,
    bids,
    damp_vec,
    disp,
    vel,
    imass,
    foot_sum,
    internal,
    index,
    row_buf,
    rows_all,
    load_sem,
    x_send,
    x_recv,
    y_send,
    y_recv,
    a_send,
    a_recv,
    b_send,
    b_recv,
    t_send,
    t_recv,
):
    gx = lax.axis_index("gx")
    gy = lax.axis_index("gy")
    me = gx * n_gy + gy
    n_dev = n_gx * n_gy
    gx_up, gx_down = lax.rem(gx + 1, n_gx), lax.rem(gx + n_gx - 1, n_gx)
    gy_up, gy_down = lax.rem(gy + 1, n_gy), lax.rem(gy + n_gy - 1, n_gy)
    cells_x, cells_z, cells_y = soil.shape[1:]
    tiles_z = cells_z // 8
    buildings = foot.shape[0]
    inner = pl.ds(COL, cells_x)
    rows = pl.ds(ROW, cells_z)

    def load(k, source, target):
        copy = pltpu.make_async_copy(source, target, load_sem.at[k])
        copy.start()
        return copy

    load_stress = load(0, soil.at[pl.ds(SXX, 6)], first.at[pl.ds(SXX, 6), inner, rows])
    load_velocity = load(1, soil.at[pl.ds(0, 3)], first.at[pl.ds(0, 3), inner, rows])
    load_material = load(2, material, raw)
    load_small = [
        load(4 + k, source, target)
        for k, (source, target) in enumerate(
            (
                (hbm_dashpot, dashpot),
                (hbm_foot, foot),
                (hbm_table, table),
                (hbm_links, links),
                (hbm_count, count),
                (hbm_inverse_mass, inverse_mass),
                (hbm_frame_disp, frame_disp),
                (hbm_frame_vel, frame_vel),
            )
        )
    ]
    load_matrix = load(3, stiff, matrix)

    barrier = pltpu.get_barrier_semaphore()
    for k in range(1, n_gx):
        pl.semaphore_signal(
            barrier, inc=1, device_id={"gx": lax.rem(gx + k, n_gx)}, device_id_type=MESH
        )
    for k in range(1, n_gy):
        pl.semaphore_signal(
            barrier, inc=1, device_id={"gy": lax.rem(gy + k, n_gy)}, device_id_type=MESH
        )

    corners = [
        {"gx": row, "gy": column} for row in (gx_down, gx_up) for column in (gy_down, gy_up)
    ]
    for device in corners:
        pl.semaphore_signal(barrier, inc=1, device_id=device, device_id_type=MESH)

    zero_tile = jnp.zeros((8, cells_y), F32)

    def clear(x, carry):
        for ref, members in (
            (first, (SZZ, SXZ, SYZ)),
            (vel_a, (0, 1, 2)),
            (str_a, (2, 4, 5)),
            (vel_b, (0, 1, 2)),
        ):
            for member in members:
                ref[member, x, pl.ds(0, 8), :] = zero_tile
                ref[member, x, pl.ds(ROW + cells_z, 8), :] = zero_tile
        return carry

    lax.fori_loop(COL, COL + cells_x, clear, 0)

    def clear_top(x, carry):
        for member in (VX, VY, VZ, SZZ, SXZ, SYZ):
            for part in range(2):
                top[member, x, part, pl.ds(0, 8), :] = zero_tile
        return carry

    lax.fori_loop(0, top.shape[1], clear_top, 0)

    def remote(source, target, send, recv, device):
        copy = pltpu.make_async_remote_copy(
            src_ref=source,
            dst_ref=target,
            send_sem=send,
            recv_sem=recv,
            device_id=device,
            device_id_type=MESH,
        )
        copy.start()
        return copy

    def send_x(stage, source, start, target, groups, up, down):
        copies = []
        for k, (origin, member, size) in enumerate(groups):
            ids, into = pl.ds(origin, size), pl.ds(member, size)
            copies.append(
                remote(
                    source.at[ids, pl.ds(start + cells_x - up, up), rows if start else pl.ds(0, cells_z)],
                    target.at[into, pl.ds(COL - up, up), rows],
                    x_send.at[stage, k, 0],
                    x_recv.at[stage, k, 0],
                    {"gx": gx_up},
                )
            )
            copies.append(
                remote(
                    source.at[ids, pl.ds(start, down), rows if start else pl.ds(0, cells_z)],
                    target.at[into, pl.ds(COL + cells_x, down), rows],
                    x_send.at[stage, k, 1],
                    x_recv.at[stage, k, 1],
                    {"gx": gx_down},
                )
            )
        return copies

    def send_y(stage):
        return [
            remote(
                edges.at[stage],
                from_low.at[stage],
                y_send.at[stage, 0],
                y_recv.at[stage, 0],
                {"gy": gy_up},
            ),
            remote(
                edges.at[stage],
                from_high.at[stage],
                y_send.at[stage, 1],
                y_recv.at[stage, 1],
                {"gy": gy_down},
            ),
        ]

    leaving = []

    def finish(copies):
        for copy in copies:
            copy.wait_recv()
        leaving.extend(copies)

    def outside_zero_x(ref, members, low, high):
        @pl.when(gx == 0)
        def _():
            for member in members:
                for layer in range(low):
                    ref[member, COL - 1 - layer, rows, :] = jnp.zeros((cells_z, cells_y), F32)

        @pl.when(gx == n_gx - 1)
        def _():
            for member in members:
                for layer in range(high):
                    ref[member, COL + cells_x + layer, rows, :] = jnp.zeros((cells_z, cells_y), F32)

    lane = iota((8, cells_y), 1)
    slot = lane & 3

    def pack(stage, values, cell):
        group = cell // 4
        for k in range(3):
            packed = edges[stage, k, group]
            for z in range(tiles_z):
                place = (cell & 3) * tiles_z + z
                packed = jnp.where(
                    lane >> 2 == place, rolled(values[z][k], (4 * place + 2) & 127), packed
                )
            edges[stage, k, group] = packed

    def prepare(stage, forward):
        for k in range(3):
            for group in range(edges.shape[2]):
                low = jnp.where(gy > 0, from_low[stage, k, group], 0.0)
                high = jnp.where(gy < n_gy - 1, from_high[stage, k, group], 0.0)
                beyond = jnp.where(slot < 2, low, high)
                back_2, back_1 = rolled(beyond, 126), rolled(beyond, 127)
                on_1, on_2 = rolled(beyond, 1), rolled(beyond, 2)
                if forward:
                    value = jnp.where(
                        slot == 0,
                        FAR * back_2,
                        jnp.where(
                            slot == 1,
                            NEAR * back_1 + FAR * back_2,
                            jnp.where(slot == 2, -FAR * on_1, 0.0),
                        ),
                    )
                else:
                    value = jnp.where(
                        slot == 1,
                        FAR * back_1,
                        jnp.where(
                            slot == 2,
                            -NEAR * on_1 - FAR * on_2,
                            jnp.where(slot == 3, -FAR * on_2, 0.0),
                        ),
                    )
                correction[stage, k, group] = value

    at_edge = (lane < 2) | (lane >= cells_y - 2)

    def along_y(ref, members, stage, cell, forward):
        parts = []
        for member in members:
            value = ref[member, cell + COL, rows, :]
            high = value.astype(BF16)
            low = (value - high.astype(F32)).astype(BF16)
            parts.append(jnp.concatenate([high, low], 1))
        both = jnp.dot(
            jnp.concatenate(parts, 0), band[int(forward)], preferred_element_type=F32
        )
        group = cell // 4
        result = []
        for z in range(tiles_z):
            shift = (254 - 4 * ((cell & 3) * tiles_z + z)) & 127
            line = []
            for k in range(3):
                tile = slice(k * cells_z + 8 * z, k * cells_z + 8 * z + 8)
                inside = NEAR * both[tile, 0:128] + FAR * both[tile, 128:256]
                line.append(
                    inside + jnp.where(at_edge, rolled(correction[stage, k, group], shift), 0.0)
                )
            result.append(line)
        return result

    def at(ref, member, x, row):
        return ref[member, x, pl.ds(row, 8), :]

    def along_x(ref, member, x, row, forward):
        shift = 1 if forward else 0
        return stencil(
            at(ref, member, x + shift, row),
            at(ref, member, x + shift - 1, row),
            at(ref, member, x + shift + 1, row),
            at(ref, member, x + shift - 2, row),
        )

    def along_z(ref, member, x, row, forward):
        shift = 1 if forward else 0
        return stencil(
            at(ref, member, x, row + shift),
            at(ref, member, x, row + shift - 1),
            at(ref, member, x, row + shift + 1),
            at(ref, member, x, row + shift - 2),
        )

    def velocity_layers(stage, stress, base, old, new, begin, end, out=None):
        sxx, syy, szz, sxy, sxz, syz = range(base, base + 6)

        def layer(i, carry):
            cell = (i + cells_x - 1) & (cells_x - 1)
            x = cell + COL
            y_all = along_y(stress, (sxy, syy, syz), stage, cell, False)
            results = []
            for z in range(tiles_z):
                row = ROW + 8 * z
                y_of = y_all[z]
                accel = (
                    along_x(stress, sxx, x, row, False) + y_of[0] + along_z(stress, sxz, x, row, False),
                    along_x(stress, sxy, x, row, False) + y_of[1] + along_z(stress, syz, x, row, False),
                    along_x(stress, sxz, x, row, False) + y_of[2] + along_z(stress, szz, x, row, False),
                )
                density = coef[0, cell, pl.ds(8 * z, 8), :]
                after = [at(old, k, x, row) + density * accel[k] for k in range(3)]
                for k in range(3):
                    new[k, x, pl.ds(row, 8), :] = after[k]
                    if out is not None:
                        out[k, cell, pl.ds(8 * z, 8), :] = after[k]
                results.append(after)
            pack(stage + 1, results, cell)
            return carry

        lax.fori_loop(begin, end, layer, 0)

    def stress_layers(stage, moving, stress, base, new, new_x, new_row, begin, end, packing):
        def layer(i, carry):
            cell = (i + cells_x - 2) & (cells_x - 1)
            x = cell + COL
            y_all = along_y(moving, (0, 1, 2), stage, cell, True)
            results = []
            for z in range(tiles_z):
                row = ROW + 8 * z
                y_of = y_all[z]
                x_of = [along_x(moving, k, x, row, True) for k in range(3)]
                z_of = [along_z(moving, k, x, row, True) for k in range(3)]
                lame = coef[1, cell, pl.ds(8 * z, 8), :]
                shear = coef[2, cell, pl.ds(8 * z, 8), :]
                volume = lame * (x_of[0] + y_of[1] + z_of[2])
                twice = shear + shear
                change = (
                    volume + twice * x_of[0],
                    volume + twice * y_of[1],
                    volume + twice * z_of[2],
                    shear * (y_of[0] + x_of[1]),
                    shear * (z_of[0] + x_of[2]),
                    shear * (z_of[1] + y_of[2]),
                )
                after = [at(stress, base + k, x, row) + change[k] for k in range(6)]
                for k in range(6):
                    new[k, cell + new_x, pl.ds(new_row + 8 * z, 8), :] = after[k]
                results.append((after[3], after[1], after[5]))
            if packing:
                pack(stage + 1, results, cell)
            return carry

        lax.fori_loop(begin, end, layer, 0)

    stress_groups = ((SXX, SXX, 1), (SXY, SXY, 2))
    inner_groups = ((0, 0, 1), (3, 3, 2))
    move_groups = ((0, 0, 3),)

    fields = top.shape[0]

    def top_own(cell, carry):
        for member in range(fields):
            if member < 9:
                value = at(first, member, cell + COL, ROW)
            else:
                value = coef[member - 9, cell, pl.ds(0, 8), :]
            top[member, cell + LOW, 0, pl.ds(8, 8), :] = value
        return carry

    def pack_rims():
        packed = None
        for slot_id in range(fields * cells_x):
            member, cell = divmod(slot_id, cells_x)
            begin = RIM * (slot_id % SLOTS)
            value = rolled(top[member, cell + LOW, 0, pl.ds(8, 8), :], (begin + LOW) % 128)
            packed = value if begin == 0 else jnp.where(lane < begin, packed, value)
            if slot_id % SLOTS == SLOTS - 1 or slot_id == fields * cells_x - 1:
                rims[slot_id // SLOTS] = packed

    rim_tiles = -(-fields * cells_x // SLOTS)
    corner_tiles = -(-(fields - 2) * cells_x // SLOTS)

    def send_top():
        copies = []
        top_rows = pl.ds(8, 8)
        flow = (
            (first, VX, 3, VX, 3, 3, ROW, COL),
            (first, SXX, 6, SXX, LOW, HIGH, ROW, COL),
            (coef, 0, 3, 9, 3, 3, 0, 0),
        )
        for k, (source, origin, size, member, up, down, row, layer) in enumerate(flow):
            copies.append(
                remote(
                    source.at[pl.ds(origin, size), pl.ds(layer + cells_x - up, up), pl.ds(row, 8)],
                    top.at[pl.ds(member, size), pl.ds(LOW - up, up), 0, top_rows],
                    t_send.at[k],
                    t_recv.at[k],
                    {"gx": gx_up},
                )
            )
            copies.append(
                remote(
                    source.at[pl.ds(origin, size), pl.ds(layer, down), pl.ds(row, 8)],
                    top.at[pl.ds(member, size), pl.ds(LOW + cells_x, down), 0, top_rows],
                    t_send.at[3 + k],
                    t_recv.at[3 + k],
                    {"gx": gx_down},
                )
            )
        for k, (device, row, column, size) in enumerate(
            (
                ({"gx": gx_up, "gy": gy_up}, 0, 0, corner_tiles),
                ({"gx": gx_up, "gy": gy_down}, 0, 1, corner_tiles),
                ({"gx": gx_down, "gy": gy_up}, 2, 0, corner_tiles),
                ({"gx": gx_down, "gy": gy_down}, 2, 1, corner_tiles),
                ({"gy": gy_up}, 1, 0, rim_tiles),
                ({"gy": gy_down}, 1, 1, rim_tiles),
            )
        ):
            copies.append(
                remote(
                    rims.at[pl.ds(0, size)],
                    rims_in.at[row, column, pl.ds(0, size)],
                    t_send.at[6 + k],
                    t_recv.at[6 + k],
                    device,
                )
            )
        return copies

    def unpack_rims():
        spot = lane - RIM * ((lane * 57) >> 9)
        near = (lane < HIGH) | (lane >= 128 - LOW)

        for row, tiles, members, cells, shown in (
            (1, rim_tiles, fields, range(cells_x), True),
            (0, corner_tiles, fields - 2, range(cells_x - LOW, cells_x), gx > 0),
            (2, corner_tiles, fields - 2, range(HIGH), gx < n_gx - 1),
        ):
            both = []
            for tile in range(tiles):
                low = jnp.where(shown & (gy > 0), rims_in[row, 0, tile], 0.0)
                high = jnp.where(shown & (gy < n_gy - 1), rims_in[row, 1, tile], 0.0)
                both.append(jnp.where(spot < LOW, low, high))
            for cell in cells:
                x = cell + LOW + (row - 1) * cells_x
                for member in range(fields):
                    if member < members:
                        slot_id = member * cells_x + cell
                        begin = RIM * (slot_id % SLOTS)
                        value = rolled(both[slot_id // SLOTS], (256 - LOW - begin) % 128)
                        value = jnp.where(near, value, 0.0)
                    else:
                        value = zero_tile
                    top[member, x, 1, pl.ds(8, 8), :] = value

        def outside(x, carry):
            for member in range(fields):
                top[member, x, 0, pl.ds(8, 8), :] = zero_tile
            return carry

        @pl.when(gx == 0)
        def _():
            lax.fori_loop(0, LOW, outside, 0)

        @pl.when(gx == n_gx - 1)
        def _():
            lax.fori_loop(LOW + cells_x, LOW + cells_x + HIGH, outside, 0)

    def top_at(member, x, part, row=8):
        return top[member, x, part, pl.ds(row, 8), :]

    def top_along_y(member, x, forward):
        parts = [top_at(member, x, 0), top_at(member, x, 1)]

        def moved(shift):
            mine, other = [rolled(part, shift & 127) for part in parts]
            across = lane < shift if shift > 0 else lane >= 128 + shift
            return jnp.where(across, other, mine), jnp.where(across, mine, other)

        if forward:
            terms = (moved(-1), parts, moved(-2), moved(1))
        else:
            terms = (parts, moved(1), moved(-1), moved(2))
        return [stencil(*(term[part] for term in terms)) for part in range(2)]

    def top_along_x(member, x, part, shift):
        return stencil(
            top_at(member, x + shift, part),
            top_at(member, x + shift - 1, part),
            top_at(member, x + shift + 1, part),
            top_at(member, x + shift - 2, part),
        )

    def top_along_z(member, x, part, shift):
        return stencil(
            top_at(member, x, part, 8 + shift),
            top_at(member, x, part, 7 + shift),
            top_at(member, x, part, 9 + shift),
            top_at(member, x, part, 6 + shift),
        )

    def top_velocity(x, parts):
        y_of = [top_along_y(member, x, False) for member in (SXY, SYY, SYZ)]
        for part in range(parts):
            accel = (
                top_along_x(SXX, x, part, 0) + y_of[0][part] + top_along_z(SXZ, x, part, 0),
                top_along_x(SXY, x, part, 0) + y_of[1][part] + top_along_z(SYZ, x, part, 0),
                top_along_x(SXZ, x, part, 0) + y_of[2][part] + top_along_z(SZZ, x, part, 0),
            )
            for k in range(3):
                top[k, x, part, pl.ds(8, 8), :] = (
                    top_at(k, x, part) + top_at(9, x, part) * accel[k]
                )

    def top_stress(x):
        y_of = [top_along_y(member, x, True) for member in range(3)]
        for part in range(2):
            x_of = [top_along_x(member, x, part, 1) for member in range(3)]
            z_of = [top_along_z(member, x, part, 1) for member in range(3)]
            shear = top_at(11, x, part)
            volume = top_at(10, x, part) * (x_of[0] + y_of[1][part] + z_of[2])
            twice = shear + shear
            change = (
                volume + twice * x_of[0],
                volume + twice * y_of[1][part],
                volume + twice * z_of[2],
                shear * (y_of[0][part] + x_of[1]),
                shear * (z_of[0] + x_of[2]),
                shear * (z_of[1] + y_of[2][part]),
            )
            for k in range(6):
                top[SXX + k, x, part, pl.ds(8, 8), :] = top_at(SXX + k, x, part) + change[k]

    def top_layers(update, begin, size, groups, *more):
        def layers(i, carry):
            for k in range(size):
                update(begin + i * size + k, *more)
            return carry

        lax.fori_loop(0, groups, layers, 0)

    load_stress.wait()

    edges[...] = jnp.zeros(edges.shape, F32)

    def pack_first(cell, carry):
        values = [
            [at(first, k, cell + COL, ROW + 8 * z) for k in (SXY, SYY, SYZ)] for z in range(tiles_z)
        ]
        pack(0, values, cell)
        return carry

    lax.fori_loop(0, cells_x, pack_first, 0)

    load_material.wait()

    def widen(cell, carry):
        for k in range(3):
            coef[k, cell] = TIME_SOIL * raw[k, cell].astype(F32)
        return carry

    lax.fori_loop(0, cells_x, widen, 0)
    load_velocity.wait()
    source = iota((256, 256), 0) & 127
    column = iota((256, 256), 1)
    wanted = column & 127
    for forward in range(2):
        reach = jnp.where(column < 128, 0, 1)
        plus = source == wanted + forward + reach
        minus = source == wanted + forward - 1 - reach
        band[forward] = jnp.where(plus, 1.0, jnp.where(minus, -1.0, 0.0)).astype(BF16)


    for copy in load_small:
        copy.wait()
    big = (128, 128)
    big_lane = iota(big, 1)
    big_lane_f = big_lane.astype(F32)
    small_row = iota((8, 128), 0)
    small_lane = iota((8, 128), 1)

    for b in range(buildings):
        for h in range(2):
            piece = pl.ds(b * 256 + h * 128, 128)
            live = iota((1, 128), 1) + h * 128 < count[b]
            for end in range(2):
                nodes = links[pl.ds(end, 1), piece]
                index[b, h * 2 + end] = jnp.broadcast_to(nodes, (8, 128))
                kept = jnp.where(live, nodes, -1).astype(F32)
                columns = jnp.broadcast_to(kept, big).T
                spread[b, pl.ds(h * 128, 128), pl.ds(end * 128, 128)] = (
                    jnp.where(columns == big_lane_f, 1.0, 0.0).astype(BF16)
                )

    group_of = (iota((n_dev, 128), 1) // 2) % GROUPS
    holder = iota((n_dev, 128), 0)
    for j in range(1, GROUPS):
        entries = table[pl.ds(j - 1, 1), :].astype(F32)
        columns = jnp.broadcast_to(entries, (128, n_dev)).T.astype(jnp.int32)
        holder = jnp.where(group_of == j, columns, holder)
    owners[...] = holder

    bid = jnp.zeros((16, 128), F32)
    for b in range(buildings):
        cell = foot[pl.ds(b, 1), :]
        place_x = jnp.where(iota((16, 128), 0) == cell // cells_y, float(b), 0.0).astype(BF16)
        place_y = jnp.where(iota(big, 0) == cell % cells_y, 1.0, 0.0).astype(BF16)
        bid += lax.dot_general(
            place_x, place_y, (((1,), (1,)), ((), ())), preferred_element_type=F32
        )
    bids[...] = bid[0:8].astype(jnp.int32)

    blank = jnp.zeros((2, 128), F32)
    for b in range(buildings):
        piece = pl.ds(b * 128, 128)
        disp[b] = jnp.concatenate([frame_disp[:, piece], blank], 0)
        vel[b] = jnp.concatenate([frame_vel[:, piece], blank], 0)
        imass[b] = TIME_FRAME * jnp.concatenate([inverse_mass[:, piece], blank], 0)
        foot_sum[b] = jnp.zeros((8, 128), F32)

    load_matrix.wait()

    def internal_forces(b):
        place = disp[b]
        forces = []
        for h in range(2):
            ends = (
                lane_gather(place, index[b, h * 2]),
                lane_gather(place, index[b, h * 2 + 1]),
            )
            piece = pl.ds(b * 256 + h * 128, 128)
            total = None
            for a in range(12):
                row = ends[a // 6][a % 6 : a % 6 + 1, :]
                term = matrix[a, :, piece] * row
                total = term if total is None else total + term
            forces.append(jnp.concatenate([total, jnp.zeros((4, 128), F32)], 0))
        forces = jnp.concatenate(forces, 1)
        high = forces.astype(BF16)
        low = (forces - high.astype(F32)).astype(BF16)
        parts = jnp.dot(
            jnp.concatenate([high, low], 0), spread[b], preferred_element_type=F32
        )
        parts = parts[0:16] + parts[16:32]
        internal[b] = parts[0:8, 0:128] + parts[6:14, 128:256]

    def advance(b):
        speed = vel[b]
        loads = damp_vec[0, b] - damp_vec[1, b] * speed - internal[b]
        speed = speed + imass[b] * loads
        vel[b] = speed
        disp[b] = disp[b] + TIME_FRAME * speed
        foot_sum[b] += speed

    for b in range(buildings):
        internal_forces(b)

    lax.fori_loop(0, cells_x, top_own, 0)
    pack_rims()
    pl.semaphore_wait(barrier, n_gx + n_gy + 2)
    sent_y = send_y(0)
    sent_top = send_top()
    sent_x = send_x(0, soil, 0, first, stress_groups, 2, 1)

    finish(sent_y)
    prepare(0, False)
    velocity_layers(0, first, SXX, first, vel_a, 3, cells_x)

    finish(sent_top)
    unpack_rims()
    top_layers(top_velocity, LOW - 3, 7, (cells_x + 6) // 7, 2)
    top_layers(top_stress, LOW - 2, 4, (cells_x + 4) // 4)
    top_layers(top_velocity, LOW, 4, cells_x // 4, 1)

    surface = [top[k, pl.ds(LOW, cells_x), 0, 8, :] for k in range(3)]
    dash = dashpot[...]
    terms = [dash * surface[0], dash * surface[1], dash * surface[2], dash]
    bid = bids[...]
    sums = [
        jnp.sum(jnp.where(bid == b, term, 0.0), axis=0, keepdims=True)
        for term in terms
        for b in range(buildings)
    ]
    sums = jnp.concatenate(sums + [jnp.zeros((128 - len(sums), 128), F32)], 0)
    mine = jnp.sum(sums.T, axis=0, keepdims=True)

    def far_first(count, ring):
        outer = count // ring

        def hops(k):
            return min(k // ring, outer - k // ring) + (min(k % ring, ring - k % ring) if ring > 2 else 0)

        return sorted(range(1, count), key=lambda k: -hops(k))

    def gather_along_gy(turn, value):
        row_buf[turn, gy] = value
        return [
            remote(
                row_buf.at[turn, gy],
                row_buf.at[turn, gy],
                a_send.at[turn, k - 1],
                a_recv.at[turn, k - 1],
                {"gy": lax.rem(gy + k, n_gy)},
            )
            for k in far_first(n_gy, 4)
        ]

    def gather_along_gx(turn):
        rows_all[turn, gx] = row_buf[turn].reshape(n_gy, 128)
        return [
            remote(
                rows_all.at[turn, gx],
                rows_all.at[turn, gx],
                b_send.at[turn, k - 1],
                b_recv.at[turn, k - 1],
                {"gx": lax.rem(gx + k, n_gx)},
            )
            for k in far_first(n_gx, 2)
        ]

    gathering = gather_along_gy(0, mine)

    finish(sent_x)
    outside_zero_x(first, (SXX, SXY, SXZ), 2, 1)
    velocity_layers(0, first, SXX, first, vel_a, 0, 3)
    sent = send_x(1, vel_a, COL, vel_a, move_groups, 1, 2)
    sent += send_y(1)

    finish(gathering)
    gathering = gather_along_gx(0)

    finish(sent)
    outside_zero_x(vel_a, (0, 1, 2), 1, 2)
    prepare(1, True)

    stress_layers(1, vel_a, first, SXX, str_a, COL, ROW, 0, 3, True)
    sent = send_x(2, str_a, COL, str_a, inner_groups, 2, 1)
    stress_layers(1, vel_a, first, SXX, str_a, COL, ROW, 3, cells_x, True)
    sent += send_y(2)
    finish(gathering)
    arrived = rows_all[0].reshape(n_dev, 128)
    owned = jnp.sum(jnp.where(owners[...] == me, arrived, 0.0), axis=0, keepdims=True)
    owned = jnp.broadcast_to(owned, (8, 128))

    at_footing = (small_row < 3) & (small_lane == 0)
    drives, dampers = [], []
    for b in range(buildings):
        pick = jnp.minimum(small_row * buildings + b, 127)
        drives.append(jnp.where(at_footing, lane_gather(owned, pick), 0.0))
        pick = jnp.full((8, 128), 3 * buildings + b, jnp.int32)
        dampers.append(jnp.where(at_footing, lane_gather(owned, pick), 0.0))
    for b in range(buildings):
        damp_vec[0, b] = drives[b]
        damp_vec[1, b] = dampers[b]

    def frame_step(step, carry):
        for b in range(buildings):
            advance(b)
            internal_forces(b)
        return carry

    lax.fori_loop(0, FRAME_STEPS - 1, frame_step, 0)
    for b in range(buildings):
        advance(b)

    back = jnp.zeros((8, 128), F32)
    for b in range(buildings):
        whole = jnp.broadcast_to(foot_sum[b][:, 0:1], (8, 128))
        back = jnp.where(small_lane == small_row * buildings + b, whole, back)
    back = jnp.where(small_row < 3, back, 0.0)
    gathering = gather_along_gy(1, jnp.sum(back, axis=0, keepdims=True))

    finish(sent)
    outside_zero_x(str_a, (0, 3, 4), 2, 1)
    prepare(2, False)

    velocity_layers(2, str_a, 0, vel_a, vel_b, 0, 3, moved_out)
    sent_x = send_x(3, vel_b, COL, vel_b, move_groups, 1, 2)
    velocity_layers(2, str_a, 0, vel_a, vel_b, 3, cells_x, moved_out)
    sent_y = send_y(3)

    for b in range(buildings):
        piece = pl.ds(b * 128, 128)
        disp_out[:, piece] = disp[b][0:6]
        vel_out[:, piece] = vel[b][0:6]
    finish(gathering)
    gathering = gather_along_gx(1)

    finish(sent_y)
    prepare(3, True)
    stress_layers(3, vel_b, str_a, 0, str_b, 0, 0, 3, cells_x, False)
    finish(sent_x)
    outside_zero_x(vel_b, (0, 1, 2), 1, 2)
    stress_layers(3, vel_b, str_a, 0, str_b, 0, 0, 0, 3, False)

    wanted = owners[pl.ds(me, 1), :]
    finish(gathering)
    arrived = rows_all[1].reshape(n_dev, 128)
    held = jnp.where(iota((n_dev, 128), 0) == wanted, arrived, 0.0)
    held = jnp.broadcast_to(jnp.sum(held, axis=0, keepdims=True), (8, 128))
    for k in range(3):
        total = lane_gather(held, bid + k * buildings)
        force_out[k] = dash * (FRAME_STEPS * surface[k] - total)

    for copy in leaving:
        copy.wait_send()


def write_out(moved, stress, force, disp, vel, soil_out, force_out, disp_out, vel_out, sem):
    copies = [
        pltpu.make_async_copy(source, target, sem.at[k])
        for k, (source, target) in enumerate(
            (
                (stress, soil_out.at[pl.ds(3, 6)]),
                (moved, soil_out.at[pl.ds(0, 3)]),
                (force, force_out),
                (disp, disp_out),
                (vel, vel_out),
            )
        )
    ]
    for copy in copies:
        copy.start()
    for copy in copies:
        copy.wait()


def shards(n_gx, n_gy, *args):
    soil, material, dashpot, foot, table, stiff, links = args[:7]
    cells_x, cells_z, cells_y = soil.shape[1:]
    buildings = foot.shape[0]
    wide = (cells_x + 2 * COL, cells_z + 2 * ROW, cells_y)
    n_dev = n_gx * n_gy
    anywhere = pl.BlockSpec(memory_space=pl.ANY)
    vmem = pl.BlockSpec(memory_space=pltpu.VMEM)
    dma = pltpu.SemaphoreType.DMA
    limit = 40 * 1024 * 1024
    kept = (
        pltpu.VMEM((3, cells_x, cells_z, cells_y), F32),
        pltpu.VMEM((6, cells_x, cells_z, cells_y), F32),
        pltpu.VMEM((3, cells_x, cells_y), F32),
        pltpu.VMEM(args[9].shape, F32),
        pltpu.VMEM(args[10].shape, F32),
    )
    results = pl.pallas_call(
        functools.partial(kernel, n_gx, n_gy),
        out_shape=kept,
        in_specs=[pl.BlockSpec(memory_space=pltpu.HBM)] * len(args),
        out_specs=(vmem,) * len(kept),
        scratch_shapes=[
            pltpu.VMEM((9,) + wide, F32),
            pltpu.VMEM((3,) + wide, F32),
            pltpu.VMEM((6,) + wide, F32),
            pltpu.VMEM((3,) + wide, F32),
            pltpu.VMEM(material.shape, BF16),
            pltpu.VMEM(material.shape, F32),
            pltpu.VMEM(stiff.shape, F32),
            pltpu.VMEM(dashpot.shape, F32),
            pltpu.VMEM(foot.shape, jnp.int32),
            pltpu.VMEM(table.shape, jnp.int32),
            pltpu.VMEM(links.shape, jnp.int32),
            pltpu.SMEM(args[7].shape, jnp.int32),
            pltpu.VMEM(args[8].shape, F32),
            pltpu.VMEM(args[9].shape, F32),
            pltpu.VMEM(args[10].shape, F32),
            pltpu.VMEM((buildings, 256, 256), BF16),
            pltpu.VMEM((2, 256, 256), BF16),
            pltpu.VMEM((4, 3, cells_x // 4, 8, 128), F32),
            pltpu.VMEM((4, 3, cells_x // 4, 8, 128), F32),
            pltpu.VMEM((4, 3, cells_x // 4, 8, 128), F32),
            pltpu.VMEM((4, 3, cells_x // 4, 8, 128), F32),
            pltpu.VMEM((12, cells_x + LOW + HIGH, 2, 24, 128), F32),
            pltpu.VMEM((-(-12 * cells_x // SLOTS), 8, 128), F32),
            pltpu.VMEM((3, 2, -(-12 * cells_x // SLOTS), 8, 128), F32),
            pltpu.VMEM((n_dev, 128), jnp.int32),
            pltpu.VMEM((8, 128), jnp.int32),
            pltpu.VMEM((2, buildings, 8, 128), F32),
            pltpu.VMEM((buildings, 8, 128), F32),
            pltpu.VMEM((buildings, 8, 128), F32),
            pltpu.VMEM((buildings, 8, 128), F32),
            pltpu.VMEM((buildings, 8, 128), F32),
            pltpu.VMEM((buildings, 8, 128), F32),
            pltpu.VMEM((buildings, 4, 8, 128), jnp.int32),
            pltpu.VMEM((2, n_gy, 1, 128), F32),
            pltpu.VMEM((2, n_gx, n_gy, 128), F32),
            dma((12,)),
            dma((4, 2, 2)),
            dma((4, 2, 2)),
            dma((4, 2)),
            dma((4, 2)),
            dma((2, n_gy - 1)),
            dma((2, n_gy - 1)),
            dma((2, n_gx - 1)),
            dma((2, n_gx - 1)),
            dma((12,)),
            dma((12,)),
        ],
        compiler_params=pltpu.CompilerParams(
            collective_id=0, has_side_effects=True, vmem_limit_bytes=limit
        ),
    )(*(pltpu.with_memory_space_constraint(value, pltpu.HBM) for value in args))
    return pl.pallas_call(
        write_out,
        out_shape=(
            jax.ShapeDtypeStruct(soil.shape, F32),
            jax.ShapeDtypeStruct((3, cells_x, cells_y), F32),
            jax.ShapeDtypeStruct(args[9].shape, F32),
            jax.ShapeDtypeStruct(args[10].shape, F32),
        ),
        in_specs=[vmem] * len(kept),
        out_specs=(anywhere,) * 4,
        scratch_shapes=[dma((len(kept),))],
        compiler_params=pltpu.CompilerParams(vmem_limit_bytes=limit),
    )(*results)


def solution(mesh):
    placed = (
        P(None, "gx", None, "gy"),
        P(None, "gx", None, "gy"),
        P("gx", "gy"),
        P(("gx", "gy"), None),
        P(),
        P(None, None, ("gx", "gy")),
        P(None, ("gx", "gy")),
        P(("gx", "gy")),
        P(None, ("gx", "gy")),
        P(None, ("gx", "gy")),
        P(None, ("gx", "gy")),
    )
    return jax.shard_map(
        functools.partial(shards, mesh.shape["gx"], mesh.shape["gy"]),
        mesh=mesh,
        in_specs=placed,
        out_specs=(
            P(None, "gx", None, "gy"),
            P(None, "gx", "gy"),
            P(None, ("gx", "gy")),
            P(None, ("gx", "gy")),
        ),
        check_vma=False,
    )
```

```python
import functools

import jax
import jax.numpy as jnp
from jax import lax
from jax.experimental import pallas as pl
from jax.experimental.pallas import tpu as pltpu
from jax.sharding import PartitionSpec as P

GROUPS = 4
FRAME_STEPS = 4
NEAR = 9.0 / 8.0
FAR = -1.0 / 24.0
TIME_SOIL = 0.18
TIME_FRAME = 0.05
MESH = pl.DeviceIdType.MESH
ROW = 8
COL = 2
LOW, HIGH = 5, 4
RIM = LOW + HIGH
SLOTS = 128 // RIM
F32 = jnp.float32
BF16 = jnp.bfloat16

VX, VY, VZ, SXX, SYY, SZZ, SXY, SXZ, SYZ = range(9)


def lane_gather(values, index):
    return lax.gather(
        values,
        index[:, :, None],
        lax.GatherDimensionNumbers(
            offset_dims=(),
            collapsed_slice_dims=(1,),
            start_index_map=(1,),
            operand_batching_dims=(0,),
            start_indices_batching_dims=(0,),
        ),
        (1, 1),
        mode=lax.GatherScatterMode.PROMISE_IN_BOUNDS,
    )


def iota(shape, dim):
    return lax.broadcasted_iota(jnp.int32, shape, dim)


def stencil(near_high, near_low, far_high, far_low):
    return NEAR * (near_high - near_low) + FAR * (far_high - far_low)


def rolled(value, shift):
    return pltpu.roll(value, shift, 1)


def kernel(
    n_gx,
    n_gy,
    soil,
    material,
    hbm_dashpot,
    hbm_foot,
    hbm_table,
    stiff,
    hbm_links,
    hbm_count,
    hbm_inverse_mass,
    hbm_frame_disp,
    hbm_frame_vel,
    moved_out,
    str_b,
    force_out,
    disp_out,
    vel_out,
    first,
    vel_a,
    str_a,
    vel_b,
    raw,
    coef,
    matrix,
    dashpot,
    foot,
    table,
    links,
    count,
    inverse_mass,
    frame_disp,
    frame_vel,
    spread,
    band,
    edges,
    from_low,
    from_high,
    correction,
    top,
    rims,
    rims_in,
    owners,
    bids,
    damp_vec,
    disp,
    vel,
    imass,
    foot_sum,
    internal,
    index,
    row_buf,
    rows_all,
    load_sem,
    x_send,
    x_recv,
    y_send,
    y_recv,
    a_send,
    a_recv,
    b_send,
    b_recv,
    t_send,
    t_recv,
):
    gx = lax.axis_index("gx")
    gy = lax.axis_index("gy")
    me = gx * n_gy + gy
    n_dev = n_gx * n_gy
    gx_up, gx_down = lax.rem(gx + 1, n_gx), lax.rem(gx + n_gx - 1, n_gx)
    gy_up, gy_down = lax.rem(gy + 1, n_gy), lax.rem(gy + n_gy - 1, n_gy)
    cells_x, cells_z, cells_y = soil.shape[1:]
    tiles_z = cells_z // 8
    buildings = foot.shape[0]
    inner = pl.ds(COL, cells_x)
    rows = pl.ds(ROW, cells_z)

    def load(k, source, target):
        copy = pltpu.make_async_copy(source, target, load_sem.at[k])
        copy.start()
        return copy

    load_stress = load(0, soil.at[pl.ds(SXX, 6)], first.at[pl.ds(SXX, 6), inner, rows])
    load_velocity = load(1, soil.at[pl.ds(0, 3)], first.at[pl.ds(0, 3), inner, rows])
    load_material = load(2, material, raw)
    load_small = [
        load(4 + k, source, target)
        for k, (source, target) in enumerate(
            (
                (hbm_dashpot, dashpot),
                (hbm_foot, foot),
                (hbm_table, table),
                (hbm_links, links),
                (hbm_count, count),
                (hbm_inverse_mass, inverse_mass),
                (hbm_frame_disp, frame_disp),
                (hbm_frame_vel, frame_vel),
            )
        )
    ]
    load_matrix = load(3, stiff, matrix)

    barrier = pltpu.get_barrier_semaphore()
    for k in range(1, n_gx):
        pl.semaphore_signal(
            barrier, inc=1, device_id={"gx": lax.rem(gx + k, n_gx)}, device_id_type=MESH
        )
    for k in range(1, n_gy):
        pl.semaphore_signal(
            barrier, inc=1, device_id={"gy": lax.rem(gy + k, n_gy)}, device_id_type=MESH
        )

    corners = [
        {"gx": row, "gy": column} for row in (gx_down, gx_up) for column in (gy_down, gy_up)
    ]
    for device in corners:
        pl.semaphore_signal(barrier, inc=1, device_id=device, device_id_type=MESH)

    zero_tile = jnp.zeros((8, cells_y), F32)

    def clear(x, carry):
        for ref, members in (
            (first, (SZZ, SXZ, SYZ)),
            (vel_a, (0, 1, 2)),
            (str_a, (2, 4, 5)),
            (vel_b, (0, 1, 2)),
        ):
            for member in members:
                ref[member, x, pl.ds(0, 8), :] = zero_tile
                ref[member, x, pl.ds(ROW + cells_z, 8), :] = zero_tile
        return carry

    lax.fori_loop(COL, COL + cells_x, clear, 0)

    def clear_top(x, carry):
        for member in (VX, VY, VZ, SZZ, SXZ, SYZ):
            for part in range(2):
                top[member, x, part, pl.ds(0, 8), :] = zero_tile
        return carry

    lax.fori_loop(0, top.shape[1], clear_top, 0)

    def remote(source, target, send, recv, device):
        copy = pltpu.make_async_remote_copy(
            src_ref=source,
            dst_ref=target,
            send_sem=send,
            recv_sem=recv,
            device_id=device,
            device_id_type=MESH,
        )
        copy.start()
        return copy

    def send_x(stage, source, start, target, groups, up, down):
        copies = []
        for k, (origin, member, size) in enumerate(groups):
            ids, into = pl.ds(origin, size), pl.ds(member, size)
            copies.append(
                remote(
                    source.at[ids, pl.ds(start + cells_x - up, up), rows if start else pl.ds(0, cells_z)],
                    target.at[into, pl.ds(COL - up, up), rows],
                    x_send.at[stage, k, 0],
                    x_recv.at[stage, k, 0],
                    {"gx": gx_up},
                )
            )
            copies.append(
                remote(
                    source.at[ids, pl.ds(start, down), rows if start else pl.ds(0, cells_z)],
                    target.at[into, pl.ds(COL + cells_x, down), rows],
                    x_send.at[stage, k, 1],
                    x_recv.at[stage, k, 1],
                    {"gx": gx_down},
                )
            )
        return copies

    def send_y(stage):
        return [
            remote(
                edges.at[stage],
                from_low.at[stage],
                y_send.at[stage, 0],
                y_recv.at[stage, 0],
                {"gy": gy_up},
            ),
            remote(
                edges.at[stage],
                from_high.at[stage],
                y_send.at[stage, 1],
                y_recv.at[stage, 1],
                {"gy": gy_down},
            ),
        ]

    leaving = []

    def finish(copies):
        for copy in copies:
            copy.wait_recv()
        leaving.extend(copies)

    def outside_zero_x(ref, members, low, high):
        @pl.when(gx == 0)
        def _():
            for member in members:
                for layer in range(low):
                    ref[member, COL - 1 - layer, rows, :] = jnp.zeros((cells_z, cells_y), F32)

        @pl.when(gx == n_gx - 1)
        def _():
            for member in members:
                for layer in range(high):
                    ref[member, COL + cells_x + layer, rows, :] = jnp.zeros((cells_z, cells_y), F32)

    lane = iota((8, cells_y), 1)
    slot = lane & 3

    def pack(stage, values, cell):
        group = cell // 4
        for k in range(3):
            packed = edges[stage, k, group]
            for z in range(tiles_z):
                place = (cell & 3) * tiles_z + z
                packed = jnp.where(
                    lane >> 2 == place, rolled(values[z][k], (4 * place + 2) & 127), packed
                )
            edges[stage, k, group] = packed

    def prepare(stage, forward):
        for k in range(3):
            for group in range(edges.shape[2]):
                low = jnp.where(gy > 0, from_low[stage, k, group], 0.0)
                high = jnp.where(gy < n_gy - 1, from_high[stage, k, group], 0.0)
                beyond = jnp.where(slot < 2, low, high)
                back_2, back_1 = rolled(beyond, 126), rolled(beyond, 127)
                on_1, on_2 = rolled(beyond, 1), rolled(beyond, 2)
                if forward:
                    value = jnp.where(
                        slot == 0,
                        FAR * back_2,
                        jnp.where(
                            slot == 1,
                            NEAR * back_1 + FAR * back_2,
                            jnp.where(slot == 2, -FAR * on_1, 0.0),
                        ),
                    )
                else:
                    value = jnp.where(
                        slot == 1,
                        FAR * back_1,
                        jnp.where(
                            slot == 2,
                            -NEAR * on_1 - FAR * on_2,
                            jnp.where(slot == 3, -FAR * on_2, 0.0),
                        ),
                    )
                correction[stage, k, group] = value

    at_edge = (lane < 2) | (lane >= cells_y - 2)

    def along_y(ref, members, stage, cell, forward):
        parts = []
        for member in members:
            value = ref[member, cell + COL, rows, :]
            high = value.astype(BF16)
            low = (value - high.astype(F32)).astype(BF16)
            parts.append(jnp.concatenate([high, low], 1))
        both = jnp.dot(
            jnp.concatenate(parts, 0), band[int(forward)], preferred_element_type=F32
        )
        group = cell // 4
        result = []
        for z in range(tiles_z):
            shift = (254 - 4 * ((cell & 3) * tiles_z + z)) & 127
            line = []
            for k in range(3):
                tile = slice(k * cells_z + 8 * z, k * cells_z + 8 * z + 8)
                inside = NEAR * both[tile, 0:128] + FAR * both[tile, 128:256]
                line.append(
                    inside + jnp.where(at_edge, rolled(correction[stage, k, group], shift), 0.0)
                )
            result.append(line)
        return result

    def at(ref, member, x, row):
        return ref[member, x, pl.ds(row, 8), :]

    def along_x(ref, member, x, row, forward):
        shift = 1 if forward else 0
        return stencil(
            at(ref, member, x + shift, row),
            at(ref, member, x + shift - 1, row),
            at(ref, member, x + shift + 1, row),
            at(ref, member, x + shift - 2, row),
        )

    def along_z(ref, member, x, row, forward):
        shift = 1 if forward else 0
        return stencil(
            at(ref, member, x, row + shift),
            at(ref, member, x, row + shift - 1),
            at(ref, member, x, row + shift + 1),
            at(ref, member, x, row + shift - 2),
        )

    def grouped(layer, begin, end):
        odd = (end - begin) % 2
        if odd:
            layer(jnp.int32(begin), 0)

        def pair(i, carry):
            layer(begin + odd + 2 * i, carry)
            layer(begin + odd + 2 * i + 1, carry)
            return carry

        lax.fori_loop(0, (end - begin) // 2, pair, 0)

    def velocity_layers(stage, stress, base, old, new, begin, end, out=None):
        sxx, syy, szz, sxy, sxz, syz = range(base, base + 6)

        def layer(i, carry):
            cell = (i + cells_x - 1) & (cells_x - 1)
            x = cell + COL
            y_all = along_y(stress, (sxy, syy, syz), stage, cell, False)
            results = []
            for z in range(tiles_z):
                row = ROW + 8 * z
                y_of = y_all[z]
                accel = (
                    along_x(stress, sxx, x, row, False) + y_of[0] + along_z(stress, sxz, x, row, False),
                    along_x(stress, sxy, x, row, False) + y_of[1] + along_z(stress, syz, x, row, False),
                    along_x(stress, sxz, x, row, False) + y_of[2] + along_z(stress, szz, x, row, False),
                )
                density = coef[0, cell, pl.ds(8 * z, 8), :]
                after = [at(old, k, x, row) + density * accel[k] for k in range(3)]
                for k in range(3):
                    new[k, x, pl.ds(row, 8), :] = after[k]
                    if out is not None:
                        out[k, cell, pl.ds(8 * z, 8), :] = after[k]
                results.append(after)
            pack(stage + 1, results, cell)
            return carry

        grouped(layer, begin, end)

    def stress_layers(stage, moving, stress, base, new, new_x, new_row, begin, end, packing):
        def layer(i, carry):
            cell = (i + cells_x - 2) & (cells_x - 1)
            x = cell + COL
            y_all = along_y(moving, (0, 1, 2), stage, cell, True)
            results = []
            for z in range(tiles_z):
                row = ROW + 8 * z
                y_of = y_all[z]
                x_of = [along_x(moving, k, x, row, True) for k in range(3)]
                z_of = [along_z(moving, k, x, row, True) for k in range(3)]
                lame = coef[1, cell, pl.ds(8 * z, 8), :]
                shear = coef[2, cell, pl.ds(8 * z, 8), :]
                volume = lame * (x_of[0] + y_of[1] + z_of[2])
                twice = shear + shear
                change = (
                    volume + twice * x_of[0],
                    volume + twice * y_of[1],
                    volume + twice * z_of[2],
                    shear * (y_of[0] + x_of[1]),
                    shear * (z_of[0] + x_of[2]),
                    shear * (z_of[1] + y_of[2]),
                )
                after = [at(stress, base + k, x, row) + change[k] for k in range(6)]
                for k in range(6):
                    new[k, cell + new_x, pl.ds(new_row + 8 * z, 8), :] = after[k]
                results.append((after[3], after[1], after[5]))
            if packing:
                pack(stage + 1, results, cell)
            return carry

        grouped(layer, begin, end)

    stress_groups = ((SXX, SXX, 1), (SXY, SXY, 2))
    inner_groups = ((0, 0, 1), (3, 3, 2))
    move_groups = ((0, 0, 3),)

    fields = top.shape[0]

    def top_own(cell, carry):
        for member in range(fields):
            if member < 9:
                value = at(first, member, cell + COL, ROW)
            else:
                value = coef[member - 9, cell, pl.ds(0, 8), :]
            top[member, cell + LOW, 0, pl.ds(8, 8), :] = value
        return carry

    def pack_rims():
        packed = None
        for slot_id in range(fields * cells_x):
            member, cell = divmod(slot_id, cells_x)
            begin = RIM * (slot_id % SLOTS)
            value = rolled(top[member, cell + LOW, 0, pl.ds(8, 8), :], (begin + LOW) % 128)
            packed = value if begin == 0 else jnp.where(lane < begin, packed, value)
            if slot_id % SLOTS == SLOTS - 1 or slot_id == fields * cells_x - 1:
                rims[slot_id // SLOTS] = packed

    rim_tiles = -(-fields * cells_x // SLOTS)
    corner_tiles = -(-(fields - 2) * cells_x // SLOTS)

    def send_top():
        copies = []
        top_rows = pl.ds(8, 8)
        flow = (
            (first, VX, 3, VX, 3, 3, ROW, COL),
            (first, SXX, 6, SXX, LOW, HIGH, ROW, COL),
            (coef, 0, 3, 9, 3, 3, 0, 0),
        )
        for k, (source, origin, size, member, up, down, row, layer) in enumerate(flow):
            copies.append(
                remote(
                    source.at[pl.ds(origin, size), pl.ds(layer + cells_x - up, up), pl.ds(row, 8)],
                    top.at[pl.ds(member, size), pl.ds(LOW - up, up), 0, top_rows],
                    t_send.at[k],
                    t_recv.at[k],
                    {"gx": gx_up},
                )
            )
            copies.append(
                remote(
                    source.at[pl.ds(origin, size), pl.ds(layer, down), pl.ds(row, 8)],
                    top.at[pl.ds(member, size), pl.ds(LOW + cells_x, down), 0, top_rows],
                    t_send.at[3 + k],
                    t_recv.at[3 + k],
                    {"gx": gx_down},
                )
            )
        for k, (device, row, column, size) in enumerate(
            (
                ({"gx": gx_up, "gy": gy_up}, 0, 0, corner_tiles),
                ({"gx": gx_up, "gy": gy_down}, 0, 1, corner_tiles),
                ({"gx": gx_down, "gy": gy_up}, 2, 0, corner_tiles),
                ({"gx": gx_down, "gy": gy_down}, 2, 1, corner_tiles),
                ({"gy": gy_up}, 1, 0, rim_tiles),
                ({"gy": gy_down}, 1, 1, rim_tiles),
            )
        ):
            copies.append(
                remote(
                    rims.at[pl.ds(0, size)],
                    rims_in.at[row, column, pl.ds(0, size)],
                    t_send.at[6 + k],
                    t_recv.at[6 + k],
                    device,
                )
            )
        return copies

    def unpack_rims():
        spot = lane - RIM * ((lane * 57) >> 9)
        near = (lane < HIGH) | (lane >= 128 - LOW)

        for row, tiles, members, cells, shown in (
            (1, rim_tiles, fields, range(cells_x), True),
            (0, corner_tiles, fields - 2, range(cells_x - LOW, cells_x), gx > 0),
            (2, corner_tiles, fields - 2, range(HIGH), gx < n_gx - 1),
        ):
            both = []
            for tile in range(tiles):
                low = jnp.where(shown & (gy > 0), rims_in[row, 0, tile], 0.0)
                high = jnp.where(shown & (gy < n_gy - 1), rims_in[row, 1, tile], 0.0)
                both.append(jnp.where(spot < LOW, low, high))
            for cell in cells:
                x = cell + LOW + (row - 1) * cells_x
                for member in range(fields):
                    if member < members:
                        slot_id = member * cells_x + cell
                        begin = RIM * (slot_id % SLOTS)
                        value = rolled(both[slot_id // SLOTS], (256 - LOW - begin) % 128)
                        value = jnp.where(near, value, 0.0)
                    else:
                        value = zero_tile
                    top[member, x, 1, pl.ds(8, 8), :] = value

        def outside(x, carry):
            for member in range(fields):
                top[member, x, 0, pl.ds(8, 8), :] = zero_tile
            return carry

        @pl.when(gx == 0)
        def _():
            lax.fori_loop(0, LOW, outside, 0)

        @pl.when(gx == n_gx - 1)
        def _():
            lax.fori_loop(LOW + cells_x, LOW + cells_x + HIGH, outside, 0)

    def top_at(member, x, part, row=8):
        return top[member, x, part, pl.ds(row, 8), :]

    def top_along_y(member, x, forward):
        parts = [top_at(member, x, 0), top_at(member, x, 1)]

        def moved(shift):
            mine, other = [rolled(part, shift & 127) for part in parts]
            across = lane < shift if shift > 0 else lane >= 128 + shift
            return jnp.where(across, other, mine), jnp.where(across, mine, other)

        if forward:
            terms = (moved(-1), parts, moved(-2), moved(1))
        else:
            terms = (parts, moved(1), moved(-1), moved(2))
        return [stencil(*(term[part] for term in terms)) for part in range(2)]

    def top_along_x(member, x, part, shift):
        return stencil(
            top_at(member, x + shift, part),
            top_at(member, x + shift - 1, part),
            top_at(member, x + shift + 1, part),
            top_at(member, x + shift - 2, part),
        )

    def top_along_z(member, x, part, shift):
        return stencil(
            top_at(member, x, part, 8 + shift),
            top_at(member, x, part, 7 + shift),
            top_at(member, x, part, 9 + shift),
            top_at(member, x, part, 6 + shift),
        )

    def top_velocity(x, parts):
        y_of = [top_along_y(member, x, False) for member in (SXY, SYY, SYZ)]
        for part in range(parts):
            accel = (
                top_along_x(SXX, x, part, 0) + y_of[0][part] + top_along_z(SXZ, x, part, 0),
                top_along_x(SXY, x, part, 0) + y_of[1][part] + top_along_z(SYZ, x, part, 0),
                top_along_x(SXZ, x, part, 0) + y_of[2][part] + top_along_z(SZZ, x, part, 0),
            )
            for k in range(3):
                top[k, x, part, pl.ds(8, 8), :] = (
                    top_at(k, x, part) + top_at(9, x, part) * accel[k]
                )

    def top_stress(x):
        y_of = [top_along_y(member, x, True) for member in range(3)]
        for part in range(2):
            x_of = [top_along_x(member, x, part, 1) for member in range(3)]
            z_of = [top_along_z(member, x, part, 1) for member in range(3)]
            shear = top_at(11, x, part)
            volume = top_at(10, x, part) * (x_of[0] + y_of[1][part] + z_of[2])
            twice = shear + shear
            change = (
                volume + twice * x_of[0],
                volume + twice * y_of[1][part],
                volume + twice * z_of[2],
                shear * (y_of[0][part] + x_of[1]),
                shear * (z_of[0] + x_of[2]),
                shear * (z_of[1] + y_of[2][part]),
            )
            for k in range(6):
                top[SXX + k, x, part, pl.ds(8, 8), :] = top_at(SXX + k, x, part) + change[k]

    def top_layers(update, begin, size, groups, *more):
        def layers(i, carry):
            for k in range(size):
                update(begin + i * size + k, *more)
            return carry

        lax.fori_loop(0, groups, layers, 0)

    load_stress.wait()

    edges[...] = jnp.zeros(edges.shape, F32)

    def pack_first(cell, carry):
        values = [
            [at(first, k, cell + COL, ROW + 8 * z) for k in (SXY, SYY, SYZ)] for z in range(tiles_z)
        ]
        pack(0, values, cell)
        return carry

    lax.fori_loop(0, cells_x, pack_first, 0)

    load_material.wait()

    def widen(cell, carry):
        for k in range(3):
            coef[k, cell] = TIME_SOIL * raw[k, cell].astype(F32)
        return carry

    lax.fori_loop(0, cells_x, widen, 0)
    load_velocity.wait()
    source = iota((256, 256), 0) & 127
    column = iota((256, 256), 1)
    wanted = column & 127
    for forward in range(2):
        reach = jnp.where(column < 128, 0, 1)
        plus = source == wanted + forward + reach
        minus = source == wanted + forward - 1 - reach
        band[forward] = jnp.where(plus, 1.0, jnp.where(minus, -1.0, 0.0)).astype(BF16)


    for copy in load_small:
        copy.wait()
    big = (128, 128)
    big_lane = iota(big, 1)
    big_lane_f = big_lane.astype(F32)
    small_row = iota((8, 128), 0)
    small_lane = iota((8, 128), 1)

    for b in range(buildings):
        for h in range(2):
            piece = pl.ds(b * 256 + h * 128, 128)
            live = iota((1, 128), 1) + h * 128 < count[b]
            for end in range(2):
                nodes = links[pl.ds(end, 1), piece]
                index[b, h * 2 + end] = jnp.broadcast_to(nodes, (8, 128))
                kept = jnp.where(live, nodes, -1).astype(F32)
                columns = jnp.broadcast_to(kept, big).T
                spread[b, pl.ds(h * 128, 128), pl.ds(end * 128, 128)] = (
                    jnp.where(columns == big_lane_f, 1.0, 0.0).astype(BF16)
                )

    group_of = (iota((n_dev, 128), 1) // 2) % GROUPS
    holder = iota((n_dev, 128), 0)
    for j in range(1, GROUPS):
        entries = table[pl.ds(j - 1, 1), :].astype(F32)
        columns = jnp.broadcast_to(entries, (128, n_dev)).T.astype(jnp.int32)
        holder = jnp.where(group_of == j, columns, holder)
    owners[...] = holder

    bid = jnp.zeros((16, 128), F32)
    for b in range(buildings):
        cell = foot[pl.ds(b, 1), :]
        place_x = jnp.where(iota((16, 128), 0) == cell // cells_y, float(b), 0.0).astype(BF16)
        place_y = jnp.where(iota(big, 0) == cell % cells_y, 1.0, 0.0).astype(BF16)
        bid += lax.dot_general(
            place_x, place_y, (((1,), (1,)), ((), ())), preferred_element_type=F32
        )
    bids[...] = bid[0:8].astype(jnp.int32)

    blank = jnp.zeros((2, 128), F32)
    for b in range(buildings):
        piece = pl.ds(b * 128, 128)
        disp[b] = jnp.concatenate([frame_disp[:, piece], blank], 0)
        vel[b] = jnp.concatenate([frame_vel[:, piece], blank], 0)
        imass[b] = TIME_FRAME * jnp.concatenate([inverse_mass[:, piece], blank], 0)
        foot_sum[b] = jnp.zeros((8, 128), F32)

    load_matrix.wait()

    def internal_forces(b):
        place = disp[b]
        forces = []
        for h in range(2):
            ends = (
                lane_gather(place, index[b, h * 2]),
                lane_gather(place, index[b, h * 2 + 1]),
            )
            piece = pl.ds(b * 256 + h * 128, 128)
            total = None
            for a in range(12):
                row = ends[a // 6][a % 6 : a % 6 + 1, :]
                term = matrix[a, :, piece] * row
                total = term if total is None else total + term
            forces.append(jnp.concatenate([total, jnp.zeros((4, 128), F32)], 0))
        forces = jnp.concatenate(forces, 1)
        high = forces.astype(BF16)
        low = (forces - high.astype(F32)).astype(BF16)
        parts = jnp.dot(
            jnp.concatenate([high, low], 0), spread[b], preferred_element_type=F32
        )
        parts = parts[0:16] + parts[16:32]
        internal[b] = parts[0:8, 0:128] + parts[6:14, 128:256]

    def advance(b):
        speed = vel[b]
        loads = damp_vec[0, b] - damp_vec[1, b] * speed - internal[b]
        speed = speed + imass[b] * loads
        vel[b] = speed
        disp[b] = disp[b] + TIME_FRAME * speed
        foot_sum[b] += speed

    for b in range(buildings):
        internal_forces(b)

    lax.fori_loop(0, cells_x, top_own, 0)
    pack_rims()
    pl.semaphore_wait(barrier, n_gx + n_gy + 2)
    sent_y = send_y(0)
    sent_top = send_top()
    sent_x = send_x(0, soil, 0, first, stress_groups, 2, 1)

    finish(sent_y)
    prepare(0, False)
    velocity_layers(0, first, SXX, first, vel_a, 3, cells_x)

    finish(sent_top)
    unpack_rims()
    top_layers(top_velocity, LOW - 3, 7, (cells_x + 6) // 7, 2)
    top_layers(top_stress, LOW - 2, 4, (cells_x + 4) // 4)
    top_layers(top_velocity, LOW, 4, cells_x // 4, 1)

    surface = [top[k, pl.ds(LOW, cells_x), 0, 8, :] for k in range(3)]
    dash = dashpot[...]
    terms = [dash * surface[0], dash * surface[1], dash * surface[2], dash]
    bid = bids[...]
    sums = [
        jnp.sum(jnp.where(bid == b, term, 0.0), axis=0, keepdims=True)
        for term in terms
        for b in range(buildings)
    ]
    sums = jnp.concatenate(sums + [jnp.zeros((128 - len(sums), 128), F32)], 0)
    mine = jnp.sum(sums.T, axis=0, keepdims=True)

    def far_first(count, ring):
        outer = count // ring

        def hops(k):
            return min(k // ring, outer - k // ring) + (min(k % ring, ring - k % ring) if ring > 2 else 0)

        return sorted(range(1, count), key=lambda k: -hops(k))

    def gather_along_gy(turn, value):
        row_buf[turn, gy] = value
        return [
            remote(
                row_buf.at[turn, gy],
                row_buf.at[turn, gy],
                a_send.at[turn, k - 1],
                a_recv.at[turn, k - 1],
                {"gy": lax.rem(gy + k, n_gy)},
            )
            for k in far_first(n_gy, 4)
        ]

    def gather_along_gx(turn):
        rows_all[turn, gx] = row_buf[turn].reshape(n_gy, 128)
        return [
            remote(
                rows_all.at[turn, gx],
                rows_all.at[turn, gx],
                b_send.at[turn, k - 1],
                b_recv.at[turn, k - 1],
                {"gx": lax.rem(gx + k, n_gx)},
            )
            for k in far_first(n_gx, 2)
        ]

    gathering = gather_along_gy(0, mine)

    finish(sent_x)
    outside_zero_x(first, (SXX, SXY, SXZ), 2, 1)
    velocity_layers(0, first, SXX, first, vel_a, 0, 3)
    sent = send_x(1, vel_a, COL, vel_a, move_groups, 1, 2)
    sent += send_y(1)

    finish(gathering)
    gathering = gather_along_gx(0)

    finish(sent)
    outside_zero_x(vel_a, (0, 1, 2), 1, 2)
    prepare(1, True)

    stress_layers(1, vel_a, first, SXX, str_a, COL, ROW, 0, 3, True)
    sent = send_x(2, str_a, COL, str_a, inner_groups, 2, 1)
    stress_layers(1, vel_a, first, SXX, str_a, COL, ROW, 3, cells_x, True)
    sent += send_y(2)
    finish(gathering)
    arrived = rows_all[0].reshape(n_dev, 128)
    owned = jnp.sum(jnp.where(owners[...] == me, arrived, 0.0), axis=0, keepdims=True)
    owned = jnp.broadcast_to(owned, (8, 128))

    at_footing = (small_row < 3) & (small_lane == 0)
    drives, dampers = [], []
    for b in range(buildings):
        pick = jnp.minimum(small_row * buildings + b, 127)
        drives.append(jnp.where(at_footing, lane_gather(owned, pick), 0.0))
        pick = jnp.full((8, 128), 3 * buildings + b, jnp.int32)
        dampers.append(jnp.where(at_footing, lane_gather(owned, pick), 0.0))
    for b in range(buildings):
        damp_vec[0, b] = drives[b]
        damp_vec[1, b] = dampers[b]

    def frame_step(step, carry):
        for b in range(buildings):
            advance(b)
            internal_forces(b)
        return carry

    lax.fori_loop(0, FRAME_STEPS - 1, frame_step, 0)
    for b in range(buildings):
        advance(b)

    back = jnp.zeros((8, 128), F32)
    for b in range(buildings):
        whole = jnp.broadcast_to(foot_sum[b][:, 0:1], (8, 128))
        back = jnp.where(small_lane == small_row * buildings + b, whole, back)
    back = jnp.where(small_row < 3, back, 0.0)
    gathering = gather_along_gy(1, jnp.sum(back, axis=0, keepdims=True))

    finish(sent)
    outside_zero_x(str_a, (0, 3, 4), 2, 1)
    prepare(2, False)

    velocity_layers(2, str_a, 0, vel_a, vel_b, 0, 3, moved_out)
    sent_x = send_x(3, vel_b, COL, vel_b, move_groups, 1, 2)
    velocity_layers(2, str_a, 0, vel_a, vel_b, 3, cells_x, moved_out)
    sent_y = send_y(3)

    for b in range(buildings):
        piece = pl.ds(b * 128, 128)
        disp_out[:, piece] = disp[b][0:6]
        vel_out[:, piece] = vel[b][0:6]
    finish(gathering)
    gathering = gather_along_gx(1)

    finish(sent_y)
    prepare(3, True)
    stress_layers(3, vel_b, str_a, 0, str_b, 0, 0, 3, cells_x, False)
    finish(sent_x)
    outside_zero_x(vel_b, (0, 1, 2), 1, 2)
    stress_layers(3, vel_b, str_a, 0, str_b, 0, 0, 0, 3, False)

    wanted = owners[pl.ds(me, 1), :]
    finish(gathering)
    arrived = rows_all[1].reshape(n_dev, 128)
    held = jnp.where(iota((n_dev, 128), 0) == wanted, arrived, 0.0)
    held = jnp.broadcast_to(jnp.sum(held, axis=0, keepdims=True), (8, 128))
    for k in range(3):
        total = lane_gather(held, bid + k * buildings)
        force_out[k] = dash * (FRAME_STEPS * surface[k] - total)

    for copy in leaving:
        copy.wait_send()


def write_out(moved, stress, force, disp, vel, soil_out, force_out, disp_out, vel_out, sem):
    copies = [
        pltpu.make_async_copy(source, target, sem.at[k])
        for k, (source, target) in enumerate(
            (
                (stress, soil_out.at[pl.ds(3, 6)]),
                (moved, soil_out.at[pl.ds(0, 3)]),
                (force, force_out),
                (disp, disp_out),
                (vel, vel_out),
            )
        )
    ]
    for copy in copies:
        copy.start()
    for copy in copies:
        copy.wait()


def shards(n_gx, n_gy, *args):
    soil, material, dashpot, foot, table, stiff, links = args[:7]
    cells_x, cells_z, cells_y = soil.shape[1:]
    buildings = foot.shape[0]
    wide = (cells_x + 2 * COL, cells_z + 2 * ROW, cells_y)
    n_dev = n_gx * n_gy
    anywhere = pl.BlockSpec(memory_space=pl.ANY)
    vmem = pl.BlockSpec(memory_space=pltpu.VMEM)
    dma = pltpu.SemaphoreType.DMA
    limit = 40 * 1024 * 1024
    kept = (
        pltpu.VMEM((3, cells_x, cells_z, cells_y), F32),
        pltpu.VMEM((6, cells_x, cells_z, cells_y), F32),
        pltpu.VMEM((3, cells_x, cells_y), F32),
        pltpu.VMEM(args[9].shape, F32),
        pltpu.VMEM(args[10].shape, F32),
    )
    results = pl.pallas_call(
        functools.partial(kernel, n_gx, n_gy),
        out_shape=kept,
        in_specs=[pl.BlockSpec(memory_space=pltpu.HBM)] * len(args),
        out_specs=(vmem,) * len(kept),
        scratch_shapes=[
            pltpu.VMEM((9,) + wide, F32),
            pltpu.VMEM((3,) + wide, F32),
            pltpu.VMEM((6,) + wide, F32),
            pltpu.VMEM((3,) + wide, F32),
            pltpu.VMEM(material.shape, BF16),
            pltpu.VMEM(material.shape, F32),
            pltpu.VMEM(stiff.shape, F32),
            pltpu.VMEM(dashpot.shape, F32),
            pltpu.VMEM(foot.shape, jnp.int32),
            pltpu.VMEM(table.shape, jnp.int32),
            pltpu.VMEM(links.shape, jnp.int32),
            pltpu.SMEM(args[7].shape, jnp.int32),
            pltpu.VMEM(args[8].shape, F32),
            pltpu.VMEM(args[9].shape, F32),
            pltpu.VMEM(args[10].shape, F32),
            pltpu.VMEM((buildings, 256, 256), BF16),
            pltpu.VMEM((2, 256, 256), BF16),
            pltpu.VMEM((4, 3, cells_x // 4, 8, 128), F32),
            pltpu.VMEM((4, 3, cells_x // 4, 8, 128), F32),
            pltpu.VMEM((4, 3, cells_x // 4, 8, 128), F32),
            pltpu.VMEM((4, 3, cells_x // 4, 8, 128), F32),
            pltpu.VMEM((12, cells_x + LOW + HIGH, 2, 24, 128), F32),
            pltpu.VMEM((-(-12 * cells_x // SLOTS), 8, 128), F32),
            pltpu.VMEM((3, 2, -(-12 * cells_x // SLOTS), 8, 128), F32),
            pltpu.VMEM((n_dev, 128), jnp.int32),
            pltpu.VMEM((8, 128), jnp.int32),
            pltpu.VMEM((2, buildings, 8, 128), F32),
            pltpu.VMEM((buildings, 8, 128), F32),
            pltpu.VMEM((buildings, 8, 128), F32),
            pltpu.VMEM((buildings, 8, 128), F32),
            pltpu.VMEM((buildings, 8, 128), F32),
            pltpu.VMEM((buildings, 8, 128), F32),
            pltpu.VMEM((buildings, 4, 8, 128), jnp.int32),
            pltpu.VMEM((2, n_gy, 1, 128), F32),
            pltpu.VMEM((2, n_gx, n_gy, 128), F32),
            dma((12,)),
            dma((4, 2, 2)),
            dma((4, 2, 2)),
            dma((4, 2)),
            dma((4, 2)),
            dma((2, n_gy - 1)),
            dma((2, n_gy - 1)),
            dma((2, n_gx - 1)),
            dma((2, n_gx - 1)),
            dma((12,)),
            dma((12,)),
        ],
        compiler_params=pltpu.CompilerParams(
            collective_id=0, has_side_effects=True, vmem_limit_bytes=limit
        ),
    )(*(pltpu.with_memory_space_constraint(value, pltpu.HBM) for value in args))
    return pl.pallas_call(
        write_out,
        out_shape=(
            jax.ShapeDtypeStruct(soil.shape, F32),
            jax.ShapeDtypeStruct((3, cells_x, cells_y), F32),
            jax.ShapeDtypeStruct(args[9].shape, F32),
            jax.ShapeDtypeStruct(args[10].shape, F32),
        ),
        in_specs=[vmem] * len(kept),
        out_specs=(anywhere,) * 4,
        scratch_shapes=[dma((len(kept),))],
        compiler_params=pltpu.CompilerParams(vmem_limit_bytes=limit),
    )(*results)


def solution(mesh):
    placed = (
        P(None, "gx", None, "gy"),
        P(None, "gx", None, "gy"),
        P("gx", "gy"),
        P(("gx", "gy"), None),
        P(),
        P(None, None, ("gx", "gy")),
        P(None, ("gx", "gy")),
        P(("gx", "gy")),
        P(None, ("gx", "gy")),
        P(None, ("gx", "gy")),
        P(None, ("gx", "gy")),
    )
    return jax.shard_map(
        functools.partial(shards, mesh.shape["gx"], mesh.shape["gy"]),
        mesh=mesh,
        in_specs=placed,
        out_specs=(
            P(None, "gx", None, "gy"),
            P(None, "gx", "gy"),
            P(None, ("gx", "gy")),
            P(None, ("gx", "gy")),
        ),
        check_vma=False,
    )
```

```python
import functools

import jax
import jax.numpy as jnp
from jax import lax
from jax.experimental import pallas as pl
from jax.experimental.pallas import tpu as pltpu
from jax.sharding import PartitionSpec as P

GROUPS = 4
FRAME_STEPS = 4
NEAR = 9.0 / 8.0
FAR = -1.0 / 24.0
TIME_SOIL = 0.18
TIME_FRAME = 0.05
MESH = pl.DeviceIdType.MESH
ROW = 8
COL = 2
LOW, HIGH = 5, 4
RIM = LOW + HIGH
SLOTS = 128 // RIM
F32 = jnp.float32
BF16 = jnp.bfloat16

VX, VY, VZ, SXX, SYY, SZZ, SXY, SXZ, SYZ = range(9)


def lane_gather(values, index):
    return lax.gather(
        values,
        index[:, :, None],
        lax.GatherDimensionNumbers(
            offset_dims=(),
            collapsed_slice_dims=(1,),
            start_index_map=(1,),
            operand_batching_dims=(0,),
            start_indices_batching_dims=(0,),
        ),
        (1, 1),
        mode=lax.GatherScatterMode.PROMISE_IN_BOUNDS,
    )


def iota(shape, dim):
    return lax.broadcasted_iota(jnp.int32, shape, dim)


def stencil(near_high, near_low, far_high, far_low):
    return NEAR * (near_high - near_low) + FAR * (far_high - far_low)


def rolled(value, shift):
    return pltpu.roll(value, shift, 1)


def kernel(
    n_gx,
    n_gy,
    soil,
    material,
    hbm_dashpot,
    hbm_foot,
    hbm_table,
    stiff,
    hbm_links,
    hbm_count,
    hbm_inverse_mass,
    hbm_frame_disp,
    hbm_frame_vel,
    moved_out,
    str_b,
    force_out,
    disp_out,
    vel_out,
    first,
    vel_a,
    str_a,
    vel_b,
    raw,
    coef,
    matrix,
    dashpot,
    foot,
    table,
    links,
    count,
    inverse_mass,
    frame_disp,
    frame_vel,
    spread,
    band,
    edges,
    from_low,
    from_high,
    correction,
    top,
    rims,
    rims_in,
    owners,
    bids,
    damp_vec,
    disp,
    vel,
    imass,
    foot_sum,
    internal,
    index,
    row_buf,
    rows_all,
    load_sem,
    x_send,
    x_recv,
    y_send,
    y_recv,
    a_send,
    a_recv,
    b_send,
    b_recv,
    t_send,
    t_recv,
):
    gx = lax.axis_index("gx")
    gy = lax.axis_index("gy")
    me = gx * n_gy + gy
    n_dev = n_gx * n_gy
    gx_up, gx_down = lax.rem(gx + 1, n_gx), lax.rem(gx + n_gx - 1, n_gx)
    gy_up, gy_down = lax.rem(gy + 1, n_gy), lax.rem(gy + n_gy - 1, n_gy)
    cells_x, cells_z, cells_y = soil.shape[1:]
    tiles_z = cells_z // 8
    buildings = foot.shape[0]
    inner = pl.ds(COL, cells_x)
    rows = pl.ds(ROW, cells_z)

    def load(k, source, target):
        copy = pltpu.make_async_copy(source, target, load_sem.at[k])
        copy.start()
        return copy

    load_stress = load(0, soil.at[pl.ds(SXX, 6)], first.at[pl.ds(SXX, 6), inner, rows])
    load_velocity = load(1, soil.at[pl.ds(0, 3)], first.at[pl.ds(0, 3), inner, rows])
    load_material = load(2, material, raw)
    load_small = [
        load(4 + k, source, target)
        for k, (source, target) in enumerate(
            (
                (hbm_dashpot, dashpot),
                (hbm_foot, foot),
                (hbm_table, table),
                (hbm_links, links),
                (hbm_count, count),
                (hbm_inverse_mass, inverse_mass),
                (hbm_frame_disp, frame_disp),
                (hbm_frame_vel, frame_vel),
            )
        )
    ]
    load_matrix = load(3, stiff, matrix)

    barrier = pltpu.get_barrier_semaphore()
    for k in range(1, n_gx):
        pl.semaphore_signal(
            barrier, inc=1, device_id={"gx": lax.rem(gx + k, n_gx)}, device_id_type=MESH
        )
    for k in range(1, n_gy):
        pl.semaphore_signal(
            barrier, inc=1, device_id={"gy": lax.rem(gy + k, n_gy)}, device_id_type=MESH
        )

    corners = [
        {"gx": row, "gy": column} for row in (gx_down, gx_up) for column in (gy_down, gy_up)
    ]
    for device in corners:
        pl.semaphore_signal(barrier, inc=1, device_id=device, device_id_type=MESH)

    zero_tile = jnp.zeros((8, cells_y), F32)

    def clear(x, carry):
        for ref, members in (
            (first, (SZZ, SXZ, SYZ)),
            (vel_a, (0, 1, 2)),
            (str_a, (2, 4, 5)),
            (vel_b, (0, 1, 2)),
        ):
            for member in members:
                ref[member, x, pl.ds(0, 8), :] = zero_tile
                ref[member, x, pl.ds(ROW + cells_z, 8), :] = zero_tile
        return carry

    lax.fori_loop(COL, COL + cells_x, clear, 0)

    def clear_top(x, carry):
        for member in (VX, VY, VZ, SZZ, SXZ, SYZ):
            for part in range(2):
                top[member, x, part, pl.ds(0, 8), :] = zero_tile
        return carry

    lax.fori_loop(0, top.shape[1], clear_top, 0)

    def remote(source, target, send, recv, device):
        copy = pltpu.make_async_remote_copy(
            src_ref=source,
            dst_ref=target,
            send_sem=send,
            recv_sem=recv,
            device_id=device,
            device_id_type=MESH,
        )
        copy.start()
        return copy

    def send_x(stage, source, start, target, groups, up, down):
        copies = []
        for k, (origin, member, size) in enumerate(groups):
            ids, into = pl.ds(origin, size), pl.ds(member, size)
            copies.append(
                remote(
                    source.at[ids, pl.ds(start + cells_x - up, up), rows if start else pl.ds(0, cells_z)],
                    target.at[into, pl.ds(COL - up, up), rows],
                    x_send.at[stage, k, 0],
                    x_recv.at[stage, k, 0],
                    {"gx": gx_up},
                )
            )
            copies.append(
                remote(
                    source.at[ids, pl.ds(start, down), rows if start else pl.ds(0, cells_z)],
                    target.at[into, pl.ds(COL + cells_x, down), rows],
                    x_send.at[stage, k, 1],
                    x_recv.at[stage, k, 1],
                    {"gx": gx_down},
                )
            )
        return copies

    def send_y(stage):
        return [
            remote(
                edges.at[stage],
                from_low.at[stage],
                y_send.at[stage, 0],
                y_recv.at[stage, 0],
                {"gy": gy_up},
            ),
            remote(
                edges.at[stage],
                from_high.at[stage],
                y_send.at[stage, 1],
                y_recv.at[stage, 1],
                {"gy": gy_down},
            ),
        ]

    leaving = []

    def finish(copies):
        for copy in copies:
            copy.wait_recv()
        leaving.extend(copies)

    def outside_zero_x(ref, members, low, high):
        @pl.when(gx == 0)
        def _():
            for member in members:
                for layer in range(low):
                    ref[member, COL - 1 - layer, rows, :] = jnp.zeros((cells_z, cells_y), F32)

        @pl.when(gx == n_gx - 1)
        def _():
            for member in members:
                for layer in range(high):
                    ref[member, COL + cells_x + layer, rows, :] = jnp.zeros((cells_z, cells_y), F32)

    lane = iota((8, cells_y), 1)
    slot = lane & 3

    def pack(stage, values, cell):
        group = cell // 4
        for k in range(3):
            packed = edges[stage, k, group]
            for z in range(tiles_z):
                place = (cell & 3) * tiles_z + z
                packed = jnp.where(
                    lane >> 2 == place, rolled(values[z][k], (4 * place + 2) & 127), packed
                )
            edges[stage, k, group] = packed

    def prepare(stage, forward):
        for k in range(3):
            for group in range(edges.shape[2]):
                low = jnp.where(gy > 0, from_low[stage, k, group], 0.0)
                high = jnp.where(gy < n_gy - 1, from_high[stage, k, group], 0.0)
                beyond = jnp.where(slot < 2, low, high)
                back_2, back_1 = rolled(beyond, 126), rolled(beyond, 127)
                on_1, on_2 = rolled(beyond, 1), rolled(beyond, 2)
                if forward:
                    value = jnp.where(
                        slot == 0,
                        FAR * back_2,
                        jnp.where(
                            slot == 1,
                            NEAR * back_1 + FAR * back_2,
                            jnp.where(slot == 2, -FAR * on_1, 0.0),
                        ),
                    )
                else:
                    value = jnp.where(
                        slot == 1,
                        FAR * back_1,
                        jnp.where(
                            slot == 2,
                            -NEAR * on_1 - FAR * on_2,
                            jnp.where(slot == 3, -FAR * on_2, 0.0),
                        ),
                    )
                correction[stage, k, group] = value

    at_edge = (lane < 2) | (lane >= cells_y - 2)

    def along_y(ref, members, stage, cell, forward):
        parts = []
        for member in members:
            value = ref[member, cell + COL, rows, :]
            high = value.astype(BF16)
            low = (value - high.astype(F32)).astype(BF16)
            parts.append(jnp.concatenate([high, low], 1))
        both = jnp.dot(
            jnp.concatenate(parts, 0), band[int(forward)], preferred_element_type=F32
        )
        group = cell // 4
        result = []
        for z in range(tiles_z):
            shift = (254 - 4 * ((cell & 3) * tiles_z + z)) & 127
            line = []
            for k in range(3):
                tile = slice(k * cells_z + 8 * z, k * cells_z + 8 * z + 8)
                inside = NEAR * both[tile, 0:128] + FAR * both[tile, 128:256]
                line.append(
                    inside + jnp.where(at_edge, rolled(correction[stage, k, group], shift), 0.0)
                )
            result.append(line)
        return result

    def at(ref, member, x, row):
        return ref[member, x, pl.ds(row, 8), :]

    def along_x(ref, member, x, row, forward):
        shift = 1 if forward else 0
        return stencil(
            at(ref, member, x + shift, row),
            at(ref, member, x + shift - 1, row),
            at(ref, member, x + shift + 1, row),
            at(ref, member, x + shift - 2, row),
        )

    def along_z(ref, member, x, row, forward):
        shift = 1 if forward else 0
        return stencil(
            at(ref, member, x, row + shift),
            at(ref, member, x, row + shift - 1),
            at(ref, member, x, row + shift + 1),
            at(ref, member, x, row + shift - 2),
        )

    def grouped(layer, begin, end):
        odd = (end - begin) % 2
        if odd:
            layer(jnp.int32(begin), 0)

        def pair(i, carry):
            layer(begin + odd + 2 * i, carry)
            layer(begin + odd + 2 * i + 1, carry)
            return carry

        lax.fori_loop(0, (end - begin) // 2, pair, 0)

    def velocity_layers(stage, stress, base, old, new, begin, end, out=None):
        sxx, syy, szz, sxy, sxz, syz = range(base, base + 6)

        def layer(i, carry):
            cell = (i + cells_x - 1) & (cells_x - 1)
            x = cell + COL
            y_all = along_y(stress, (sxy, syy, syz), stage, cell, False)
            results = []
            for z in range(tiles_z):
                row = ROW + 8 * z
                y_of = y_all[z]
                accel = (
                    along_x(stress, sxx, x, row, False) + y_of[0] + along_z(stress, sxz, x, row, False),
                    along_x(stress, sxy, x, row, False) + y_of[1] + along_z(stress, syz, x, row, False),
                    along_x(stress, sxz, x, row, False) + y_of[2] + along_z(stress, szz, x, row, False),
                )
                density = coef[0, cell, pl.ds(8 * z, 8), :]
                after = [at(old, k, x, row) + density * accel[k] for k in range(3)]
                for k in range(3):
                    new[k, x, pl.ds(row, 8), :] = after[k]
                    if out is not None:
                        out[k, cell, pl.ds(8 * z, 8), :] = after[k]
                results.append(after)
            pack(stage + 1, results, cell)
            return carry

        grouped(layer, begin, end)

    def stress_layers(stage, moving, stress, base, new, new_x, new_row, begin, end, packing):
        def layer(i, carry):
            cell = (i + cells_x - 2) & (cells_x - 1)
            x = cell + COL
            y_all = along_y(moving, (0, 1, 2), stage, cell, True)
            results = []
            for z in range(tiles_z):
                row = ROW + 8 * z
                y_of = y_all[z]
                x_of = [along_x(moving, k, x, row, True) for k in range(3)]
                z_of = [along_z(moving, k, x, row, True) for k in range(3)]
                lame = coef[1, cell, pl.ds(8 * z, 8), :]
                shear = coef[2, cell, pl.ds(8 * z, 8), :]
                volume = lame * (x_of[0] + y_of[1] + z_of[2])
                twice = shear + shear
                change = (
                    volume + twice * x_of[0],
                    volume + twice * y_of[1],
                    volume + twice * z_of[2],
                    shear * (y_of[0] + x_of[1]),
                    shear * (z_of[0] + x_of[2]),
                    shear * (z_of[1] + y_of[2]),
                )
                after = [at(stress, base + k, x, row) + change[k] for k in range(6)]
                for k in range(6):
                    new[k, cell + new_x, pl.ds(new_row + 8 * z, 8), :] = after[k]
                results.append((after[3], after[1], after[5]))
            if packing:
                pack(stage + 1, results, cell)
            return carry

        grouped(layer, begin, end)

    stress_groups = ((SXX, SXX, 1), (SXY, SXY, 2))
    inner_groups = ((0, 0, 1), (3, 3, 2))
    move_groups = ((0, 0, 3),)

    fields = top.shape[0]

    def top_own(cell, carry):
        for member in range(fields):
            if member < 9:
                value = at(first, member, cell + COL, ROW)
            else:
                value = coef[member - 9, cell, pl.ds(0, 8), :]
            top[member, cell + LOW, 0, pl.ds(8, 8), :] = value
        return carry

    def pack_rims():
        packed = None
        for slot_id in range(fields * cells_x):
            member, cell = divmod(slot_id, cells_x)
            begin = RIM * (slot_id % SLOTS)
            value = rolled(top[member, cell + LOW, 0, pl.ds(8, 8), :], (begin + LOW) % 128)
            packed = value if begin == 0 else jnp.where(lane < begin, packed, value)
            if slot_id % SLOTS == SLOTS - 1 or slot_id == fields * cells_x - 1:
                rims[slot_id // SLOTS] = packed

    rim_tiles = -(-fields * cells_x // SLOTS)
    corner_tiles = -(-(fields - 2) * cells_x // SLOTS)

    def send_top():
        copies = []
        top_rows = pl.ds(8, 8)
        flow = (
            (first, VX, 3, VX, 3, 3, ROW, COL),
            (first, SXX, 6, SXX, LOW, HIGH, ROW, COL),
            (coef, 0, 3, 9, 3, 3, 0, 0),
        )
        for k, (source, origin, size, member, up, down, row, layer) in enumerate(flow):
            copies.append(
                remote(
                    source.at[pl.ds(origin, size), pl.ds(layer + cells_x - up, up), pl.ds(row, 8)],
                    top.at[pl.ds(member, size), pl.ds(LOW - up, up), 0, top_rows],
                    t_send.at[k],
                    t_recv.at[k],
                    {"gx": gx_up},
                )
            )
            copies.append(
                remote(
                    source.at[pl.ds(origin, size), pl.ds(layer, down), pl.ds(row, 8)],
                    top.at[pl.ds(member, size), pl.ds(LOW + cells_x, down), 0, top_rows],
                    t_send.at[3 + k],
                    t_recv.at[3 + k],
                    {"gx": gx_down},
                )
            )
        for k, (device, row, column, size) in enumerate(
            (
                ({"gx": gx_up, "gy": gy_up}, 0, 0, corner_tiles),
                ({"gx": gx_up, "gy": gy_down}, 0, 1, corner_tiles),
                ({"gx": gx_down, "gy": gy_up}, 2, 0, corner_tiles),
                ({"gx": gx_down, "gy": gy_down}, 2, 1, corner_tiles),
                ({"gy": gy_up}, 1, 0, rim_tiles),
                ({"gy": gy_down}, 1, 1, rim_tiles),
            )
        ):
            copies.append(
                remote(
                    rims.at[pl.ds(0, size)],
                    rims_in.at[row, column, pl.ds(0, size)],
                    t_send.at[6 + k],
                    t_recv.at[6 + k],
                    device,
                )
            )
        return copies

    def unpack_rims():
        spot = lane - RIM * ((lane * 57) >> 9)
        near = (lane < HIGH) | (lane >= 128 - LOW)

        for row, tiles, members, cells, shown in (
            (1, rim_tiles, fields, range(cells_x), True),
            (0, corner_tiles, fields - 2, range(cells_x - LOW, cells_x), gx > 0),
            (2, corner_tiles, fields - 2, range(HIGH), gx < n_gx - 1),
        ):
            both = []
            for tile in range(tiles):
                low = jnp.where(shown & (gy > 0), rims_in[row, 0, tile], 0.0)
                high = jnp.where(shown & (gy < n_gy - 1), rims_in[row, 1, tile], 0.0)
                both.append(jnp.where(spot < LOW, low, high))
            for cell in cells:
                x = cell + LOW + (row - 1) * cells_x
                for member in range(fields):
                    if member < members:
                        slot_id = member * cells_x + cell
                        begin = RIM * (slot_id % SLOTS)
                        value = rolled(both[slot_id // SLOTS], (256 - LOW - begin) % 128)
                        value = jnp.where(near, value, 0.0)
                    else:
                        value = zero_tile
                    top[member, x, 1, pl.ds(8, 8), :] = value

        def outside(x, carry):
            for member in range(fields):
                top[member, x, 0, pl.ds(8, 8), :] = zero_tile
            return carry

        @pl.when(gx == 0)
        def _():
            lax.fori_loop(0, LOW, outside, 0)

        @pl.when(gx == n_gx - 1)
        def _():
            lax.fori_loop(LOW + cells_x, LOW + cells_x + HIGH, outside, 0)

    def top_at(member, x, part, row=8):
        return top[member, x, part, pl.ds(row, 8), :]

    def top_along_y(member, x, forward):
        parts = [top_at(member, x, 0), top_at(member, x, 1)]

        def moved(shift):
            mine, other = [rolled(part, shift & 127) for part in parts]
            across = lane < shift if shift > 0 else lane >= 128 + shift
            return jnp.where(across, other, mine), jnp.where(across, mine, other)

        if forward:
            terms = (moved(-1), parts, moved(-2), moved(1))
        else:
            terms = (parts, moved(1), moved(-1), moved(2))
        return [stencil(*(term[part] for term in terms)) for part in range(2)]

    def top_along_x(member, x, part, shift):
        return stencil(
            top_at(member, x + shift, part),
            top_at(member, x + shift - 1, part),
            top_at(member, x + shift + 1, part),
            top_at(member, x + shift - 2, part),
        )

    def top_along_z(member, x, part, shift):
        return stencil(
            top_at(member, x, part, 8 + shift),
            top_at(member, x, part, 7 + shift),
            top_at(member, x, part, 9 + shift),
            top_at(member, x, part, 6 + shift),
        )

    def top_velocity(x, parts):
        y_of = [top_along_y(member, x, False) for member in (SXY, SYY, SYZ)]
        for part in range(parts):
            accel = (
                top_along_x(SXX, x, part, 0) + y_of[0][part] + top_along_z(SXZ, x, part, 0),
                top_along_x(SXY, x, part, 0) + y_of[1][part] + top_along_z(SYZ, x, part, 0),
                top_along_x(SXZ, x, part, 0) + y_of[2][part] + top_along_z(SZZ, x, part, 0),
            )
            for k in range(3):
                top[k, x, part, pl.ds(8, 8), :] = (
                    top_at(k, x, part) + top_at(9, x, part) * accel[k]
                )

    def top_stress(x):
        y_of = [top_along_y(member, x, True) for member in range(3)]
        for part in range(2):
            x_of = [top_along_x(member, x, part, 1) for member in range(3)]
            z_of = [top_along_z(member, x, part, 1) for member in range(3)]
            shear = top_at(11, x, part)
            volume = top_at(10, x, part) * (x_of[0] + y_of[1][part] + z_of[2])
            twice = shear + shear
            change = (
                volume + twice * x_of[0],
                volume + twice * y_of[1][part],
                volume + twice * z_of[2],
                shear * (y_of[0][part] + x_of[1]),
                shear * (z_of[0] + x_of[2]),
                shear * (z_of[1] + y_of[2][part]),
            )
            for k in range(6):
                top[SXX + k, x, part, pl.ds(8, 8), :] = top_at(SXX + k, x, part) + change[k]

    def top_layers(update, begin, size, groups, *more):
        def layers(i, carry):
            for k in range(size):
                update(begin + i * size + k, *more)
            return carry

        lax.fori_loop(0, groups, layers, 0)

    load_stress.wait()

    edges[...] = jnp.zeros(edges.shape, F32)

    def pack_first(cell, carry):
        values = [
            [at(first, k, cell + COL, ROW + 8 * z) for k in (SXY, SYY, SYZ)] for z in range(tiles_z)
        ]
        pack(0, values, cell)
        return carry

    lax.fori_loop(0, cells_x, pack_first, 0)

    load_material.wait()

    def widen(cell, carry):
        for k in range(3):
            coef[k, cell] = TIME_SOIL * raw[k, cell].astype(F32)
        return carry

    lax.fori_loop(0, cells_x, widen, 0)
    load_velocity.wait()
    source = iota((256, 256), 0) & 127
    column = iota((256, 256), 1)
    wanted = column & 127
    for forward in range(2):
        reach = jnp.where(column < 128, 0, 1)
        plus = source == wanted + forward + reach
        minus = source == wanted + forward - 1 - reach
        band[forward] = jnp.where(plus, 1.0, jnp.where(minus, -1.0, 0.0)).astype(BF16)


    for copy in load_small:
        copy.wait()
    big = (128, 128)
    big_lane = iota(big, 1)
    big_lane_f = big_lane.astype(F32)
    small_row = iota((8, 128), 0)
    small_lane = iota((8, 128), 1)

    for b in range(buildings):
        for h in range(2):
            piece = pl.ds(b * 256 + h * 128, 128)
            live = iota((1, 128), 1) + h * 128 < count[b]
            for end in range(2):
                nodes = links[pl.ds(end, 1), piece]
                index[b, h * 2 + end] = jnp.broadcast_to(nodes, (8, 128))
                kept = jnp.where(live, nodes, -1).astype(F32)
                columns = jnp.broadcast_to(kept, big).T
                spread[b, pl.ds(h * 128, 128), pl.ds(end * 128, 128)] = (
                    jnp.where(columns == big_lane_f, 1.0, 0.0).astype(BF16)
                )

    group_of = (iota((n_dev, 128), 1) // 2) % GROUPS
    holder = iota((n_dev, 128), 0)
    for j in range(1, GROUPS):
        entries = table[pl.ds(j - 1, 1), :].astype(F32)
        columns = jnp.broadcast_to(entries, (128, n_dev)).T.astype(jnp.int32)
        holder = jnp.where(group_of == j, columns, holder)
    owners[...] = holder

    bid = jnp.zeros((16, 128), F32)
    for b in range(buildings):
        cell = foot[pl.ds(b, 1), :]
        place_x = jnp.where(iota((16, 128), 0) == cell // cells_y, float(b), 0.0).astype(BF16)
        place_y = jnp.where(iota(big, 0) == cell % cells_y, 1.0, 0.0).astype(BF16)
        bid += lax.dot_general(
            place_x, place_y, (((1,), (1,)), ((), ())), preferred_element_type=F32
        )
    bids[...] = bid[0:8].astype(jnp.int32)

    blank = jnp.zeros((2, 128), F32)
    for b in range(buildings):
        piece = pl.ds(b * 128, 128)
        disp[b] = jnp.concatenate([frame_disp[:, piece], blank], 0)
        vel[b] = jnp.concatenate([frame_vel[:, piece], blank], 0)
        imass[b] = TIME_FRAME * jnp.concatenate([inverse_mass[:, piece], blank], 0)
        foot_sum[b] = jnp.zeros((8, 128), F32)

    load_matrix.wait()

    def internal_forces(b):
        place = disp[b]
        forces = []
        for h in range(2):
            ends = (
                lane_gather(place, index[b, h * 2]),
                lane_gather(place, index[b, h * 2 + 1]),
            )
            piece = pl.ds(b * 256 + h * 128, 128)
            total = None
            for a in range(12):
                row = ends[a // 6][a % 6 : a % 6 + 1, :]
                term = matrix[a, :, piece] * row
                total = term if total is None else total + term
            forces.append(jnp.concatenate([total, jnp.zeros((4, 128), F32)], 0))
        forces = jnp.concatenate(forces, 1)
        high = forces.astype(BF16)
        low = (forces - high.astype(F32)).astype(BF16)
        parts = jnp.dot(
            jnp.concatenate([high, low], 0), spread[b], preferred_element_type=F32
        )
        parts = parts[0:16] + parts[16:32]
        internal[b] = parts[0:8, 0:128] + parts[6:14, 128:256]

    def advance(b):
        speed = vel[b]
        loads = damp_vec[0, b] - damp_vec[1, b] * speed - internal[b]
        speed = speed + imass[b] * loads
        vel[b] = speed
        disp[b] = disp[b] + TIME_FRAME * speed
        foot_sum[b] += speed

    for b in range(buildings):
        internal_forces(b)

    dash = dashpot[...]
    bid = bids[...]
    stands = [jnp.where(bid == b, dash, 0.0) for b in range(buildings)]
    damping = [jnp.sum(value, axis=0, keepdims=True) for value in stands]
    lax.fori_loop(0, cells_x, top_own, 0)
    pack_rims()
    pl.semaphore_wait(barrier, n_gx + n_gy + 2)
    sent_y = send_y(0)
    sent_top = send_top()
    sent_x = send_x(0, soil, 0, first, stress_groups, 2, 1)

    finish(sent_y)
    prepare(0, False)
    velocity_layers(0, first, SXX, first, vel_a, 3, cells_x)

    finish(sent_top)
    unpack_rims()
    top_layers(top_velocity, LOW - 3, 7, (cells_x + 6) // 7, 2)
    top_layers(top_stress, LOW - 2, 4, (cells_x + 4) // 4)
    top_layers(top_velocity, LOW, 4, cells_x // 4, 1)

    surface = [top[k, pl.ds(LOW, cells_x), 0, 8, :] for k in range(3)]
    sums = [
        jnp.sum(stands[b] * surface[k], axis=0, keepdims=True)
        for k in range(3)
        for b in range(buildings)
    ]
    sums += damping
    sums = jnp.concatenate(sums + [jnp.zeros((128 - len(sums), 128), F32)], 0)
    mine = jnp.sum(sums.T, axis=0, keepdims=True)

    def far_first(count, ring):
        outer = count // ring

        def hops(k):
            return min(k // ring, outer - k // ring) + (min(k % ring, ring - k % ring) if ring > 2 else 0)

        return sorted(range(1, count), key=lambda k: -hops(k))

    def gather_along_gy(turn, value):
        row_buf[turn, gy] = value
        return [
            remote(
                row_buf.at[turn, gy],
                row_buf.at[turn, gy],
                a_send.at[turn, k - 1],
                a_recv.at[turn, k - 1],
                {"gy": lax.rem(gy + k, n_gy)},
            )
            for k in far_first(n_gy, 4)
        ]

    def gather_along_gx(turn):
        rows_all[turn, gx] = row_buf[turn].reshape(n_gy, 128)
        return [
            remote(
                rows_all.at[turn, gx],
                rows_all.at[turn, gx],
                b_send.at[turn, k - 1],
                b_recv.at[turn, k - 1],
                {"gx": lax.rem(gx + k, n_gx)},
            )
            for k in far_first(n_gx, 2)
        ]

    gathering = gather_along_gy(0, mine)

    finish(sent_x)
    outside_zero_x(first, (SXX, SXY, SXZ), 2, 1)
    velocity_layers(0, first, SXX, first, vel_a, 0, 3)
    sent = send_x(1, vel_a, COL, vel_a, move_groups, 1, 2)
    sent += send_y(1)

    finish(gathering)
    gathering = gather_along_gx(0)

    finish(sent)
    outside_zero_x(vel_a, (0, 1, 2), 1, 2)
    prepare(1, True)

    stress_layers(1, vel_a, first, SXX, str_a, COL, ROW, 0, 3, True)
    sent = send_x(2, str_a, COL, str_a, inner_groups, 2, 1)
    stress_layers(1, vel_a, first, SXX, str_a, COL, ROW, 3, cells_x, True)
    sent += send_y(2)
    finish(gathering)
    arrived = rows_all[0].reshape(n_dev, 128)
    owned = jnp.sum(jnp.where(owners[...] == me, arrived, 0.0), axis=0, keepdims=True)
    owned = jnp.broadcast_to(owned, (8, 128))

    at_footing = (small_row < 3) & (small_lane == 0)
    drives, dampers = [], []
    for b in range(buildings):
        pick = jnp.minimum(small_row * buildings + b, 127)
        drives.append(jnp.where(at_footing, lane_gather(owned, pick), 0.0))
        pick = jnp.full((8, 128), 3 * buildings + b, jnp.int32)
        dampers.append(jnp.where(at_footing, lane_gather(owned, pick), 0.0))
    for b in range(buildings):
        damp_vec[0, b] = drives[b]
        damp_vec[1, b] = dampers[b]

    def frame_step(step, carry):
        for b in range(buildings):
            advance(b)
            internal_forces(b)
        return carry

    lax.fori_loop(0, FRAME_STEPS - 1, frame_step, 0)
    for b in range(buildings):
        advance(b)

    back = jnp.zeros((8, 128), F32)
    for b in range(buildings):
        whole = jnp.broadcast_to(foot_sum[b][:, 0:1], (8, 128))
        back = jnp.where(small_lane == small_row * buildings + b, whole, back)
    back = jnp.where(small_row < 3, back, 0.0)
    gathering = gather_along_gy(1, jnp.sum(back, axis=0, keepdims=True))

    finish(sent)
    outside_zero_x(str_a, (0, 3, 4), 2, 1)
    prepare(2, False)

    velocity_layers(2, str_a, 0, vel_a, vel_b, 0, 3, moved_out)
    sent_x = send_x(3, vel_b, COL, vel_b, move_groups, 1, 2)
    velocity_layers(2, str_a, 0, vel_a, vel_b, 3, cells_x, moved_out)
    sent_y = send_y(3)

    for b in range(buildings):
        piece = pl.ds(b * 128, 128)
        disp_out[:, piece] = disp[b][0:6]
        vel_out[:, piece] = vel[b][0:6]
    finish(gathering)
    gathering = gather_along_gx(1)

    finish(sent_y)
    prepare(3, True)
    stress_layers(3, vel_b, str_a, 0, str_b, 0, 0, 3, cells_x, False)
    finish(sent_x)
    outside_zero_x(vel_b, (0, 1, 2), 1, 2)
    stress_layers(3, vel_b, str_a, 0, str_b, 0, 0, 0, 3, False)

    wanted = owners[pl.ds(me, 1), :]
    finish(gathering)
    arrived = rows_all[1].reshape(n_dev, 128)
    held = jnp.where(iota((n_dev, 128), 0) == wanted, arrived, 0.0)
    held = jnp.broadcast_to(jnp.sum(held, axis=0, keepdims=True), (8, 128))
    for k in range(3):
        total = lane_gather(held, bid + k * buildings)
        force_out[k] = dash * (FRAME_STEPS * surface[k] - total)

    for copy in leaving:
        copy.wait_send()


def write_out(moved, stress, force, disp, vel, soil_out, force_out, disp_out, vel_out, sem):
    copies = [
        pltpu.make_async_copy(source, target, sem.at[k])
        for k, (source, target) in enumerate(
            (
                (stress, soil_out.at[pl.ds(3, 6)]),
                (moved, soil_out.at[pl.ds(0, 3)]),
                (force, force_out),
                (disp, disp_out),
                (vel, vel_out),
            )
        )
    ]
    for copy in copies:
        copy.start()
    for copy in copies:
        copy.wait()


def shards(n_gx, n_gy, *args):
    soil, material, dashpot, foot, table, stiff, links = args[:7]
    cells_x, cells_z, cells_y = soil.shape[1:]
    buildings = foot.shape[0]
    wide = (cells_x + 2 * COL, cells_z + 2 * ROW, cells_y)
    n_dev = n_gx * n_gy
    anywhere = pl.BlockSpec(memory_space=pl.ANY)
    vmem = pl.BlockSpec(memory_space=pltpu.VMEM)
    dma = pltpu.SemaphoreType.DMA
    limit = 40 * 1024 * 1024
    kept = (
        pltpu.VMEM((3, cells_x, cells_z, cells_y), F32),
        pltpu.VMEM((6, cells_x, cells_z, cells_y), F32),
        pltpu.VMEM((3, cells_x, cells_y), F32),
        pltpu.VMEM(args[9].shape, F32),
        pltpu.VMEM(args[10].shape, F32),
    )
    results = pl.pallas_call(
        functools.partial(kernel, n_gx, n_gy),
        out_shape=kept,
        in_specs=[pl.BlockSpec(memory_space=pltpu.HBM)] * len(args),
        out_specs=(vmem,) * len(kept),
        scratch_shapes=[
            pltpu.VMEM((9,) + wide, F32),
            pltpu.VMEM((3,) + wide, F32),
            pltpu.VMEM((6,) + wide, F32),
            pltpu.VMEM((3,) + wide, F32),
            pltpu.VMEM(material.shape, BF16),
            pltpu.VMEM(material.shape, F32),
            pltpu.VMEM(stiff.shape, F32),
            pltpu.VMEM(dashpot.shape, F32),
            pltpu.VMEM(foot.shape, jnp.int32),
            pltpu.VMEM(table.shape, jnp.int32),
            pltpu.VMEM(links.shape, jnp.int32),
            pltpu.SMEM(args[7].shape, jnp.int32),
            pltpu.VMEM(args[8].shape, F32),
            pltpu.VMEM(args[9].shape, F32),
            pltpu.VMEM(args[10].shape, F32),
            pltpu.VMEM((buildings, 256, 256), BF16),
            pltpu.VMEM((2, 256, 256), BF16),
            pltpu.VMEM((4, 3, cells_x // 4, 8, 128), F32),
            pltpu.VMEM((4, 3, cells_x // 4, 8, 128), F32),
            pltpu.VMEM((4, 3, cells_x // 4, 8, 128), F32),
            pltpu.VMEM((4, 3, cells_x // 4, 8, 128), F32),
            pltpu.VMEM((12, cells_x + LOW + HIGH, 2, 24, 128), F32),
            pltpu.VMEM((-(-12 * cells_x // SLOTS), 8, 128), F32),
            pltpu.VMEM((3, 2, -(-12 * cells_x // SLOTS), 8, 128), F32),
            pltpu.VMEM((n_dev, 128), jnp.int32),
            pltpu.VMEM((8, 128), jnp.int32),
            pltpu.VMEM((2, buildings, 8, 128), F32),
            pltpu.VMEM((buildings, 8, 128), F32),
            pltpu.VMEM((buildings, 8, 128), F32),
            pltpu.VMEM((buildings, 8, 128), F32),
            pltpu.VMEM((buildings, 8, 128), F32),
            pltpu.VMEM((buildings, 8, 128), F32),
            pltpu.VMEM((buildings, 4, 8, 128), jnp.int32),
            pltpu.VMEM((2, n_gy, 1, 128), F32),
            pltpu.VMEM((2, n_gx, n_gy, 128), F32),
            dma((12,)),
            dma((4, 2, 2)),
            dma((4, 2, 2)),
            dma((4, 2)),
            dma((4, 2)),
            dma((2, n_gy - 1)),
            dma((2, n_gy - 1)),
            dma((2, n_gx - 1)),
            dma((2, n_gx - 1)),
            dma((12,)),
            dma((12,)),
        ],
        compiler_params=pltpu.CompilerParams(
            collective_id=0, has_side_effects=True, vmem_limit_bytes=limit
        ),
    )(*(pltpu.with_memory_space_constraint(value, pltpu.HBM) for value in args))
    return pl.pallas_call(
        write_out,
        out_shape=(
            jax.ShapeDtypeStruct(soil.shape, F32),
            jax.ShapeDtypeStruct((3, cells_x, cells_y), F32),
            jax.ShapeDtypeStruct(args[9].shape, F32),
            jax.ShapeDtypeStruct(args[10].shape, F32),
        ),
        in_specs=[vmem] * len(kept),
        out_specs=(anywhere,) * 4,
        scratch_shapes=[dma((len(kept),))],
        compiler_params=pltpu.CompilerParams(vmem_limit_bytes=limit),
    )(*results)


def solution(mesh):
    placed = (
        P(None, "gx", None, "gy"),
        P(None, "gx", None, "gy"),
        P("gx", "gy"),
        P(("gx", "gy"), None),
        P(),
        P(None, None, ("gx", "gy")),
        P(None, ("gx", "gy")),
        P(("gx", "gy")),
        P(None, ("gx", "gy")),
        P(None, ("gx", "gy")),
        P(None, ("gx", "gy")),
    )
    return jax.shard_map(
        functools.partial(shards, mesh.shape["gx"], mesh.shape["gy"]),
        mesh=mesh,
        in_specs=placed,
        out_specs=(
            P(None, "gx", None, "gy"),
            P(None, "gx", "gy"),
            P(None, ("gx", "gy")),
            P(None, ("gx", "gy")),
        ),
        check_vma=False,
    )
```
